32 devices in a mesh: dp: 4 (over y, x), fsdp: 8 (over z, core).
Axes of the slice: x: 2, y: 2, z: 4, core: 2. Of those that a mesh axis runs over, the one named last changes fastest.
Arguments:
- tokens: bfloat16 [30720, 768], P(('dp', 'fsdp')), may hold values from -6 to 6
- ln1_gain: bfloat16 [768], P('fsdp'), may hold values from 0.5 to 1.5
- ln1_bias: bfloat16 [768], P('fsdp'), may hold values from -3 to 3
- w_qkv: bfloat16 [768, 2304], P('fsdp'), may hold values from -0.21875 to 0.21875
- qv_bias: bfloat16 [2, 768], P(None, 'fsdp'), may hold values from -3 to 3
- w_proj: bfloat16 [768, 768], P('fsdp'), may hold values from -2 to 2
- proj_bias: bfloat16 [768], P('fsdp'), may hold values from -3 to 3
- ln2_gain: bfloat16 [768], P('fsdp'), may hold values from 0.5 to 1.5
- ln2_bias: bfloat16 [768], P('fsdp'), may hold values from -3 to 3
- w_up: bfloat16 [768, 3072], P('fsdp'), may hold values from -0.21875 to 0.21875
- up_bias: bfloat16 [3072], P('fsdp'), may hold values from -3 to 3
- w_down: bfloat16 [3072, 768], P('fsdp'), may hold values from -0.109375 to 0.109375
- down_bias: bfloat16 [768], P('fsdp'), may hold values from -3 to 3
- w_head: bfloat16 [768, 1024], P('fsdp'), may hold values from -0.21875 to 0.21875
- head_bias: bfloat16 [1024], P('fsdp'), may hold values from -3 to 3
- clip_counts: int32 [32, 32], replicated, may hold values from 0 to 157, as said below
- cot_out: bfloat16 [30720, 768], P(('dp', 'fsdp')), may hold values from -6 to 6
- cot_align: bfloat16 [30720, 1024], P(('dp', 'fsdp')), may hold values from -6 to 6
Outputs:
- block_out: bfloat16 [30720, 768], P(('dp', 'fsdp'))
- aligned: bfloat16 [30720, 1024], P(('dp', 'fsdp'))
- grad_tokens: bfloat16 [30720, 768], P(('dp', 'fsdp'))
- grad_ln1_gain: float32 [768], P('fsdp')
- grad_ln1_bias: float32 [768], P('fsdp')
- grad_w_qkv: float32 [768, 2304], P('fsdp')
- grad_qv_bias: float32 [2, 768], P(None, 'fsdp')
- grad_w_proj: float32 [768, 768], P('fsdp')
- grad_proj_bias: float32 [768], P('fsdp')
- grad_ln2_gain: float32 [768], P('fsdp')
- grad_ln2_bias: float32 [768], P('fsdp')
- grad_w_up: float32 [768, 3072], P('fsdp')
- grad_up_bias: float32 [3072], P('fsdp')
- grad_w_down: float32 [3072, 768], P('fsdp')
- grad_down_bias: float32 [768], P('fsdp')
- grad_w_head: float32 [768, 1024], P('fsdp')
- grad_head_bias: float32 [1024], P('fsdp')
The draws below stay inside these ranges and needn't reach their ends.
Inputs may be any that keep to these rules, and one draw needn't show every extreme that they name: `clip_counts`: in each sequence the nonzero counts come first and lie between 40 and 157, the rest are 0; they sum to at most 960 and to more than 803.
All inputs are finite; a program needn't handle non-finite values.
Results may differ from the reference program's by a relative error of at most 0.012.
Values may be sent and summed in bfloat16 or wider, within the bound.
No kernel may reach another device: no remote copies, remote signals or barrier semaphores. Data moves between devices by JAX's collectives and lax.ppermute only.
A program may use at most 192 MiB of HBM per device.

```python
import jax
import jax.numpy as jnp
from jax import lax

D = 768
HEADS = 12
HEAD = 64
FF = 3072
ALIGN = 1024
SEQ_LEN = 960
CLIP_MIN = 40
CLIP_MAX = 157
SLOTS = 32
SEQS = 32
TOKENS = 30720


def draw_clip_counts(key, part):
    key = jax.random.fold_in(key, 7)
    counts = jax.random.randint(key, (SEQS, SLOTS), CLIP_MIN, CLIP_MAX + 1, dtype=jnp.int32)
    ends = jnp.cumsum(counts, axis=1)
    return jnp.where(ends <= SEQ_LEN, counts, 0).astype(jnp.int32)


def shard_levels(key, extent, pieces, smallest, largest):
    level = 1.0
    for position, shards_of in pieces:
        heights = jax.random.uniform(jax.random.fold_in(jax.random.fold_in(key, 6), position), (shards_of,), jnp.float32, smallest / len(pieces), largest / len(pieces))
        level = level * jnp.repeat(jnp.exp(heights), extent[position] // shards_of).reshape((-1,) + (1,) * (len(extent) - 1 - position))
    return level


def scatter_about(own_key, extent, scale, reach, shards=(), held_as=jnp.bfloat16):
    level = shard_levels(own_key, extent, shards, -0.22, 0.18) if shards else 1.0
    entries = jax.random.normal(own_key, extent, jnp.float32) * scale * level
    return jnp.minimum(jnp.maximum(entries, -reach), reach).astype(held_as)


def setup_inputs(seed: int = 0) -> dict:
    key_of = jax.random.split(jax.random.key(seed), 19)
    return {
        "tokens": scatter_about(key_of[0], (TOKENS, D), 1.0, 6.0, ((0, 32),)),
        "ln1_gain": jnp.clip(1.0 + 0.1 * jax.random.normal(key_of[1], (D,), jnp.float32), 0.5, 1.5).astype(jnp.bfloat16),
        "ln1_bias": scatter_about(key_of[2], (D,), 0.5, 3.0, ((0, 8),)),
        "w_qkv": scatter_about(key_of[3], (D, 3 * D), D ** -0.5, 0.21875, ((0, 8),)),
        "qv_bias": scatter_about(key_of[4], (2, D), 0.5, 3.0, ((1, 8),)),
        "w_proj": scatter_about(key_of[5], (D, D), (2 * D // (CLIP_MIN + CLIP_MAX)) ** -0.5, 2.0, ((0, 8),)),
        "proj_bias": scatter_about(key_of[6], (D,), 0.5, 3.0, ((0, 8),)),
        "ln2_gain": jnp.clip(1.0 + 0.1 * jax.random.normal(key_of[7], (D,), jnp.float32), 0.5, 1.5).astype(jnp.bfloat16),
        "ln2_bias": scatter_about(key_of[8], (D,), 0.5, 3.0, ((0, 8),)),
        "w_up": scatter_about(key_of[9], (D, FF), D ** -0.5, 0.21875, ((0, 8),)),
        "up_bias": scatter_about(key_of[10], (FF,), 0.5, 3.0, ((0, 8),)),
        "w_down": scatter_about(key_of[11], (FF, D), FF ** -0.5, 0.109375, ((0, 8),)),
        "down_bias": scatter_about(key_of[12], (D,), 0.5, 3.0, ((0, 8),)),
        "w_head": scatter_about(key_of[13], (D, ALIGN), D ** -0.5, 0.21875, ((0, 8),)),
        "head_bias": scatter_about(key_of[14], (ALIGN,), 0.5, 3.0, ((0, 8),)),
        "clip_counts": draw_clip_counts(jax.random.fold_in(key_of[18], 71), 0),
        "cot_out": scatter_about(key_of[16], (TOKENS, D), 1.0, 6.0, ((0, 32),)),
        "cot_align": scatter_about(key_of[17], (TOKENS, ALIGN), 1.0, 6.0, ((0, 32),)),
    }


epsilon = 1e-06
masked_score = -1e+30

@jax.custom_vjp
def low(v):
    return lax.optimization_barrier(v.astype(jnp.bfloat16)).astype(jnp.float32)

@jax.custom_vjp
def low_back(v):
    return v

def low_keep(v):
    return (low(v), None)

def low_pass(kept, grad):
    return (grad,)

def back_keep(v):
    return (v, None)

def back_low(kept, grad):
    return (low(grad),)
low.defvjp(low_keep, low_pass)
low_back.defvjp(back_keep, back_low)

def matmul(left, right):
    return jnp.dot(left, right, precision=lax.Precision.HIGHEST, preferred_element_type=jnp.float32)

def normalize(values, gain, shift):
    center = values - lax.optimization_barrier(jnp.mean(values, axis=-1, keepdims=True))
    spread = lax.optimization_barrier(jnp.mean(center * center, axis=-1, keepdims=True))
    return center * lax.rsqrt(spread + epsilon) * gain + shift

def sequence_layer(params, item):
    ln1_gain, ln1_bias, w_qkv, qv_bias, w_proj, proj_bias, ln2_gain, ln2_bias, w_up, up_bias, w_down, down_bias, w_head, head_bias = params
    inputs, segment, valid = item
    scale = HEAD ** (-0.5)
    hidden_one = low(normalize(inputs, ln1_gain, ln1_bias))
    projected = matmul(hidden_one, w_qkv)
    queries = low_back(low((projected[:, :D] + qv_bias[0]) * scale))
    keys_all = low_back(low(projected[:, D:2 * D]))
    values_all = low_back(low(projected[:, 2 * D:] + qv_bias[1]))
    scores = jnp.einsum('qhd,khd->hqk', queries.reshape(SEQ_LEN, HEADS, HEAD), keys_all.reshape(SEQ_LEN, HEADS, HEAD), precision=lax.Precision.HIGHEST)
    scores = low_back(scores)
    allowed = segment[:, None] == segment[None, :]
    scores = jnp.where(allowed[None], scores, masked_score)
    top_score = lax.optimization_barrier(jnp.max(scores, axis=-1, keepdims=True))
    weights = jnp.exp(scores - top_score)
    probs = low(weights / lax.optimization_barrier(jnp.sum(weights, axis=-1, keepdims=True)))
    attended = jnp.einsum('hqk,khd->qhd', probs, values_all.reshape(SEQ_LEN, HEADS, HEAD), precision=lax.Precision.HIGHEST).reshape(SEQ_LEN, D)
    attended = low_back(low(attended))
    branch_one = low_back(matmul(attended, w_proj) + proj_bias)
    middle = inputs + branch_one
    hidden_two = low(normalize(middle, ln2_gain, ln2_bias))
    up_value = low_back(matmul(hidden_two, w_up) + up_bias)
    activated = low(jax.nn.gelu(up_value, approximate=False))
    branch_two = low_back(matmul(activated, w_down) + down_bias)
    result = middle + branch_two
    head_value = matmul(low(result), w_head) + head_bias
    return (result * valid, head_value * valid)

def reference(tokens, ln1_gain, ln1_bias, w_qkv, qv_bias, w_proj, proj_bias, ln2_gain, ln2_bias, w_up, up_bias, w_down, down_bias, w_head, head_bias, clip_counts, cot_out, cot_align):
    params = tuple((item.astype(jnp.float32) for item in (ln1_gain, ln1_bias, w_qkv, qv_bias, w_proj, proj_bias, ln2_gain, ln2_bias, w_up, up_bias, w_down, down_bias, w_head, head_bias)))
    ends = jnp.cumsum(clip_counts, axis=1).astype(jnp.int32)
    places = jnp.arange(SEQ_LEN, dtype=jnp.int32)
    segment = lax.optimization_barrier(jnp.sum((ends[:, None, :] <= places[None, :, None]).astype(jnp.int32), axis=-1)).astype(jnp.int32)
    valid = (places[None, :] < ends[:, -1:]).astype(jnp.float32)[:, :, None]
    inputs = tokens.astype(jnp.float32).reshape(SEQS, SEQ_LEN, D)
    checked = jax.checkpoint(sequence_layer)

    def forward(weights, rows):

        def one_sequence(item):
            return checked(weights, item)
        return lax.map(one_sequence, (rows, segment, valid))
    outputs, pullback = jax.vjp(forward, params, inputs)
    grads, grad_rows = pullback((cot_out.astype(jnp.float32).reshape(SEQS, SEQ_LEN, D), cot_align.astype(jnp.float32).reshape(SEQS, SEQ_LEN, ALIGN)))
    block_out = outputs[0].reshape(TOKENS, D).astype(jnp.bfloat16)
    aligned = outputs[1].reshape(TOKENS, ALIGN).astype(jnp.bfloat16)
    grad_tokens = grad_rows.reshape(TOKENS, D).astype(jnp.bfloat16)
    return (block_out, aligned, grad_tokens, grads[0], grads[1], grads[2], grads[3], grads[4], grads[5], grads[6], grads[7], grads[8], grads[9], grads[10], grads[11], grads[12], grads[13])
```

```python
import functools
import math

import jax
import jax.numpy as jnp
from jax import lax
from jax.experimental import pallas as pl
from jax.experimental.pallas import tpu as pltpu
from jax.sharding import PartitionSpec as P

HEADS = 12
LONGEST = 157
EPSILON = 1e-06
MASKED = -1e30
VMEM_BYTES = 56 * 1024 * 1024
TILE = 128

f32 = jnp.float32
bf16 = jnp.bfloat16


def dot_nn(left, right):
    return lax.dot_general(left, right, (((1,), (0,)), ((), ())), preferred_element_type=f32)


def dot_nt(left, right):
    return lax.dot_general(left, right, (((1,), (1,)), ((), ())), preferred_element_type=f32)


def dot_tn(left, right):
    return lax.dot_general(left, right, (((0,), (0,)), ((), ())), preferred_element_type=f32)


def attention_tiles(rows):
    tiles, offset = [], 0
    reach = LONGEST - 1
    for start in range(0, rows, TILE):
        size = min(TILE, rows - start)
        low = max(0, (start - reach) // 16 * 16)
        high = min(rows, -(-(start + size + reach) // 16) * 16)
        tiles.append((start, size, low, high - low, offset))
        offset += high - low
    return tiles, offset


def row_tile(rows, most):
    for size in range(most, 15, -16):
        if rows % size == 0:
            return size
    return rows


def params(*semantics):
    return pltpu.CompilerParams(vmem_limit_bytes=VMEM_BYTES)


def whole(shape):
    return pl.BlockSpec(shape, lambda *_: (0,) * len(shape), pipeline_mode=pl.Buffered(1))


def out_whole(shape):
    return pl.BlockSpec(shape, lambda *_: (0,) * len(shape))


SMEM = pl.BlockSpec(memory_space=pltpu.SMEM)


def mask_kernel(tiles, seq_ref, counts_ref, bias_ref, seg_ref):
    rows = seg_ref.shape[0]
    slots = counts_ref.shape[1]
    seq = seq_ref[0]
    ends, total = [], jnp.int32(0)
    for slot in range(slots):
        total = total + counts_ref[seq, slot]
        ends.append(total)
    places = lax.broadcasted_iota(jnp.int32, (rows, TILE), 0)
    seg = jnp.zeros((rows, TILE), jnp.int32)
    for end in ends:
        seg = seg + jnp.where(places >= end, 1, 0)
    seg_ref[...] = seg
    lanes = lax.broadcasted_iota(jnp.int32, (8, TILE), 1)
    for start, size, low, keys, offset in tiles:
        own = start + jnp.where(lanes >= size, lanes - size, lanes)
        seg_own = jnp.zeros((8, TILE), jnp.int32)
        for end in ends:
            seg_own = seg_own + jnp.where(own >= end, 1, 0)
        same = seg_ref[low : low + keys, :] == seg_own[0:1, :]
        bias_ref[offset : offset + keys, :] = jnp.where(same, 0.0, MASKED).astype(f32)


def make_masks(seq, counts, rows):
    tiles, total = attention_tiles(rows)
    return pl.pallas_call(
        functools.partial(mask_kernel, tiles),
        out_shape=jax.ShapeDtypeStruct((total, TILE), f32),
        in_specs=[SMEM, SMEM],
        out_specs=pl.BlockSpec(memory_space=pltpu.VMEM),
        scratch_shapes=[pltpu.VMEM((rows, TILE), jnp.int32)],
        compiler_params=params(),
        name="masks",
    )(seq, counts)


def normed(values):
    center = values - jnp.mean(values, axis=-1, keepdims=True)
    spread = jnp.mean(center * center, axis=-1, keepdims=True)
    inverse = lax.rsqrt(spread + EPSILON)
    return center * inverse, inverse


def qkv_kernel(scale, tok_ref, gain_ref, shift_ref, w_ref, qvb_ref, h_ref, q_ref, k_ref, v_ref):
    width = tok_ref.shape[1]
    n1, _ = normed(tok_ref[...].astype(f32))
    hidden = (n1 * gain_ref[...].astype(f32) + shift_ref[...].astype(f32)).astype(bf16)
    h_ref[...] = hidden
    qvb = qvb_ref[...].astype(f32)
    q = dot_nn(hidden, w_ref[:, :width])
    q_ref[...] = ((q + qvb[0:1, :]) * scale).astype(bf16)
    k = dot_nn(hidden, w_ref[:, width : 2 * width])
    k_ref[...] = k.astype(bf16)
    v = dot_nn(hidden, w_ref[:, 2 * width :])
    v_ref[...] = (v + qvb[1:2, :]).astype(bf16)


def project_qkv(tokens, gain, shift, w_qkv, qv_bias):
    rows, width = tokens.shape
    scale = (width // HEADS) ** (-0.5)
    size = row_tile(rows, 320)
    rowwise = pl.BlockSpec((size, width), lambda i: (i, 0))
    out = jax.ShapeDtypeStruct((rows, width), bf16)
    return pl.pallas_call(
        functools.partial(qkv_kernel, scale),
        grid=(rows // size,),
        out_shape=(out,) * 4,
        in_specs=[rowwise, whole(gain.shape), whole(shift.shape), whole(w_qkv.shape), whole(qv_bias.shape)],
        out_specs=(rowwise,) * 4,
        compiler_params=params(),
        name="norm_qkv",
    )(tokens, gain, shift, w_qkv, qv_bias)


def stack_heads(pair, size):
    lanes = lax.broadcasted_iota(jnp.int32, pair.shape, 1)
    half = pair.shape[1] // 2
    zero = jnp.zeros_like(pair)
    first = jnp.where(lanes < half, pair, zero)
    second = jnp.where(lanes < half, zero, pair)
    return jnp.concatenate([first, second], axis=0)


def both(bias, size):
    return bias if size < TILE else jnp.concatenate([bias, bias], axis=1)


def unstack(columns, size, half):
    return jnp.concatenate([columns[:half, :size], columns[half:, size:]], axis=0).T


def attend_kernel(tiles, bias_ref, q_ref, k_ref, v_ref, o_ref, lse_ref):
    half = q_ref.shape[1] // 2
    for index, (start, size, low, keys, offset) in enumerate(tiles):
        stacked = stack_heads(q_ref[start : start + size, :], size)
        scores = dot_nt(k_ref[low : low + keys, :], stacked)
        scores = scores + both(bias_ref[offset : offset + keys, :], size)
        top = jnp.max(scores, axis=0, keepdims=True)
        weights = jnp.exp(scores - top)
        total = jnp.sum(weights, axis=0, keepdims=True)
        probs = (weights * (1.0 / total)).astype(bf16)
        columns = dot_tn(v_ref[low : low + keys, :], probs)
        o_ref[start : start + size, :] = unstack(columns, size, half).astype(bf16)
        lse_ref[0, index : index + 1, : 2 * size] = top + jnp.log(total)


def attend(bias, q, k, v):
    rows, width = q.shape
    tiles, _ = attention_tiles(rows)
    span = 2 * (width // HEADS)
    pairs = HEADS // 2
    column = pl.BlockSpec((rows, span), lambda p: (0, p))
    return pl.pallas_call(
        functools.partial(attend_kernel, tiles),
        grid=(pairs,),
        out_shape=(
            jax.ShapeDtypeStruct((rows, width), bf16),
            jax.ShapeDtypeStruct((pairs, len(tiles), 2 * TILE), f32),
        ),
        in_specs=[whole(bias.shape), column, column, column],
        out_specs=(column, pl.BlockSpec((1, len(tiles), 2 * TILE), lambda p: (p, 0, 0))),
        compiler_params=params(),
        name="attend",
    )(bias, q, k, v)


def attend_back_kernel(
    tiles, scale, bias_ref, q_ref, k_ref, v_ref, o_ref, do_ref, lse_ref, dq_ref, dk_ref, dv_ref, dqv_ref, dk_sum, dv_sum
):
    half = q_ref.shape[1] // 2
    dk_sum[...] = jnp.zeros_like(dk_sum)
    dv_sum[...] = jnp.zeros_like(dv_sum)
    dq_total = jnp.zeros((1, 2 * half), f32)
    for index, (start, size, low, keys, offset) in enumerate(tiles):
        window = slice(low, low + keys)
        rows = slice(start, start + size)
        q2 = stack_heads(q_ref[rows, :], size)
        grads = do_ref[rows, :]
        do2 = stack_heads(grads, size)
        scores = dot_nt(k_ref[window, :], q2) + both(bias_ref[offset : offset + keys, :], size)
        probs = jnp.exp(scores - lse_ref[0, index : index + 1, : 2 * size])
        dprobs = dot_nt(v_ref[window, :], do2)
        meet = (grads.astype(f32) * o_ref[rows, :].astype(f32)).T
        delta = jnp.concatenate(
            [
                jnp.sum(meet[:half, :], axis=0, keepdims=True),
                jnp.sum(meet[half:, :], axis=0, keepdims=True),
            ],
            axis=1,
        )
        dv_sum[window, :] += dot_nn(probs.astype(bf16), do2)
        dscores = (probs * (dprobs - delta)).astype(bf16)
        dk_sum[window, :] += dot_nn(dscores, q2)
        columns = dot_tn(k_ref[window, :], dscores)
        dq = unstack(columns, size, half).astype(bf16) * bf16(scale)
        dq_ref[rows, :] = dq
        dq_total = dq_total + jnp.sum(dq.astype(f32), axis=0, keepdims=True)
    dk_ref[...] = dk_sum[...].astype(bf16)
    dv = dv_sum[...].astype(bf16)
    dv_ref[...] = dv
    dqv_ref[0:1, :] = dq_total
    dqv_ref[1:2, :] = jnp.sum(dv.astype(f32), axis=0, keepdims=True)


def attend_back(bias, q, k, v, o, do, lse):
    rows, width = q.shape
    tiles, _ = attention_tiles(rows)
    span = 2 * (width // HEADS)
    pairs = HEADS // 2
    scale = (width // HEADS) ** (-0.5)
    column = pl.BlockSpec((rows, span), lambda p: (0, p))
    out = jax.ShapeDtypeStruct((rows, width), bf16)
    return pl.pallas_call(
        functools.partial(attend_back_kernel, tiles, scale),
        grid=(pairs,),
        out_shape=(out, out, out, jax.ShapeDtypeStruct((2, width), f32)),
        in_specs=[whole(bias.shape)]
        + [column] * 5
        + [pl.BlockSpec((1, len(tiles), 2 * TILE), lambda p: (p, 0, 0))],
        out_specs=(column, column, column, pl.BlockSpec((2, span), lambda p: (0, p))),
        scratch_shapes=[pltpu.VMEM((rows, span), f32), pltpu.VMEM((rows, span), f32)],
        compiler_params=params(),
        name="attend_back",
    )(bias, q, k, v, o, do, lse)


PARTS = 4


def middle_kernel(
    seq_ref,
    counts_ref,
    tok_ref,
    o_ref,
    cot_out_ref,
    cot_align_ref,
    w_proj_ref,
    w_up_ref,
    w_down_ref,
    w_head_ref,
    b_proj_ref,
    gain_ref,
    shift_ref,
    b_up_ref,
    b_down_ref,
    b_head_ref,
    out_ref,
    aligned_ref,
    z_ref,
    e_ref,
    h_ref,
    g_ref,
    du_ref,
    dm_ref,
    dx_ref,
    da_ref,
    do_ref,
    s_head_ref,
    s_down_ref,
    s_up_ref,
    s_gain_ref,
    s_shift_ref,
    s_proj_ref,
):
    step = pl.program_id(0)
    size, width = tok_ref.shape
    hidden_units = w_up_ref.shape[1]
    part = hidden_units // PARTS
    seq = seq_ref[0]
    total = jnp.int32(0)
    for slot in range(counts_ref.shape[1]):
        total = total + counts_ref[seq, slot]
    places = lax.broadcasted_iota(jnp.int32, (size, 1), 0) + step * size
    valid = jnp.where(places < total, 1.0, 0.0).astype(f32)

    @pl.when(step == 0)
    def _():
        for ref in (s_head_ref, s_down_ref, s_up_ref, s_gain_ref, s_shift_ref, s_proj_ref):
            ref[...] = jnp.zeros_like(ref)

    x1 = tok_ref[...].astype(f32) + dot_nn(o_ref[...], w_proj_ref[...]) + b_proj_ref[...].astype(f32)
    n2, inverse = normed(x1)
    gain = gain_ref[...].astype(f32)
    h2 = (n2 * gain + shift_ref[...].astype(f32)).astype(bf16)
    h_ref[...] = h2

    e_al = (cot_align_ref[...].astype(f32) * valid).astype(bf16)
    e_ref[...] = e_al
    s_head_ref[...] += jnp.sum(e_al.astype(f32), axis=0, keepdims=True)
    dx2 = cot_out_ref[...].astype(f32) * valid + dot_nt(e_al, w_head_ref[...])
    dm = dx2.astype(bf16)
    dm_ref[...] = dm
    s_down_ref[...] += jnp.sum(dm.astype(f32), axis=0, keepdims=True)

    x2 = x1 + b_down_ref[...].astype(f32)
    dh2 = jnp.zeros((size, width), f32)
    for index in range(PARTS):
        span = slice(index * part, (index + 1) * part)
        u = dot_nn(h2, w_up_ref[:, span]) + b_up_ref[:, span].astype(f32)
        cdf = 0.5 * (1.0 + lax.erf(u * (1.0 / math.sqrt(2.0))))
        pdf = jnp.exp(-0.5 * u * u) * (1.0 / math.sqrt(2.0 * math.pi))
        g = (u * cdf).astype(bf16)
        g_ref[:, span] = g
        x2 = x2 + dot_nn(g, w_down_ref[span, :])
        du = (dot_nt(dm, w_down_ref[span, :]) * (cdf + u * pdf)).astype(bf16)
        du_ref[:, span] = du
        s_up_ref[:, span] += jnp.sum(du.astype(f32), axis=0, keepdims=True)
        dh2 = dh2 + dot_nt(du, w_up_ref[:, span])
    out_ref[...] = (x2 * valid).astype(bf16)
    z = x2.astype(bf16)
    z_ref[...] = z
    aligned_ref[...] = ((dot_nn(z, w_head_ref[...]) + b_head_ref[...].astype(f32)) * valid).astype(bf16)

    s_gain_ref[...] += jnp.sum(dh2 * n2, axis=0, keepdims=True)
    s_shift_ref[...] += jnp.sum(dh2, axis=0, keepdims=True)
    t = dh2 * gain
    inner = t - jnp.mean(t, axis=-1, keepdims=True) - n2 * jnp.mean(t * n2, axis=-1, keepdims=True)
    dx1 = dx2 + inverse * inner
    dx_ref[...] = dx1
    da = dx1.astype(bf16)
    da_ref[...] = da
    s_proj_ref[...] += jnp.sum(da.astype(f32), axis=0, keepdims=True)
    do_ref[...] = dot_nt(da, w_proj_ref[...]).astype(bf16)


def middle(seq, counts, tokens, o, cot_out, cot_align, w_proj, w_up, w_down, w_head, small):
    rows, width = tokens.shape
    hidden, align = w_up.shape[1], w_head.shape[1]
    size = row_tile(rows, 240)

    def by_row(columns):
        return pl.BlockSpec((size, columns), lambda i: (i, 0))

    def row_shape(columns, dtype=bf16):
        return jax.ShapeDtypeStruct((rows, columns), dtype)

    outs = [
        (by_row(width), row_shape(width)),
        (by_row(align), row_shape(align)),
        (by_row(width), row_shape(width)),
        (by_row(align), row_shape(align)),
        (by_row(width), row_shape(width)),
        (by_row(hidden), row_shape(hidden)),
        (by_row(hidden), row_shape(hidden)),
        (by_row(width), row_shape(width)),
        (by_row(width), row_shape(width, f32)),
        (by_row(width), row_shape(width)),
        (by_row(width), row_shape(width)),
    ]
    for columns in (align, width, hidden, width, width, width):
        outs.append((out_whole((1, columns)), jax.ShapeDtypeStruct((1, columns), f32)))
    weights = (w_proj, w_up, w_down, w_head) + tuple(small)
    return pl.pallas_call(
        middle_kernel,
        grid=(rows // size,),
        out_shape=tuple(shape for _, shape in outs),
        in_specs=[SMEM, SMEM, by_row(width), by_row(width), by_row(width), by_row(align)]
        + [whole(w.shape) for w in weights],
        out_specs=tuple(spec for spec, _ in outs),
        compiler_params=params(),
        name="middle",
    )(seq, counts, tokens, o, cot_out, cot_align, *weights)


def outer_kernel(l_ref, r_ref, out_ref):
    out_ref[...] = dot_tn(l_ref[...], r_ref[...]).astype(out_ref.dtype)


def outer(left, right, rows_out, columns_out, name):
    rows, m = left.shape
    n = right.shape[1]
    tm, tn = min(rows_out, m), min(columns_out, n)
    return pl.pallas_call(
        outer_kernel,
        grid=(m // tm, n // tn),
        out_shape=jax.ShapeDtypeStruct((m, n), bf16),
        in_specs=[
            pl.BlockSpec((rows, tm), lambda i, j: (0, i)),
            pl.BlockSpec((rows, tn), lambda i, j: (0, j)),
        ],
        out_specs=pl.BlockSpec((tm, tn), lambda i, j: (i, j)),
        compiler_params=params(),
        name=name,
    )(left, right)


def first_back_kernel(tok_ref, dx_ref, dq_ref, dk_ref, dv_ref, w_ref, gain_ref, out_ref, s_gain_ref, s_shift_ref):
    width = tok_ref.shape[1]

    @pl.when(pl.program_id(0) == 0)
    def _():
        s_gain_ref[...] = jnp.zeros_like(s_gain_ref)
        s_shift_ref[...] = jnp.zeros_like(s_shift_ref)

    dh = dot_nt(dq_ref[...], w_ref[:, :width])
    dh = dh + dot_nt(dk_ref[...], w_ref[:, width : 2 * width])
    dh = dh + dot_nt(dv_ref[...], w_ref[:, 2 * width :])
    n1, inverse = normed(tok_ref[...].astype(f32))
    s_gain_ref[...] += jnp.sum(dh * n1, axis=0, keepdims=True)
    s_shift_ref[...] += jnp.sum(dh, axis=0, keepdims=True)
    t = dh * gain_ref[...].astype(f32)
    inner = t - jnp.mean(t, axis=-1, keepdims=True) - n1 * jnp.mean(t * n1, axis=-1, keepdims=True)
    out_ref[...] = (dx_ref[...] + inverse * inner).astype(bf16)


def first_back(tokens, dx1, dq, dk, dv, w_qkv, gain):
    rows, width = tokens.shape
    size = row_tile(rows, 320)
    rowwise = pl.BlockSpec((size, width), lambda i: (i, 0))
    total = jax.ShapeDtypeStruct((1, width), f32)
    return pl.pallas_call(
        first_back_kernel,
        grid=(rows // size,),
        out_shape=(jax.ShapeDtypeStruct((rows, width), bf16), total, total),
        in_specs=[rowwise] * 5 + [whole(w_qkv.shape), whole(gain.shape)],
        out_specs=(rowwise, out_whole((1, width)), out_whole((1, width))),
        compiler_params=params(),
        name="first_back",
    )(tokens, dx1, dq, dk, dv, w_qkv, gain)


def local(
    tokens,
    ln1_gain,
    ln1_bias,
    w_qkv,
    qv_bias,
    w_proj,
    proj_bias,
    ln2_gain,
    ln2_bias,
    w_up,
    up_bias,
    w_down,
    down_bias,
    w_head,
    head_bias,
    clip_counts,
    cot_out,
    cot_align,
):
    rows, width = tokens.shape
    shards = lax.axis_size("fsdp")

    def gather(value):
        return lax.all_gather(value, "fsdp", axis=0, tiled=True)

    vectors = (ln1_gain, ln1_bias, qv_bias[0], qv_bias[1], proj_bias, ln2_gain, ln2_bias, up_bias, down_bias, head_bias)
    packed = gather(jnp.concatenate(vectors)[None])
    parts, at = [], 0
    for vector in vectors:
        parts.append(packed[:, at : at + vector.shape[0]].reshape(1, -1))
        at += vector.shape[0]
    gain_one, shift_one, b_q, b_v, b_proj, gain_two, shift_two, b_up, b_down, b_head = parts
    full_qkv, full_proj, full_up, full_down, full_head = (gather(w) for w in (w_qkv, w_proj, w_up, w_down, w_head))

    seq = (lax.axis_index("dp") * shards + lax.axis_index("fsdp")).astype(jnp.int32)[None]
    bias = make_masks(seq, clip_counts, rows)
    h1, q, k, v = project_qkv(tokens, gain_one, shift_one, full_qkv, jnp.concatenate([b_q, b_v]))
    o, lse = attend(bias, q, k, v)
    (block_out, aligned, z, e_al, h2, g, du, dm, dx1, da, do, s_head, s_down, s_up, s_gain, s_shift, s_proj) = middle(
        seq,
        clip_counts,
        tokens,
        o,
        cot_out,
        cot_align,
        full_proj,
        full_up,
        full_down,
        full_head,
        (b_proj, gain_two, shift_two, b_up, b_down, b_head),
    )
    g_up = outer(h2, du, 768, 512, "grad_up")
    g_down = outer(g, dm, 512, 768, "grad_down")
    g_head = outer(z, e_al, 768, 512, "grad_head")
    g_proj = outer(o, da, 768, 384, "grad_proj")
    dq, dk, dv, s_qv = attend_back(bias, q, k, v, o, do, lse)
    grad_tokens, s_gain_one, s_shift_one = first_back(tokens, dx1, dq, dk, dv, full_qkv, gain_one)
    g_qkv = outer(h1, jnp.concatenate([dq, dk, dv], axis=1), 768, 768, "grad_qkv")

    def reduce(value):
        part = lax.psum_scatter(value, "fsdp", scatter_dimension=0, tiled=True)
        return lax.psum(part.astype(f32), "dp")

    d_up, d_down, d_head, d_proj, d_qkv = (reduce(w) for w in (g_up, g_down, g_head, g_proj, g_qkv))
    sums = (s_gain_one, s_shift_one, s_qv[0:1], s_qv[1:2], s_proj, s_gain, s_shift, s_up, s_down, s_head)
    packed = jnp.concatenate([s.reshape(shards, -1) for s in sums], axis=1)
    mine = lax.psum(lax.psum_scatter(packed, "fsdp", scatter_dimension=0, tiled=True), "dp")[0]
    parts, at = [], 0
    for vector in vectors:
        parts.append(mine[at : at + vector.shape[0]])
        at += vector.shape[0]
    return (
        block_out,
        aligned,
        grad_tokens,
        parts[0],
        parts[1],
        d_qkv,
        jnp.stack([parts[2], parts[3]]),
        d_proj,
        parts[4],
        parts[5],
        parts[6],
        d_up,
        parts[7],
        d_down,
        parts[8],
        d_head,
        parts[9],
    )


def solution(mesh):
    rows = P(("dp", "fsdp"), None)
    matrix, vector, pair = P("fsdp", None), P("fsdp"), P(None, "fsdp")
    return jax.shard_map(
        local,
        mesh=mesh,
        in_specs=(
            rows,
            vector,
            vector,
            matrix,
            pair,
            matrix,
            vector,
            vector,
            vector,
            matrix,
            vector,
            matrix,
            vector,
            matrix,
            vector,
            P(),
            rows,
            rows,
        ),
        out_specs=(
            rows,
            rows,
            rows,
            vector,
            vector,
            matrix,
            pair,
            matrix,
            vector,
            vector,
            vector,
            matrix,
            vector,
            matrix,
            vector,
            matrix,
            vector,
        ),
        check_vma=False,
    )
```

```python
import functools
import math

import jax
import jax.numpy as jnp
from jax import lax
from jax.experimental import pallas as pl
from jax.experimental.pallas import tpu as pltpu
from jax.sharding import PartitionSpec as P

HEADS = 12
LONGEST = 157
EPSILON = 1e-06
MASKED = -1e30
VMEM_BYTES = 56 * 1024 * 1024
TILE = 128

f32 = jnp.float32
bf16 = jnp.bfloat16


def dot_nn(left, right):
    return lax.dot_general(left, right, (((1,), (0,)), ((), ())), preferred_element_type=f32)


def dot_nt(left, right):
    return lax.dot_general(left, right, (((1,), (1,)), ((), ())), preferred_element_type=f32)


def dot_tn(left, right):
    return lax.dot_general(left, right, (((0,), (0,)), ((), ())), preferred_element_type=f32)


def attention_tiles(rows):
    tiles, offset = [], 0
    reach = LONGEST - 1
    for start in range(0, rows, TILE):
        size = min(TILE, rows - start)
        low = max(0, (start - reach) // 16 * 16)
        high = min(rows, -(-(start + size + reach) // 16) * 16)
        tiles.append((start, size, low, high - low, offset))
        offset += high - low
    return tiles, offset


def row_tile(rows, most):
    for size in range(most, 15, -16):
        if rows % size == 0:
            return size
    return rows


LONG = pl.CostEstimate(flops=10**10, bytes_accessed=1, transcendentals=0)


def whole(shape):
    return pl.BlockSpec(shape, lambda *_: (0,) * len(shape), pipeline_mode=pl.Buffered(1))


def out_whole(shape):
    return pl.BlockSpec(shape, lambda *_: (0,) * len(shape))


SMEM = pl.BlockSpec(memory_space=pltpu.SMEM)
VMEM = pl.BlockSpec(memory_space=pltpu.VMEM)
ANY = pl.BlockSpec(memory_space=pl.ANY)


def shape_of(shape, dtype=bf16):
    return jax.ShapeDtypeStruct(tuple(shape), dtype)


class Order:
    def __init__(self, place):
        self.place, self.last = place, None

    def __call__(self, kernel, name, arrays, in_specs, outs, grid=(), scratch=(), into=(), after=()):
        in_specs, arrays = list(in_specs), list(arrays)
        seen = 1 + len(arrays)
        aliases = {seen + i: i for i in range(len(into))}
        extra = (list(into) or ([] if self.last is None else [self.last])) + list(after)
        in_specs += [ANY] * len(extra)
        arrays += extra

        def body(*refs):
            kernel(*refs[:seen], *refs[seen + len(extra) :])

        result = pl.pallas_call(
            body,
            grid_spec=pltpu.PrefetchScalarGridSpec(
                num_scalar_prefetch=1,
                grid=grid,
                in_specs=in_specs,
                out_specs=tuple(spec for spec, _ in outs),
                scratch_shapes=list(scratch),
            ),
            out_shape=tuple(shape for _, shape in outs),
            cost_estimate=LONG,
            input_output_aliases=aliases,
            compiler_params=pltpu.CompilerParams(vmem_limit_bytes=VMEM_BYTES),
            name=name,
        )(self.place, *arrays)
        self.last = result[0]
        return result


Z, CORE, Y, X, SEQ = range(5)


def position():
    dp, fsdp = lax.axis_index("dp"), lax.axis_index("fsdp")
    seq = dp * lax.axis_size("fsdp") + fsdp
    return jnp.stack([fsdp // 2, fsdp % 2, dp // 2, dp % 2, seq]).astype(jnp.int32)


def swap(value, name, dp=0, fsdp=0):
    m, n = lax.axis_size("dp"), lax.axis_size("fsdp")
    pairs = [(i * n + j, (i ^ dp) * n + (j ^ fsdp)) for i in range(m) for j in range(n)]
    with jax.named_scope(f"{name}_{dp}_{fsdp}"):
        return lax.ppermute(value, ("dp", "fsdp"), pairs)


class Weight:
    def __init__(self, arrays, column, shape):
        self.arrays, self.column, self.shape = list(arrays), column, tuple(shape)
        if len(self.arrays) == 1:
            self.scratch = self.shape
        else:
            levels, rows, _ = arrays[0].shape
            self.scratch = (levels, 2, rows, shape[1])

    def copies(self, place, refs, weight, sems, first):
        columns = pl.ds(self.column, self.shape[1])
        if len(refs) == 1:
            return [pltpu.make_async_copy(refs[0], weight, sems.at[first])]
        return [
            pltpu.make_async_copy(ref.at[:, :, columns], weight.at[:, place[CORE] ^ i], sems.at[first + i])
            for i, ref in enumerate(refs)
        ]


def matrix(ref, columns=slice(None)):
    if len(ref.shape) == 2:
        return ref[:, columns]
    value = ref[:, :, :, columns]
    return value.reshape(-1, value.shape[-1])


def fetch_all(place, weights, arrays, scratch, sems):
    copies = []
    for weight, refs, target in zip(weights, arrays, scratch):
        copies += weight.copies(place, refs, target, sems, len(copies))
    for copy in copies:
        copy.start()
    for copy in copies:
        copy.wait()


def split_refs(refs, weights):
    groups, at = [], 0
    for weight in weights:
        groups.append(refs[at : at + len(weight.arrays)])
        at += len(weight.arrays)
    return groups, refs[at:]


def weight_scratch(weights):
    scratch = [pltpu.VMEM(w.scratch, bf16) for w in weights]
    return scratch + [pltpu.SemaphoreType.DMA((sum(len(w.arrays) for w in weights),))]


def mask_kernel(tiles, place_ref, counts_ref, bias_ref, seg_ref):
    rows = seg_ref.shape[0]
    slots = counts_ref.shape[1]
    seq = place_ref[SEQ]
    ends, total = [], jnp.int32(0)
    for slot in range(slots):
        total = total + counts_ref[seq, slot]
        ends.append(total)
    places = lax.broadcasted_iota(jnp.int32, (rows, TILE), 0)
    seg = jnp.zeros((rows, TILE), jnp.int32)
    for end in ends:
        seg = seg + jnp.where(places >= end, 1, 0)
    seg_ref[...] = seg
    lanes = lax.broadcasted_iota(jnp.int32, (8, TILE), 1)
    for start, size, low, keys, offset in tiles:
        own = start + jnp.where(lanes >= size, lanes - size, lanes)
        seg_own = jnp.zeros((8, TILE), jnp.int32)
        for end in ends:
            seg_own = seg_own + jnp.where(own >= end, 1, 0)
        same = seg_ref[low : low + keys, :] == seg_own[0:1, :]
        bias_ref[offset : offset + keys, :] = jnp.where(same, 0.0, MASKED).astype(f32)


def make_masks(order, counts, rows):
    tiles, total = attention_tiles(rows)
    return order(
        functools.partial(mask_kernel, tiles),
        "masks",
        [counts],
        [SMEM],
        [(out_whole((total, TILE)), shape_of((total, TILE), f32))],
        scratch=[pltpu.VMEM((rows, TILE), jnp.int32)],
    )[0]


def normed(values):
    center = values - jnp.mean(values, axis=-1, keepdims=True)
    spread = jnp.mean(center * center, axis=-1, keepdims=True)
    inverse = lax.rsqrt(spread + EPSILON)
    return center * inverse, inverse


def qkv_kernel(scale, weight, place_ref, tok_ref, gain_ref, shift_ref, qb_ref, vb_ref, *refs):
    arrays, (h_ref, q_ref, k_ref, v_ref, w_ref, sems) = split_refs(refs, [weight])
    width = tok_ref.shape[1]

    @pl.when(pl.program_id(0) == 0)
    def _():
        fetch_all(place_ref, [weight], arrays, [w_ref], sems)

    n1, _ = normed(tok_ref[...].astype(f32))
    hidden = (n1 * gain_ref[...].astype(f32) + shift_ref[...].astype(f32)).astype(bf16)
    h_ref[...] = hidden
    q = dot_nn(hidden, matrix(w_ref, slice(0, width)))
    q_ref[...] = ((q + qb_ref[...].astype(f32)) * scale).astype(bf16)
    k = dot_nn(hidden, matrix(w_ref, slice(width, 2 * width)))
    k_ref[...] = k.astype(bf16)
    v = dot_nn(hidden, matrix(w_ref, slice(2 * width, 3 * width)))
    v_ref[...] = (v + vb_ref[...].astype(f32)).astype(bf16)


def project_qkv(order, tokens, gain, shift, b_q, b_v, weight):
    rows, width = tokens.shape
    scale = (width // HEADS) ** (-0.5)
    size = row_tile(rows, 320)
    rowwise = pl.BlockSpec((size, width), lambda i, p: (i, 0))
    return order(
        functools.partial(qkv_kernel, scale, weight),
        "norm_qkv",
        [tokens, gain, shift, b_q, b_v] + weight.arrays,
        [rowwise] + [whole(gain.shape)] * 4 + [ANY] * len(weight.arrays),
        [(rowwise, shape_of((rows, width)))] * 4,
        grid=(rows // size,),
        scratch=weight_scratch([weight]),
    )


def stack_heads(pair, size):
    lanes = lax.broadcasted_iota(jnp.int32, pair.shape, 1)
    half = pair.shape[1] // 2
    zero = jnp.zeros_like(pair)
    first = jnp.where(lanes < half, pair, zero)
    second = jnp.where(lanes < half, zero, pair)
    return jnp.concatenate([first, second], axis=0)


def both(bias, size):
    return bias if size < TILE else jnp.concatenate([bias, bias], axis=1)


def unstack(columns, size, half):
    return jnp.concatenate([columns[:half, :size], columns[half:, size:]], axis=0).T


def attend_kernel(tiles, place_ref, bias_ref, q_ref, k_ref, v_ref, o_ref, lse_ref):
    half = q_ref.shape[1] // 2
    for index, (start, size, low, keys, offset) in enumerate(tiles):
        stacked = stack_heads(q_ref[start : start + size, :], size)
        scores = dot_nt(k_ref[low : low + keys, :], stacked)
        scores = scores + both(bias_ref[offset : offset + keys, :], size)
        top = jnp.max(scores, axis=0, keepdims=True)
        weights = jnp.exp(scores - top)
        total = jnp.sum(weights, axis=0, keepdims=True)
        probs = (weights * (1.0 / total)).astype(bf16)
        columns = dot_tn(v_ref[low : low + keys, :], probs)
        o_ref[start : start + size, :] = unstack(columns, size, half).astype(bf16)
        lse_ref[0, index : index + 1, : 2 * size] = top + jnp.log(total)


def attend(order, bias, q, k, v):
    rows, width = q.shape
    tiles, total = attention_tiles(rows)
    span = 2 * (width // HEADS)
    pairs = HEADS // 2
    column = pl.BlockSpec((rows, span), lambda i, p: (0, i))
    return order(
        functools.partial(attend_kernel, tiles),
        "attend",
        [bias, q, k, v],
        [whole(bias.shape), column, column, column],
        [
            (column, shape_of((rows, width))),
            (
                pl.BlockSpec((1, len(tiles), 2 * TILE), lambda i, p: (i, 0, 0)),
                shape_of((pairs, len(tiles), 2 * TILE), f32),
            ),
        ],
        grid=(pairs,),
    )


def attend_back_kernel(
    tiles, scale, place_ref, bias_ref, q_ref, k_ref, v_ref, o_ref, do_ref, lse_ref, d_ref, dqv_ref, dk_sum, dv_sum
):
    half = q_ref.shape[1] // 2
    dk_sum[...] = jnp.zeros_like(dk_sum)
    dv_sum[...] = jnp.zeros_like(dv_sum)
    dq_total = jnp.zeros((1, 2 * half), f32)
    for index, (start, size, low, keys, offset) in enumerate(tiles):
        window = slice(low, low + keys)
        rows = slice(start, start + size)
        q2 = stack_heads(q_ref[rows, :], size)
        grads = do_ref[rows, :]
        do2 = stack_heads(grads, size)
        scores = dot_nt(k_ref[window, :], q2) + both(bias_ref[offset : offset + keys, :], size)
        probs = jnp.exp(scores - lse_ref[0, index : index + 1, : 2 * size])
        dprobs = dot_nt(v_ref[window, :], do2)
        meet = (grads.astype(f32) * o_ref[rows, :].astype(f32)).T
        delta = jnp.concatenate(
            [
                jnp.sum(meet[:half, :], axis=0, keepdims=True),
                jnp.sum(meet[half:, :], axis=0, keepdims=True),
            ],
            axis=1,
        )
        dv_sum[window, :] += dot_nn(probs.astype(bf16), do2)
        dscores = (probs * (dprobs - delta)).astype(bf16)
        dk_sum[window, :] += dot_nn(dscores, q2)
        columns = dot_tn(k_ref[window, :], dscores)
        dq = unstack(columns, size, half).astype(bf16) * bf16(scale)
        d_ref[0, rows, :] = dq
        dq_total = dq_total + jnp.sum(dq.astype(f32), axis=0, keepdims=True)
    d_ref[1, :, :] = dk_sum[...].astype(bf16)
    dv = dv_sum[...].astype(bf16)
    d_ref[2, :, :] = dv
    dqv_ref[0:1, :] = dq_total
    dqv_ref[1:2, :] = jnp.sum(dv.astype(f32), axis=0, keepdims=True)


def attend_back(order, bias, q, k, v, o, do, lse):
    rows, width = q.shape
    tiles, total = attention_tiles(rows)
    span = 2 * (width // HEADS)
    pairs = HEADS // 2
    scale = (width // HEADS) ** (-0.5)
    column = pl.BlockSpec((rows, span), lambda i, p: (0, i))
    return order(
        functools.partial(attend_back_kernel, tiles, scale),
        "attend_back",
        [bias, q, k, v, o, do, lse],
        [whole(bias.shape)]
        + [column] * 5
        + [pl.BlockSpec((1, len(tiles), 2 * TILE), lambda i, p: (i, 0, 0))],
        [
            (pl.BlockSpec((3, rows, span), lambda i, p: (0, 0, i)), shape_of((3, rows, width))),
            (pl.BlockSpec((2, span), lambda i, p: (0, i)), shape_of((2, width), f32)),
        ],
        grid=(pairs,),
        scratch=[pltpu.VMEM((rows, span), f32)] * 2,
    )


PARTS = 4


def middle_kernel(weights, place_ref, counts_ref, tok_ref, o_ref, cot_out_ref, cot_align_ref, *refs):
    b_proj_ref, gain_ref, shift_ref, b_up_ref, b_down_ref, b_head_ref = refs[:6]
    arrays, refs = split_refs(refs[6:], weights)
    out_ref, aligned_ref, z_ref, e_ref, h_ref, g_ref, du_ref, dm_ref, dx_ref, da_ref, do_ref = refs[:11]
    s_head_ref, s_down_ref, s_up_ref, s_gain_ref, s_shift_ref, s_proj_ref = refs[11:17]
    w_proj_ref, w_up_ref, w_down_ref, w_head_ref, sems = refs[17:]
    step = pl.program_id(0)
    size, width = tok_ref.shape
    hidden_units = w_up_ref.shape[-1]
    part = hidden_units // PARTS
    seq = place_ref[SEQ]
    total = jnp.int32(0)
    for slot in range(counts_ref.shape[1]):
        total = total + counts_ref[seq, slot]
    places = lax.broadcasted_iota(jnp.int32, (size, 1), 0) + step * size
    valid = jnp.where(places < total, 1.0, 0.0).astype(f32)

    @pl.when(step == 0)
    def _():
        fetch_all(place_ref, weights, arrays, [w_proj_ref, w_up_ref, w_down_ref, w_head_ref], sems)
        for ref in (s_head_ref, s_down_ref, s_up_ref, s_gain_ref, s_shift_ref, s_proj_ref):
            ref[...] = jnp.zeros_like(ref)

    x1 = tok_ref[...].astype(f32) + dot_nn(o_ref[...], matrix(w_proj_ref)) + b_proj_ref[...].astype(f32)
    n2, inverse = normed(x1)
    gain = gain_ref[...].astype(f32)
    h2 = (n2 * gain + shift_ref[...].astype(f32)).astype(bf16)
    h_ref[...] = h2

    e_al = (cot_align_ref[...].astype(f32) * valid).astype(bf16)
    e_ref[...] = e_al
    s_head_ref[...] += jnp.sum(e_al.astype(f32), axis=0, keepdims=True)
    dx2 = cot_out_ref[...].astype(f32) * valid + dot_nt(e_al, matrix(w_head_ref))
    dm = dx2.astype(bf16)
    dm_ref[...] = dm
    s_down_ref[...] += jnp.sum(dm.astype(f32), axis=0, keepdims=True)

    x2 = x1 + b_down_ref[...].astype(f32)
    dh2 = jnp.zeros((size, width), f32)
    for index in range(PARTS):
        span = slice(index * part, (index + 1) * part)
        u = dot_nn(h2, matrix(w_up_ref, span)) + b_up_ref[:, span].astype(f32)
        cdf = 0.5 * (1.0 + lax.erf(u * (1.0 / math.sqrt(2.0))))
        pdf = jnp.exp(-0.5 * u * u) * (1.0 / math.sqrt(2.0 * math.pi))
        g = (u * cdf).astype(bf16)
        g_ref[:, span] = g
        x2 = x2 + dot_nn(g, w_down_ref[span, :])
        du = (dot_nt(dm, w_down_ref[span, :]) * (cdf + u * pdf)).astype(bf16)
        du_ref[:, span] = du
        s_up_ref[:, span] += jnp.sum(du.astype(f32), axis=0, keepdims=True)
        dh2 = dh2 + dot_nt(du, matrix(w_up_ref, span))
    out_ref[...] = (x2 * valid).astype(bf16)
    z = x2.astype(bf16)
    z_ref[...] = z
    aligned_ref[...] = ((dot_nn(z, matrix(w_head_ref)) + b_head_ref[...].astype(f32)) * valid).astype(bf16)

    s_gain_ref[...] += jnp.sum(dh2 * n2, axis=0, keepdims=True)
    s_shift_ref[...] += jnp.sum(dh2, axis=0, keepdims=True)
    t = dh2 * gain
    inner = t - jnp.mean(t, axis=-1, keepdims=True) - n2 * jnp.mean(t * n2, axis=-1, keepdims=True)
    dx1 = dx2 + inverse * inner
    dx_ref[...] = dx1
    da = dx1.astype(bf16)
    da_ref[...] = da
    s_proj_ref[...] += jnp.sum(da.astype(f32), axis=0, keepdims=True)
    do_ref[...] = dot_nt(da, matrix(w_proj_ref)).astype(bf16)


def middle(order, counts, tokens, o, cot_out, cot_align, weights, small):
    rows, width = tokens.shape
    hidden, align = weights[1].shape[1], weights[3].shape[1]
    size = row_tile(rows, 240)

    def by_row(columns):
        return pl.BlockSpec((size, columns), lambda i, p: (i, 0))

    def row_shape(columns, dtype=bf16):
        return shape_of((rows, columns), dtype)

    outs = [
        (by_row(width), row_shape(width)),
        (by_row(align), row_shape(align)),
        (by_row(width), row_shape(width)),
        (by_row(align), row_shape(align)),
        (by_row(width), row_shape(width)),
        (by_row(hidden), row_shape(hidden)),
        (by_row(hidden), row_shape(hidden)),
        (by_row(width), row_shape(width)),
        (by_row(width), row_shape(width, f32)),
        (by_row(width), row_shape(width)),
        (by_row(width), row_shape(width)),
    ]
    for columns in (align, width, hidden, width, width, width):
        outs.append((out_whole((1, columns)), shape_of((1, columns), f32)))
    arrays = [array for weight in weights for array in weight.arrays]
    return order(
        functools.partial(middle_kernel, weights),
        "middle",
        [counts, tokens, o, cot_out, cot_align, *small, *arrays],
        [SMEM, by_row(width), by_row(width), by_row(width), by_row(align)]
        + [whole(s.shape) for s in small]
        + [ANY] * len(arrays),
        outs,
        grid=(rows // size,),
        scratch=weight_scratch(weights),
    )


def outer_kernel(place_ref, l_ref, r_ref, out_ref):
    out_ref[...] = dot_tn(l_ref[...], r_ref[...]).astype(out_ref.dtype)


def outer(order, left, right, rows_out, columns_out, name):
    rows, m = left.shape
    n = right.shape[1]
    tm, tn = min(rows_out, m), min(columns_out, n)
    return order(
        outer_kernel,
        name,
        [left, right],
        [pl.BlockSpec((rows, tm), lambda i, j, p: (0, i)), pl.BlockSpec((rows, tn), lambda i, j, p: (0, j))],
        [(pl.BlockSpec((tm, tn), lambda i, j, p: (i, j)), shape_of((m, n)))],
        grid=(m // tm, n // tn),
    )[0]


BAND = 96
HALF = BAND // 2
FEW = 16


def outer_split_kernel(place_ref, l_ref, r_ref, keep_ref, send_ref, l_scratch):
    levels, _, _, columns = keep_ref.shape

    @pl.when(pl.program_id(0) == 0)
    def _():
        l_scratch[...] = l_ref[...].T

    right = r_ref[0] if len(r_ref.shape) == 3 else r_ref[...]
    total = dot_nn(l_scratch[...], right).astype(bf16)
    shape = (2, HALF, columns)
    first = place_ref[CORE] == 0
    for z in range(levels):
        low = total[2 * z * BAND : (2 * z + 1) * BAND].reshape(shape)
        high = total[(2 * z + 1) * BAND : (2 * z + 2) * BAND].reshape(shape)
        level = place_ref[Z] ^ z
        keep_ref[level] = jnp.where(first, low, high)
        send_ref[level] = jnp.where(first, high, low)


def outer_split(order, left, right, levels, columns_out, total, at, into, name, after=()):
    rows, m = left.shape
    n = right.shape[-1] * (right.shape[0] if right.ndim == 3 else 1)
    if right.ndim == 3:
        columns_out = right.shape[-1]
        r_spec = pl.BlockSpec((1, rows, columns_out), lambda j, p: (j, 0, 0))
    else:
        r_spec = pl.BlockSpec((rows, columns_out), lambda j, p: (0, j))
    out = shape_of((levels, 2, HALF, total))
    out_spec = pl.BlockSpec((levels, 2, HALF, columns_out), lambda j, p: (0, 0, 0, at // columns_out + j))
    return order(
        outer_split_kernel,
        name,
        [left, right],
        [whole(left.shape), r_spec],
        [(out_spec, out)] * 2,
        grid=(n // columns_out,),
        scratch=[pltpu.VMEM((m, rows), bf16)],
        into=into,
        after=after,
    )


def split_kernel(sets, place_ref, *refs):
    pairs, outs = refs[: 2 * len(sets)], refs[2 * len(sets) :]
    for own in range(4):

        @pl.when(place_ref[Y] * 2 + place_ref[X] == own)
        def _():
            for quarter, out_ref in enumerate(outs):
                y, x = divmod(own ^ quarter, 2)
                at = 0
                for number, members in enumerate(sets):
                    keep_ref, got_ref = pairs[2 * number : 2 * number + 2]
                    first = 0
                    for columns in members:
                        half = columns // 2
                        part = slice(first + x * half, first + (x + 1) * half)
                        out_ref[:, :, at : at + half] = keep_ref[:, y, :, part] + got_ref[:, y, :, part]
                        at, first = at + half, first + columns


def split(order, sets, pairs, name, after):
    levels = pairs[0][0].shape[0]
    total = sum(keep.shape[3] for keep, _ in pairs)
    shape = (levels, HALF, total // 2)
    return order(
        functools.partial(split_kernel, sets),
        name,
        [array for pair in pairs for array in pair],
        [VMEM] * (2 * len(pairs)),
        [(VMEM, shape_of(shape))] * 4,
        after=after,
    )


def levels_kernel(*refs):
    ins, outs = refs[1:5], refs[5:]
    for level, out_ref in enumerate(outs):
        total = ins[0][level].astype(f32)
        for ref in ins[1:]:
            total = total + ref[level].astype(f32)
        out_ref[...] = total.astype(bf16)


def by_level(order, quarters, name, after):
    levels, height, columns = quarters[0].shape
    return order(
        levels_kernel,
        name,
        quarters,
        [VMEM] * 4,
        [(VMEM, shape_of((height, columns)))] * levels,
        after=after,
    )


def add_kernel(*refs):
    total = refs[1][...].astype(f32)
    for ref in refs[2:-1]:
        total = total + ref[...].astype(f32)
    refs[-1][...] = total.astype(bf16)


def add_up(order, arrays, name, after):
    return order(
        add_kernel,
        name,
        arrays,
        [VMEM] * len(arrays),
        [(VMEM, shape_of(arrays[0].shape))],
        after=after,
    )[0]


def join_kernel(members, lengths, widen, place_ref, *refs):
    quarters, narrow, outs, lines = refs[:4], refs[4 : 4 + widen], refs[4 + widen : -1], refs[-1]
    matrices = len(members) - (1 if lengths else 0)
    for ref, out_ref in zip(narrow, outs[matrices:]):
        out_ref[...] = ref[...].astype(f32)
    for x in (0, 1):

        @pl.when(place_ref[X] == x)
        def _():
            for quarter, ref in enumerate(quarters):
                y = place_ref[Y] ^ (quarter // 2)
                across = x ^ (quarter % 2)
                at = 0
                for number, columns in enumerate(members):
                    half = columns // 2
                    if number == matrices:
                        lines[2 * y + across] = ref[0:FEW, at : at + half].astype(f32)
                    else:
                        outs[number][y, :, across * half : (across + 1) * half] = ref[:, at : at + half].astype(f32)
                    at += half

    if lengths:
        each, line = keep_lines([n for part in lengths for n in part]), 0
        for part, out_ref in zip(lengths, outs[matrices + widen :]):
            rows = []
            for length in part:
                pieces = []
                for i in range(lines_of(length)):
                    quarter, row = divmod(line + i, each)
                    pieces.append(lines[quarter, row : row + 1, : min(TILE, length - i * TILE)])
                rows.append(jnp.concatenate(pieces, axis=1) if len(pieces) > 1 else pieces[0])
                line += lines_of(length)
            if len(rows) == 1:
                out_ref[...] = rows[0][0]
            else:
                for i, row in enumerate(rows):
                    out_ref[i : i + 1, :] = row


def join(order, quarters, members, lengths, widen, name):
    matrices = members[:-1] if lengths else members
    outs = [(VMEM, shape_of((2, HALF, columns), f32)) for columns in matrices]
    outs += [(VMEM, shape_of(array.shape, f32)) for array in widen]
    for part in lengths:
        outs.append((VMEM, shape_of((part[0],) if len(part) == 1 else (len(part), part[0]), f32)))
    results = order(
        functools.partial(join_kernel, members, lengths, len(widen)),
        name,
        list(quarters) + list(widen),
        [VMEM] * (4 + len(widen)),
        outs,
        scratch=[pltpu.VMEM((4, FEW, TILE), f32)],
    )
    return [r.reshape(BAND, -1) for r in results[: len(matrices)]] + list(results[len(matrices) :])


class Reduction:
    def __init__(self, order, name, lengths=()):
        self.order, self.name, self.lengths = order, name, lengths
        self.sets, self.pairs = [], []

    def add(self, keep, send, members):
        self.sets.append(members)
        self.pairs.append((keep, swap(send, self.name + "_core", fsdp=1)))

    def split(self, after=()):
        quarters = split(self.order, self.sets, self.pairs, self.name + "_split", after)
        self.quarters = [quarters[0]] + [swap(quarters[j], self.name + "_plane", dp=j) for j in (1, 2, 3)]

    def levels(self, after=()):
        parts = by_level(self.order, self.quarters, self.name + "_levels", after)
        self.parts = [parts[0]]
        self.parts += [swap(part, self.name + "_column", fsdp=2 * level) for level, part in enumerate(parts) if level]

    def total(self, after=()):
        near = add_up(self.order, self.parts, self.name + "_total", after)
        self.near = [near] + [swap(near, self.name + "_back", dp=j) for j in (1, 2, 3)]

    def join(self, widen=()):
        members = [columns for members in self.sets for columns in members]
        return join(self.order, self.near, members, self.lengths, widen, self.name + "_join")


def lines_of(length):
    return -(-length // TILE)


def keep_lines(lengths):
    return -(-sum(lines_of(n) for n in lengths) // 4)


def pack_kernel(lengths, place_ref, *refs):
    vectors, (keep_ref, send_ref) = refs[: len(lengths)], refs[len(lengths) :]
    levels = keep_ref.shape[0]
    first = place_ref[CORE] == 0
    each = keep_lines(lengths)
    values = [ref[...] for ref in vectors]

    def lines(shard):
        rows = []
        for value, length in zip(values, lengths):
            row = value[:, shard * length : (shard + 1) * length]
            if length % TILE:
                row = jnp.concatenate([row, jnp.zeros((1, -length % TILE), f32)], axis=1)
            rows += [row[:, at : at + TILE] for at in range(0, row.shape[1], TILE)]
        return rows

    keep_ref[...] = jnp.zeros_like(keep_ref)
    send_ref[...] = jnp.zeros_like(send_ref)
    for z in range(levels):
        level = place_ref[Z] ^ z
        low, high = lines(2 * z), lines(2 * z + 1)
        for quarter in range(4):
            y, x = divmod(quarter, 2)
            part = slice(quarter * each, (quarter + 1) * each)
            blank = [jnp.zeros((FEW - len(low[part]), TILE), f32)]
            a = jnp.concatenate(low[part] + blank, axis=0)
            b = jnp.concatenate(high[part] + blank, axis=0)
            columns = slice(x * TILE, (x + 1) * TILE)
            keep_ref[level, y, 0:FEW, columns] = jnp.where(first, a, b).astype(bf16)
            send_ref[level, y, 0:FEW, columns] = jnp.where(first, b, a).astype(bf16)


def pack_vectors(order, vectors, levels):
    lengths = [v.shape[1] // (2 * levels) for v in vectors]
    shape = (levels, 2, HALF, 2 * TILE)
    return order(
        functools.partial(pack_kernel, lengths),
        "pack_vectors",
        vectors,
        [VMEM] * len(vectors),
        [(VMEM, shape_of(shape))] * 2,
    )


def unpack_kernel(lengths, place_ref, own_ref, other_ref, *out_refs):
    levels = own_ref.shape[0]
    first = place_ref[CORE] == 0
    shards = []
    for z in range(levels):
        own = own_ref[z].astype(f32)
        other = other_ref[z].astype(f32)
        shards += [jnp.where(first, own, other), jnp.where(first, other, own)]
    at = 0
    for length, out_ref in zip(lengths, out_refs):
        pieces = []
        for shard in shards:
            for line in range(lines_of(length)):
                pieces.append(shard[at + line : at + line + 1, : min(TILE, length - line * TILE)])
        out_ref[...] = jnp.concatenate(pieces, axis=1).astype(bf16)
        at += lines_of(length)


def unpack_vectors(order, own, other, lengths):
    levels = own.shape[0]
    return order(
        functools.partial(unpack_kernel, lengths),
        "unpack_vectors",
        [own, other],
        [VMEM] * 2,
        [(VMEM, shape_of((1, 2 * levels * n))) for n in lengths],
    )


def start_kernel(lengths, groups, place_ref, *refs):
    count = sum(len(g) for g in groups)
    vectors = refs[: len(refs) - count - len(groups)]
    shards, outs = refs[len(vectors) : len(vectors) + count], refs[len(vectors) + count :]
    at = 0
    for group, out_ref in zip(groups, outs):
        column = 0
        for _ in group:
            half = shards[at].shape[1]
            out_ref[:, column : column + half] = shards[at][...]
            column += half
            at += 1
    values = []
    for ref in vectors:
        value = ref[...].astype(f32)
        values += [value[i] for i in range(value.shape[0])] if value.ndim == 2 else [value]
    lines = []
    for value, length in zip(values, lengths):
        if length % TILE:
            value = jnp.concatenate([value, jnp.zeros((-length % TILE,), f32)])
        lines += [value[at : at + TILE].reshape(1, TILE) for at in range(0, value.shape[0], TILE)]
    lines.append(jnp.zeros((HALF - len(lines), TILE), f32))
    outs[0][:, outs[0].shape[1] - TILE :] = jnp.concatenate(lines, axis=0).astype(bf16)


def start_gather(order, vectors, lengths, groups):
    shards = [w for group in groups for w in group]
    outs = []
    for number, group in enumerate(groups):
        shape = (HALF, sum(w.shape[1] // 2 for w in group) + (TILE if number == 0 else 0))
        outs.append((out_whole(shape), shape_of(shape)))
    return order(
        functools.partial(start_kernel, lengths, groups),
        "quarters",
        list(vectors) + shards,
        [whole(v.shape) for v in vectors]
        + [pl.BlockSpec((w.shape[0] // 2, w.shape[1] // 2), lambda i, p: (p[Y], p[X])) for w in shards],
        outs,
        grid=(1,),
    )


def near_kernel(levels, place_ref, *refs):
    got, out_ref, lines = refs[:levels], refs[levels], refs[levels + 1 :]
    columns = out_ref.shape[2]
    for level, ref in enumerate(got):
        if level:
            out_ref[level - 1] = ref[:, :columns]
        for lines_ref in lines:
            lines_ref[place_ref[Z] ^ level] = ref[0:FEW, columns:]


def near_levels(order, got, lines, name):
    levels, (height, columns) = len(got), got[0].shape
    columns -= TILE if lines else 0
    outs = [(VMEM, shape_of((levels - 1, height, columns)))]
    if lines:
        outs.append((VMEM, shape_of((levels, FEW, TILE))))
    return order(
        functools.partial(near_kernel, levels),
        name,
        got,
        [VMEM] * levels,
        outs,
    )


def assemble_kernel(halves, place_ref, *refs):
    shards, refs = refs[: len(halves)], refs[len(halves) :]
    quarters, out_ref = refs[:4], refs[4]
    z = place_ref[Z]
    column = 0
    for shard in shards:
        columns = shard.shape[1]
        for y in (0, 1):
            out_ref[z, y, :, column : column + columns] = shard[y * HALF : (y + 1) * HALF, :]
        column += columns
    for x in (0, 1):

        @pl.when(place_ref[X] == x)
        def _():
            for quarter, ref in enumerate(quarters):
                y = place_ref[Y] ^ (quarter // 2)
                across = x ^ (quarter % 2)
                for level in range(ref.shape[0]):
                    source, column = 0, 0
                    for half in halves:
                        target = column + across * half
                        out_ref[z ^ (level + 1), y, :, target : target + half] = ref[level, :, source : source + half]
                        source, column = source + half, column + 2 * half


def assemble(order, shards, quarters, name):
    levels = quarters[0].shape[0] + 1
    halves = [shard.shape[1] // 2 for shard in shards]
    return order(
        functools.partial(assemble_kernel, halves),
        name,
        list(shards) + list(quarters),
        [VMEM] * (len(shards) + 4),
        [(VMEM, shape_of((levels, 2, HALF, 2 * sum(halves))))],
    )[0].reshape(levels, BAND, -1)


def across_plane(near, name):
    return [near] + [swap(near, name + "_plane", dp=j) for j in (1, 2, 3)]


def first_back_kernel(weight, place_ref, tok_ref, dx_ref, d_ref, gain_ref, *refs):
    arrays, (out_ref, s_gain_ref, s_shift_ref, w_ref, sems) = split_refs(refs, [weight])
    width = tok_ref.shape[1]

    @pl.when(pl.program_id(0) == 0)
    def _():
        fetch_all(place_ref, [weight], arrays, [w_ref], sems)
        s_gain_ref[...] = jnp.zeros_like(s_gain_ref)
        s_shift_ref[...] = jnp.zeros_like(s_shift_ref)

    dh = dot_nt(d_ref[0], matrix(w_ref, slice(0, width)))
    dh = dh + dot_nt(d_ref[1], matrix(w_ref, slice(width, 2 * width)))
    dh = dh + dot_nt(d_ref[2], matrix(w_ref, slice(2 * width, 3 * width)))
    n1, inverse = normed(tok_ref[...].astype(f32))
    s_gain_ref[...] += jnp.sum(dh * n1, axis=0, keepdims=True)
    s_shift_ref[...] += jnp.sum(dh, axis=0, keepdims=True)
    t = dh * gain_ref[...].astype(f32)
    inner = t - jnp.mean(t, axis=-1, keepdims=True) - n1 * jnp.mean(t * n1, axis=-1, keepdims=True)
    out_ref[...] = (dx_ref[...] + inverse * inner).astype(bf16)


def first_back(order, tokens, dx1, dqkv, weight, gain, after):
    rows, width = tokens.shape
    size = row_tile(rows, 320)
    rowwise = pl.BlockSpec((size, width), lambda i, p: (i, 0))
    total = (out_whole((1, width)), shape_of((1, width), f32))
    return order(
        functools.partial(first_back_kernel, weight),
        "first_back",
        [tokens, dx1, dqkv, gain] + weight.arrays,
        [rowwise, rowwise, pl.BlockSpec((3, size, width), lambda i, p: (0, i, 0)), whole(gain.shape)]
        + [ANY] * len(weight.arrays),
        [(rowwise, shape_of((rows, width))), total, total],
        grid=(rows // size,),
        after=after,
        scratch=weight_scratch([weight]),
    )


def local(
    tokens,
    ln1_gain,
    ln1_bias,
    w_qkv,
    qv_bias,
    w_proj,
    proj_bias,
    ln2_gain,
    ln2_bias,
    w_up,
    up_bias,
    w_down,
    down_bias,
    w_head,
    head_bias,
    clip_counts,
    cot_out,
    cot_align,
):
    rows, width = tokens.shape
    shards = lax.axis_size("fsdp")
    levels = shards // 2
    order = Order(position())
    vectors = (ln1_gain, ln1_bias, qv_bias, proj_bias, ln2_gain, ln2_bias, up_bias, down_bias, head_bias)
    parts = [[v.shape[-1]] * (v.size // v.shape[-1]) for v in vectors]
    lengths = [length for part in parts for length in part]
    paired = (
        lax.axis_size("dp") == 4
        and shards % 2 == 0
        and levels in (2, 4, 8)
        and w_qkv.shape[0] == BAND
        and sum(lines_of(n) for n in lengths) <= FEW
    )

    def gather(value):
        return lax.all_gather(value, "fsdp", axis=0, tiled=True)

    def scatter(value):
        return lax.psum_scatter(value, "fsdp", scatter_dimension=0, tiled=True)

    if paired:
        wide = [w_up, w_head, w_proj]
        p_qkv, p_wide = start_gather(order, vectors, lengths, [[w_qkv], wide])
        got = [p_qkv] + [swap(p_qkv, "qkv_column", fsdp=2 * level) for level in range(1, levels)]
        got_wide = [swap(p_wide, "wide_column", fsdp=2 * level) for level in range(2, levels)]
        bias = make_masks(order, clip_counts, rows)
        near, lines = near_levels(order, got, True, "qkv_near")
        quarters = across_plane(near, "qkv")
        other_lines = swap(lines, "vectors_core", fsdp=1)
        own = assemble(order, [w_qkv], quarters, "qkv_assemble")
        full_qkv = Weight([own, swap(own, "qkv_core", fsdp=1)], 0, (width, w_qkv.shape[1]))
        later, own = lax.optimization_barrier((p_wide, own))
        got_wide = [p_wide, swap(later, "wide_column", fsdp=2)] + got_wide
        gathered = unpack_vectors(order, lines, other_lines, lengths)
        (near,) = near_levels(order, got_wide, False, "wide_near")
        quarters = across_plane(near, "wide")
        later, near = lax.optimization_barrier((w_down, near))
        full_down = gather(later)
    else:
        pieces = [piece for v in vectors for piece in ([v[0], v[1]] if v.ndim == 2 else [v])]
        joined = gather(jnp.concatenate(pieces)[None])
        gathered, at = [], 0
        for length in lengths:
            gathered.append(joined[:, at : at + length].reshape(1, -1))
            at += length
        full_qkv, full_proj, full_up, full_head = (
            Weight([full], 0, full.shape) for full in (gather(w) for w in (w_qkv, w_proj, w_up, w_head))
        )
        full_down = gather(w_down)
        bias = make_masks(order, clip_counts, rows)
    gain_one, shift_one, b_q, b_v, b_proj, gain_two, shift_two, b_up, b_down, b_head = gathered
    full_down = Weight([full_down], 0, full_down.shape)
    h1, q, k, v = project_qkv(order, tokens, gain_one, shift_one, b_q, b_v, full_qkv)
    o, lse = attend(order, bias, q, k, v)
    if paired:
        own = assemble(order, wide, quarters, "wide_assemble")
        both_cores = [own, swap(own, "wide_core", fsdp=1)]
        at = [0, w_up.shape[1], w_up.shape[1] + w_head.shape[1]]
        full_up, full_head, full_proj = (
            Weight(both_cores, column, (width, w.shape[1])) for column, w in zip(at, wide)
        )
    (block_out, aligned, z, e_al, h2, g, du, dm, dx1, da, do, s_head, s_down, s_up, s_gain, s_shift, s_proj) = middle(
        order,
        clip_counts,
        tokens,
        o,
        cot_out,
        cot_align,
        (full_proj, full_up, full_down, full_head),
        (b_proj, gain_two, shift_two, b_up, b_down, b_head),
    )
    d_down = scatter(outer(order, g, dm, 512, 768, "grad_down"))
    if paired:
        r_wide = Reduction(order, "wide")
        pair = outer_split(order, h2, du, levels, 768, w_up.shape[1], 0, (), "grad_up")
        r_wide.add(*pair, [w_up.shape[1]])
        members = [w_head.shape[1], w_proj.shape[1]]
        pair = outer_split(order, z, e_al, levels, 512, sum(members), 0, (), "grad_head")
        pair = outer_split(order, o, da, levels, 256, sum(members), members[0], pair, "grad_proj")
        r_wide.add(*pair, members)
        r_wide.split()
    dqkv, s_qv = attend_back(order, bias, q, k, v, o, do, lse)
    if paired:
        r_qkv = Reduction(order, "qkv", parts)
        n = w_qkv.shape[1]
        r_qkv.add(*outer_split(order, h1, dqkv, levels, width, n, 0, (), "grad_qkv"), [n])
    grad_tokens, s_gain_one, s_shift_one = first_back(order, tokens, dx1, dqkv, full_qkv, gain_one, [d_down])
    d_down = lax.psum(d_down, "dp")
    sums = (s_gain_one, s_shift_one, s_qv[0:1], s_qv[1:2], s_proj, s_gain, s_shift, s_up, s_down, s_head)
    if paired:
        r_qkv.add(*pack_vectors(order, sums, levels), [2 * TILE])
        r_wide.levels()
        r_qkv.split()
        r_wide.total()
        r_qkv.levels()
        r_qkv.total(after=[d_down])
        d_up, d_head, d_proj = r_wide.join()
        d_qkv, d_down, *mine = r_qkv.join([d_down])
    else:

        def reduce(value):
            return lax.psum(scatter(value), "dp").astype(f32)

        d_down = d_down.astype(f32)
        d_up = reduce(outer(order, h2, du, 768, 512, "grad_up"))
        d_head = reduce(outer(order, z, e_al, 768, 512, "grad_head"))
        d_proj = reduce(outer(order, o, da, 768, 384, "grad_proj"))
        d_qkv = reduce(outer(order, h1, jnp.concatenate([dqkv[0], dqkv[1], dqkv[2]], axis=1), 768, 768, "grad_qkv"))
        joined = jnp.concatenate([s.reshape(shards, -1) for s in sums], axis=1)
        joined = lax.psum(lax.psum_scatter(joined, "fsdp", scatter_dimension=0, tiled=True), "dp")[0]
        mine, at = [], 0
        for part in parts:
            size = sum(part)
            mine.append(joined[at : at + size].reshape((part[0],) if len(part) == 1 else (len(part), -1)))
            at += size
    d_gain_one, d_shift_one, d_qv, d_b_proj, d_gain_two, d_shift_two, d_b_up, d_b_down, d_b_head = mine
    return (
        block_out,
        aligned,
        grad_tokens,
        d_gain_one,
        d_shift_one,
        d_qkv,
        d_qv,
        d_proj,
        d_b_proj,
        d_gain_two,
        d_shift_two,
        d_up,
        d_b_up,
        d_down,
        d_b_down,
        d_head,
        d_b_head,
    )


def solution(mesh):
    rows = P(("dp", "fsdp"), None)
    matrix, vector, pair = P("fsdp", None), P("fsdp"), P(None, "fsdp")
    return jax.shard_map(
        local,
        mesh=mesh,
        in_specs=(
            rows,
            vector,
            vector,
            matrix,
            pair,
            matrix,
            vector,
            vector,
            vector,
            matrix,
            vector,
            matrix,
            vector,
            matrix,
            vector,
            P(),
            rows,
            rows,
        ),
        out_specs=(
            rows,
            rows,
            rows,
            vector,
            vector,
            matrix,
            pair,
            matrix,
            vector,
            vector,
            vector,
            matrix,
            vector,
            matrix,
            vector,
            matrix,
            vector,
        ),
        check_vma=False,
    )
```

```python
import functools
import math

import jax
import jax.numpy as jnp
from jax import lax
from jax.experimental import pallas as pl
from jax.experimental.pallas import tpu as pltpu
from jax.sharding import PartitionSpec as P

HEADS = 12
LONGEST = 157
EPSILON = 1e-06
MASKED = -1e30
TILE = 128

f32 = jnp.float32
bf16 = jnp.bfloat16


def dot_nn(left, right):
    return lax.dot_general(left, right, (((1,), (0,)), ((), ())), preferred_element_type=f32)


def dot_nt(left, right):
    return lax.dot_general(left, right, (((1,), (1,)), ((), ())), preferred_element_type=f32)


def dot_tn(left, right):
    return lax.dot_general(left, right, (((0,), (0,)), ((), ())), preferred_element_type=f32)


def attention_tiles(rows):
    tiles, offset = [], 0
    reach = LONGEST - 1
    for start in range(0, rows, TILE):
        size = min(TILE, rows - start)
        low = max(0, (start - reach) // 16 * 16)
        high = min(rows, -(-(start + size + reach) // 16) * 16)
        tiles.append((start, size, low, high - low, offset))
        offset += high - low
    return tiles, offset


def row_tile(rows, most):
    for size in range(most, 15, -16):
        if rows % size == 0:
            return size
    return rows


USUAL = 10
TIMES = {
    "attend_back": 20,
    "first_back": 20,
}


def duration(name):
    return pl.CostEstimate(flops=TIMES.get(name, USUAL) * 10**9, bytes_accessed=1, transcendentals=0)


def whole(shape):
    return pl.BlockSpec(shape, lambda *_: (0,) * len(shape), pipeline_mode=pl.Buffered(1))


def out_whole(shape):
    return pl.BlockSpec(shape, lambda *_: (0,) * len(shape))


SMEM = pl.BlockSpec(memory_space=pltpu.SMEM)
VMEM = pl.BlockSpec(memory_space=pltpu.VMEM)
ANY = pl.BlockSpec(memory_space=pl.ANY)


def shape_of(shape, dtype=bf16):
    return jax.ShapeDtypeStruct(tuple(shape), dtype)


class Order:
    def __init__(self, place):
        self.place, self.last = place, None

    def __call__(self, kernel, name, arrays, in_specs, outs, grid=(), scratch=(), into=(), after=(), vmem=32):
        in_specs, arrays = list(in_specs), list(arrays)
        seen = 1 + len(arrays)
        aliases = {seen + i: i for i in range(len(into))}
        extra = (list(into) or ([] if self.last is None else [self.last])) + list(after)
        in_specs += [ANY] * len(extra)
        arrays += extra

        def body(*refs):
            kernel(*refs[:seen], *refs[seen + len(extra) :])

        result = pl.pallas_call(
            body,
            grid_spec=pltpu.PrefetchScalarGridSpec(
                num_scalar_prefetch=1,
                grid=grid,
                in_specs=in_specs,
                out_specs=tuple(spec for spec, _ in outs),
                scratch_shapes=list(scratch),
            ),
            out_shape=tuple(shape for _, shape in outs),
            cost_estimate=duration(name),
            input_output_aliases=aliases,
            compiler_params=pltpu.CompilerParams(vmem_limit_bytes=vmem << 20),
            name=name,
        )(self.place, *arrays)
        self.last = result[0]
        return result


Z, CORE, Y, X, SEQ = range(5)


def position():
    dp, fsdp = lax.axis_index("dp"), lax.axis_index("fsdp")
    seq = dp * lax.axis_size("fsdp") + fsdp
    return jnp.stack([fsdp // 2, fsdp % 2, dp // 2, dp % 2, seq]).astype(jnp.int32)


def swap(value, name, dp=0, fsdp=0):
    m, n = lax.axis_size("dp"), lax.axis_size("fsdp")
    pairs = [(i * n + j, (i ^ dp) * n + (j ^ fsdp)) for i in range(m) for j in range(n)]
    with jax.named_scope(f"{name}_{dp}_{fsdp}"):
        return lax.ppermute(value, ("dp", "fsdp"), pairs)


class Weight:
    def __init__(self, arrays, column, shape):
        self.arrays, self.column, self.shape = list(arrays), column, tuple(shape)
        if len(self.arrays) == 1:
            self.scratch = self.shape
        else:
            levels, rows, _ = arrays[0].shape
            self.scratch = (levels, 2, rows, shape[1])

    def copies(self, place, refs, weight, sems, first):
        columns = pl.ds(self.column, self.shape[1])
        if len(refs) == 1:
            return [pltpu.make_async_copy(refs[0], weight, sems.at[first])]
        return [
            pltpu.make_async_copy(ref.at[:, :, columns], weight.at[:, place[CORE] ^ i], sems.at[first + i])
            for i, ref in enumerate(refs)
        ]


def matrix(ref, columns=slice(None)):
    if len(ref.shape) == 2:
        return ref[:, columns]
    value = ref[:, :, :, columns]
    return value.reshape(-1, value.shape[-1])


def fetch_all(place, weights, arrays, scratch, sems):
    copies = []
    for weight, refs, target in zip(weights, arrays, scratch):
        copies += weight.copies(place, refs, target, sems, len(copies))
    for copy in copies:
        copy.start()
    for copy in copies:
        copy.wait()


def split_refs(refs, weights):
    groups, at = [], 0
    for weight in weights:
        groups.append(refs[at : at + len(weight.arrays)])
        at += len(weight.arrays)
    return groups, refs[at:]


def weight_scratch(weights):
    scratch = [pltpu.VMEM(w.scratch, bf16) for w in weights]
    return scratch + [pltpu.SemaphoreType.DMA((sum(len(w.arrays) for w in weights),))]


GAIN_ONE, SHIFT_ONE, B_Q, B_V, B_PROJ, GAIN_TWO, SHIFT_TWO, B_UP, B_DOWN, B_HEAD = range(10)
ROWS = 16


def row(vectors_ref, index, length):
    return vectors_ref[index : index + 1, :length].astype(f32)


def mask_kernel(tiles, place_ref, counts_ref, bias_ref, seg_ref):
    rows = seg_ref.shape[0]
    slots = counts_ref.shape[1]
    seq = place_ref[SEQ]
    ends, total = [], jnp.int32(0)
    for slot in range(slots):
        total = total + counts_ref[seq, slot]
        ends.append(total)
    places = lax.broadcasted_iota(jnp.int32, (rows, TILE), 0)
    seg = jnp.zeros((rows, TILE), jnp.int32)
    for end in ends:
        seg = seg + jnp.where(places >= end, 1, 0)
    seg_ref[...] = seg
    lanes = lax.broadcasted_iota(jnp.int32, (8, TILE), 1)
    for start, size, low, keys, offset in tiles:
        own = start + jnp.where(lanes >= size, lanes - size, lanes)
        seg_own = jnp.zeros((8, TILE), jnp.int32)
        for end in ends:
            seg_own = seg_own + jnp.where(own >= end, 1, 0)
        same = seg_ref[low : low + keys, :] == seg_own[0:1, :]
        bias_ref[offset : offset + keys, :] = jnp.where(same, 0.0, MASKED).astype(f32)


def make_masks(order, counts, rows):
    tiles, total = attention_tiles(rows)
    return order(
        functools.partial(mask_kernel, tiles),
        "masks",
        [counts],
        [SMEM],
        [(out_whole((total, TILE)), shape_of((total, TILE), f32))],
        scratch=[pltpu.VMEM((rows, TILE), jnp.int32)],
    )[0]


def normed(values):
    center = values - jnp.mean(values, axis=-1, keepdims=True)
    spread = jnp.mean(center * center, axis=-1, keepdims=True)
    inverse = lax.rsqrt(spread + EPSILON)
    return center * inverse, inverse


def qkv_kernel(scale, weight, place_ref, tok_ref, vec_ref, *refs):
    arrays, (h_ref, q_ref, k_ref, v_ref, w_ref, sems) = split_refs(refs, [weight])
    width = tok_ref.shape[1]

    @pl.when(pl.program_id(0) == 0)
    def _():
        fetch_all(place_ref, [weight], arrays, [w_ref], sems)

    n1, _ = normed(tok_ref[...].astype(f32))
    hidden = (n1 * row(vec_ref, GAIN_ONE, width) + row(vec_ref, SHIFT_ONE, width)).astype(bf16)
    h_ref[...] = hidden
    q = dot_nn(hidden, matrix(w_ref, slice(0, width)))
    q_ref[...] = ((q + row(vec_ref, B_Q, width)) * scale).astype(bf16)
    k = dot_nn(hidden, matrix(w_ref, slice(width, 2 * width)))
    k_ref[...] = k.astype(bf16)
    v = dot_nn(hidden, matrix(w_ref, slice(2 * width, 3 * width)))
    v_ref[...] = (v + row(vec_ref, B_V, width)).astype(bf16)


def project_qkv(order, tokens, vectors, weight):
    rows, width = tokens.shape
    scale = (width // HEADS) ** (-0.5)
    size = row_tile(rows, 320)
    rowwise = pl.BlockSpec((size, width), lambda i, p: (i, 0))
    return order(
        functools.partial(qkv_kernel, scale, weight),
        "norm_qkv",
        [tokens, vectors] + weight.arrays,
        [rowwise, whole(vectors.shape)] + [ANY] * len(weight.arrays),
        [(rowwise, shape_of((rows, width)))] * 4,
        grid=(rows // size,),
        scratch=weight_scratch([weight]),
    )


def stack_heads(pair, size):
    lanes = lax.broadcasted_iota(jnp.int32, pair.shape, 1)
    half = pair.shape[1] // 2
    zero = jnp.zeros_like(pair)
    first = jnp.where(lanes < half, pair, zero)
    second = jnp.where(lanes < half, zero, pair)
    return jnp.concatenate([first, second], axis=0)


def both(bias, size):
    return bias if size < TILE else jnp.concatenate([bias, bias], axis=1)


def unstack(columns, size, half):
    return jnp.concatenate([columns[:half, :size], columns[half:, size:]], axis=0).T


def attend_kernel(tiles, place_ref, bias_ref, q_ref, k_ref, v_ref, o_ref, lse_ref):
    half = q_ref.shape[1] // 2
    scores = []
    for start, size, low, keys, offset in tiles:
        stacked = stack_heads(q_ref[start : start + size, :], size)
        value = dot_nt(k_ref[low : low + keys, :], stacked)
        scores.append(value + both(bias_ref[offset : offset + keys, :], size))
    parts = []
    for value in scores:
        top = jnp.max(value, axis=0, keepdims=True)
        weights = jnp.exp(value - top)
        parts.append((weights.astype(bf16), top, jnp.sum(weights, axis=0, keepdims=True)))
    for index, (start, size, low, keys, _) in enumerate(tiles):
        weights, top, total = parts[index]
        columns = dot_tn(v_ref[low : low + keys, :], weights) * (1.0 / total)
        o_ref[start : start + size, :] = unstack(columns, size, half).astype(bf16)
        lse_ref[0, index : index + 1, : 2 * size] = top + jnp.log(total)


def attend(order, bias, q, k, v):
    rows, width = q.shape
    tiles, total = attention_tiles(rows)
    span = 2 * (width // HEADS)
    pairs = HEADS // 2
    column = pl.BlockSpec((rows, span), lambda i, p: (0, i))
    return order(
        functools.partial(attend_kernel, tiles),
        "attend",
        [bias, q, k, v],
        [whole(bias.shape), column, column, column],
        [
            (column, shape_of((rows, width))),
            (
                pl.BlockSpec((1, len(tiles), 2 * TILE), lambda i, p: (i, 0, 0)),
                shape_of((pairs, len(tiles), 2 * TILE), f32),
            ),
        ],
        grid=(pairs,),
    )


def attend_back_kernel(
    tiles, scale, place_ref, bias_ref, q_ref, k_ref, v_ref, o_ref, do_ref, lse_ref, d_ref, dqv_ref, dk_sum, dv_sum
):
    half = q_ref.shape[1] // 2
    dk_sum[...] = jnp.zeros_like(dk_sum)
    dv_sum[...] = jnp.zeros_like(dv_sum)
    dq_total = jnp.zeros((1, 2 * half), f32)
    for pair in range(0, len(tiles), 2):
        group = list(enumerate(tiles))[pair : pair + 2]
        held = []
        for index, (start, size, low, keys, offset) in group:
            window, rows = slice(low, low + keys), slice(start, start + size)
            q2 = stack_heads(q_ref[rows, :], size)
            grads = do_ref[rows, :]
            do2 = stack_heads(grads, size)
            scores = dot_nt(k_ref[window, :], q2) + both(bias_ref[offset : offset + keys, :], size)
            dprobs = dot_nt(v_ref[window, :], do2)
            meet = (grads.astype(f32) * o_ref[rows, :].astype(f32)).T
            delta = jnp.concatenate(
                [
                    jnp.sum(meet[:half, :], axis=0, keepdims=True),
                    jnp.sum(meet[half:, :], axis=0, keepdims=True),
                ],
                axis=1,
            )
            held.append((q2, do2, scores, dprobs, delta))
        lows = []
        for (index, (start, size, *_)), (q2, do2, scores, dprobs, delta) in zip(group, held):
            probs = jnp.exp(scores - lse_ref[0, index : index + 1, : 2 * size])
            lows.append((probs.astype(bf16), (probs * (dprobs - delta)).astype(bf16)))
        for (index, (start, size, low, keys, _)), (q2, do2, *_), (probs, dscores) in zip(group, held, lows):
            window, rows = slice(low, low + keys), slice(start, start + size)
            dv_sum[window, :] += dot_nn(probs, do2)
            dk_sum[window, :] += dot_nn(dscores, q2)
            columns = dot_tn(k_ref[window, :], dscores)
            dq = unstack(columns, size, half).astype(bf16) * bf16(scale)
            d_ref[0, rows, :] = dq
            dq_total = dq_total + jnp.sum(dq.astype(f32), axis=0, keepdims=True)
    d_ref[1, :, :] = dk_sum[...].astype(bf16)
    dv = dv_sum[...].astype(bf16)
    d_ref[2, :, :] = dv
    dqv_ref[0:1, :] = dq_total
    dqv_ref[1:2, :] = jnp.sum(dv.astype(f32), axis=0, keepdims=True)


def attend_back(order, bias, q, k, v, o, do, lse):
    rows, width = q.shape
    tiles, total = attention_tiles(rows)
    span = 2 * (width // HEADS)
    pairs = HEADS // 2
    scale = (width // HEADS) ** (-0.5)
    column = pl.BlockSpec((rows, span), lambda i, p: (0, i))
    return order(
        functools.partial(attend_back_kernel, tiles, scale),
        "attend_back",
        [bias, q, k, v, o, do, lse],
        [whole(bias.shape)]
        + [column] * 5
        + [pl.BlockSpec((1, len(tiles), 2 * TILE), lambda i, p: (i, 0, 0))],
        [
            (pl.BlockSpec((3, rows, span), lambda i, p: (0, 0, i)), shape_of((3, rows, width))),
            (pl.BlockSpec((2, span), lambda i, p: (0, i)), shape_of((2, width), f32)),
        ],
        grid=(pairs,),
        scratch=[pltpu.VMEM((rows, span), f32)] * 2,
    )


PARTS = 4


def middle_kernel(weights, place_ref, counts_ref, tok_ref, o_ref, cot_out_ref, cot_align_ref, vec_ref, *refs):
    arrays, refs = split_refs(refs, weights)
    out_ref, aligned_ref, z_ref, e_ref, h_ref, g_ref, du_ref, dm_ref, dx_ref, da_ref, do_ref = refs[:11]
    sums_ref, w_proj_ref, w_up_ref, w_down_ref, w_head_ref, sems = refs[11:]
    step = pl.program_id(0)
    size, width = tok_ref.shape
    hidden_units = w_up_ref.shape[-1]
    part = hidden_units // PARTS
    seq = place_ref[SEQ]
    total = jnp.int32(0)
    for slot in range(counts_ref.shape[1]):
        total = total + counts_ref[seq, slot]
    places = lax.broadcasted_iota(jnp.int32, (size, 1), 0) + step * size
    valid = jnp.where(places < total, 1.0, 0.0).astype(f32)

    @pl.when(step == 0)
    def _():
        fetch_all(place_ref, weights, arrays, [w_proj_ref, w_up_ref, w_down_ref, w_head_ref], sems)
        sums_ref[...] = jnp.zeros_like(sums_ref)

    def add_sum(index, first, value):
        columns = slice(first, first + value.shape[1])
        sums_ref[index : index + 1, columns] += jnp.sum(value.astype(f32), axis=0, keepdims=True)

    x1 = tok_ref[...].astype(f32) + dot_nn(o_ref[...], matrix(w_proj_ref)) + row(vec_ref, B_PROJ, width)
    n2, inverse = normed(x1)
    gain = row(vec_ref, GAIN_TWO, width)
    h2 = (n2 * gain + row(vec_ref, SHIFT_TWO, width)).astype(bf16)
    h_ref[...] = h2

    e_al = (cot_align_ref[...].astype(f32) * valid).astype(bf16)
    e_ref[...] = e_al
    add_sum(B_HEAD, 0, e_al)
    dx2 = cot_out_ref[...].astype(f32) * valid + dot_nt(e_al, matrix(w_head_ref))
    dm = dx2.astype(bf16)
    dm_ref[...] = dm
    add_sum(B_DOWN, 0, dm)

    x2 = x1 + row(vec_ref, B_DOWN, width)
    dh2 = jnp.zeros((size, width), f32)
    for index in range(PARTS):
        span = slice(index * part, (index + 1) * part)
        u = dot_nn(h2, matrix(w_up_ref, span)) + vec_ref[B_UP : B_UP + 1, span].astype(f32)
        cdf = 0.5 * (1.0 + lax.erf(u * (1.0 / math.sqrt(2.0))))
        pdf = jnp.exp(-0.5 * u * u) * (1.0 / math.sqrt(2.0 * math.pi))
        g = (u * cdf).astype(bf16)
        g_ref[:, span] = g
        x2 = x2 + dot_nn(g, w_down_ref[span, :])
        du = (dot_nt(dm, w_down_ref[span, :]) * (cdf + u * pdf)).astype(bf16)
        du_ref[:, span] = du
        add_sum(B_UP, index * part, du)
        dh2 = dh2 + dot_nt(du, matrix(w_up_ref, span))
    out_ref[...] = (x2 * valid).astype(bf16)
    z = x2.astype(bf16)
    z_ref[...] = z
    aligned_ref[...] = ((dot_nn(z, matrix(w_head_ref)) + row(vec_ref, B_HEAD, cot_align_ref.shape[1])) * valid).astype(bf16)

    add_sum(GAIN_TWO, 0, dh2 * n2)
    add_sum(SHIFT_TWO, 0, dh2)
    t = dh2 * gain
    inner = t - jnp.mean(t, axis=-1, keepdims=True) - n2 * jnp.mean(t * n2, axis=-1, keepdims=True)
    dx1 = dx2 + inverse * inner
    dx_ref[...] = dx1
    da = dx1.astype(bf16)
    da_ref[...] = da
    add_sum(B_PROJ, 0, da)
    do_ref[...] = dot_nt(da, matrix(w_proj_ref)).astype(bf16)


def middle(order, counts, tokens, o, cot_out, cot_align, weights, vectors):
    rows, width = tokens.shape
    hidden, align = weights[1].shape[1], weights[3].shape[1]
    size = row_tile(rows, 320)

    def by_row(columns):
        return pl.BlockSpec((size, columns), lambda i, p: (i, 0))

    def row_shape(columns, dtype=bf16):
        return shape_of((rows, columns), dtype)

    outs = [
        (by_row(width), row_shape(width)),
        (by_row(align), row_shape(align)),
        (by_row(width), row_shape(width)),
        (by_row(align), row_shape(align)),
        (by_row(width), row_shape(width)),
        (by_row(hidden), row_shape(hidden)),
        (by_row(hidden), row_shape(hidden)),
        (by_row(width), row_shape(width)),
        (by_row(width), row_shape(width, f32)),
        (by_row(width), row_shape(width)),
        (by_row(width), row_shape(width)),
    ]
    outs.append((out_whole(vectors.shape), shape_of(vectors.shape, f32)))
    arrays = [array for weight in weights for array in weight.arrays]
    return order(
        functools.partial(middle_kernel, weights),
        "middle",
        [counts, tokens, o, cot_out, cot_align, vectors, *arrays],
        [SMEM, by_row(width), by_row(width), by_row(width), by_row(align), whole(vectors.shape)]
        + [ANY] * len(arrays),
        outs,
        grid=(rows // size,),
        vmem=54,
        scratch=weight_scratch(weights),
    )


def outer_kernel(place_ref, l_ref, r_ref, out_ref):
    out_ref[...] = dot_tn(l_ref[...], r_ref[...]).astype(out_ref.dtype)


def outer(order, left, right, rows_out, columns_out, name):
    rows, m = left.shape
    n = right.shape[1]
    tm, tn = min(rows_out, m), min(columns_out, n)
    return order(
        outer_kernel,
        name,
        [left, right],
        [pl.BlockSpec((rows, tm), lambda i, j, p: (0, i)), pl.BlockSpec((rows, tn), lambda i, j, p: (0, j))],
        [(pl.BlockSpec((tm, tn), lambda i, j, p: (i, j)), shape_of((m, n)))],
        grid=(m // tm, n // tn),
        vmem=56,
    )[0]


BAND = 96
HALF = BAND // 2
FEW = 16


def outer_split_kernel(place_ref, l_ref, r_ref, keep_ref, send_ref, l_scratch):
    levels, _, _, columns = keep_ref.shape

    @pl.when(pl.program_id(0) == 0)
    def _():
        l_scratch[...] = l_ref[...].T

    right = r_ref[0] if len(r_ref.shape) == 3 else r_ref[...]
    total = dot_nn(l_scratch[...], right).astype(bf16)
    shape = (2, HALF, columns)
    first = place_ref[CORE] == 0
    for z in range(levels):
        low = total[2 * z * BAND : (2 * z + 1) * BAND].reshape(shape)
        high = total[(2 * z + 1) * BAND : (2 * z + 2) * BAND].reshape(shape)
        level = place_ref[Z] ^ z
        keep_ref[level] = jnp.where(first, low, high)
        send_ref[level] = jnp.where(first, high, low)


def outer_split(order, left, right, levels, columns_out, total, at, into, name, after=()):
    rows, m = left.shape
    n = right.shape[-1] * (right.shape[0] if right.ndim == 3 else 1)
    if right.ndim == 3:
        columns_out = right.shape[-1]
        r_spec = pl.BlockSpec((1, rows, columns_out), lambda j, p: (j, 0, 0))
    else:
        r_spec = pl.BlockSpec((rows, columns_out), lambda j, p: (0, j))
    out = shape_of((levels, 2, HALF, total))
    out_spec = pl.BlockSpec((levels, 2, HALF, columns_out), lambda j, p: (0, 0, 0, at // columns_out + j))
    return order(
        outer_split_kernel,
        name,
        [left, right],
        [whole(left.shape), r_spec],
        [(out_spec, out)] * 2,
        grid=(n // columns_out,),
        scratch=[pltpu.VMEM((m, rows), bf16)],
        into=into,
        vmem=56,
        after=after,
    )


def split_kernel(sets, place_ref, *refs):
    pairs, outs = refs[: 2 * len(sets)], refs[2 * len(sets) :]
    for own in range(4):

        @pl.when(place_ref[Y] * 2 + place_ref[X] == own)
        def _():
            for quarter, out_ref in enumerate(outs):
                y, x = divmod(own ^ quarter, 2)
                at = 0
                for number, members in enumerate(sets):
                    keep_ref, got_ref = pairs[2 * number : 2 * number + 2]
                    first = 0
                    for columns in members:
                        half = columns // 2
                        part = slice(first + x * half, first + (x + 1) * half)
                        out_ref[:, :, at : at + half] = keep_ref[:, y, :, part] + got_ref[:, y, :, part]
                        at, first = at + half, first + columns


def split(order, sets, pairs, name):
    levels = pairs[0][0].shape[0]
    total = sum(keep.shape[3] for keep, _ in pairs)
    shape = (levels, HALF, total // 2)
    return order(
        functools.partial(split_kernel, sets),
        name,
        [array for pair in pairs for array in pair],
        [VMEM] * (2 * len(pairs)),
        [(VMEM, shape_of(shape))] * 4,
    )


def levels_kernel(levels, place_ref, *refs):
    ins, lines, outs = refs[:4], refs[4:-levels], refs[-levels:]
    columns = ins[0].shape[2]
    for level, out_ref in enumerate(outs):
        total = ins[0][level].astype(f32)
        for ref in ins[1:]:
            total = total + ref[level].astype(f32)
        out_ref[:, :columns] = total.astype(bf16)
        if lines:
            out_ref[0:FEW, columns:] = lines[0][level] + lines[1][level]
            out_ref[FEW:, columns:] = jnp.zeros((HALF - FEW, TILE), bf16)


def by_level(order, quarters, lines, name):
    levels, height, columns = quarters[0].shape
    columns += TILE if lines else 0
    return order(
        functools.partial(levels_kernel, levels),
        name,
        list(quarters) + list(lines),
        [VMEM] * (4 + len(lines)),
        [(VMEM, shape_of((height, columns)))] * levels,
    )


def add_kernel(parts, place_ref, *refs):
    ins, beside, out_ref = refs[:parts], refs[parts:-1], refs[-1]
    columns = ins[0].shape[1]
    total = ins[0][...].astype(f32)
    for ref in ins[1:]:
        total = total + ref[...].astype(f32)
    out_ref[:, :columns] = total.astype(bf16)
    for ref in beside:
        width = ref.shape[1]
        for band in range(ref.shape[0] // HALF):
            out_ref[:, columns : columns + width] = ref[band * HALF : (band + 1) * HALF, :]
            columns += width


def add_up(order, arrays, beside, name):
    height, columns = arrays[0].shape
    columns += sum(b.size // height for b in beside)
    return order(
        functools.partial(add_kernel, len(arrays)),
        name,
        list(arrays) + list(beside),
        [VMEM] * (len(arrays) + len(beside)),
        [(VMEM, shape_of((height, columns)))],
    )[0]


def join_kernel(members, lengths, beside, place_ref, *refs):
    quarters, outs = refs[:4], refs[4:]
    for x in (0, 1):

        @pl.when(place_ref[X] == x)
        def _():
            for quarter, ref in enumerate(quarters):
                y = place_ref[Y] ^ (quarter // 2)
                across = x ^ (quarter % 2)
                at = 0
                for number, columns in enumerate(members):
                    half = columns // 2
                    outs[number][y, :, across * half : (across + 1) * half] = ref[:, at : at + half].astype(f32)
                    at += half

    at = sum(members) // 2
    if beside:
        out_ref = outs[len(members)]
        width = out_ref.shape[3]
        for quarter, ref in enumerate(quarters):
            owner = (place_ref[Y] * 2 + place_ref[X]) ^ quarter
            for band in range(out_ref.shape[1]):
                columns = slice(at + band * width, at + (band + 1) * width)
                out_ref[owner, band] = ref[:, columns].astype(f32)

    if lengths:
        lines = quarters[0][0:FEW, at : at + TILE].astype(f32)
        for ref in quarters[1:]:
            lines = lines + ref[0:FEW, at : at + TILE].astype(f32)
        line = 0
        for part, out_ref in zip(lengths, outs[len(members) :]):
            rows = []
            for length in part:
                pieces = []
                for i in range(lines_of(length)):
                    pieces.append(lines[line + i : line + i + 1, : min(TILE, length - i * TILE)])
                rows.append(jnp.concatenate(pieces, axis=1) if len(pieces) > 1 else pieces[0])
                line += lines_of(length)
            if len(rows) == 1:
                out_ref[...] = rows[0][0]
            else:
                for i, value in enumerate(rows):
                    out_ref[i : i + 1, :] = value


def join(order, quarters, members, lengths, beside, name):
    outs = [(VMEM, shape_of((2, HALF, columns), f32)) for columns in members]
    if beside:
        rows, columns = beside
        outs.append((VMEM, shape_of((4, rows // (4 * HALF), HALF, columns), f32)))
    for part in lengths:
        outs.append((VMEM, shape_of((part[0],) if len(part) == 1 else (len(part), part[0]), f32)))
    results = order(
        functools.partial(join_kernel, members, lengths, beside),
        name,
        quarters,
        [VMEM] * 4,
        outs,
    )
    matrices = len(members) + (1 if beside else 0)
    return [r.reshape(-1, r.shape[-1]) for r in results[:matrices]] + list(results[matrices:])


class Reduction:
    def __init__(self, order, name):
        self.order, self.name = order, name
        self.sets, self.pairs = [], []

    def add(self, keep, send, members):
        self.sets.append(members)
        self.pairs.append((keep, swap(send, self.name + "_core", fsdp=1)))

    def split(self):
        quarters = split(self.order, self.sets, self.pairs, self.name + "_split")
        self.quarters = [quarters[0]] + [swap(quarters[j], self.name + "_plane", dp=j) for j in (1, 2, 3)]

    def levels(self, lines=()):
        parts = by_level(self.order, self.quarters, lines, self.name + "_levels")
        self.parts = [parts[0]]
        self.parts += [swap(part, self.name + "_column", fsdp=2 * level) for level, part in enumerate(parts) if level]

    def total(self, beside=()):
        near = add_up(self.order, self.parts, beside, self.name + "_total")
        self.near = [near] + [swap(near, self.name + "_back", dp=j) for j in (1, 2, 3)]

    def join(self, lengths=(), beside=()):
        members = [columns for members in self.sets for columns in members]
        return join(self.order, self.near, members, lengths, beside, self.name + "_join")


def lines_of(length):
    return -(-length // TILE)


def pack_kernel(lengths, place_ref, sums_ref, first_ref, qv_ref, keep_ref, send_ref):
    levels = keep_ref.shape[0]
    first = place_ref[CORE] == 0
    late = {GAIN_ONE: (first_ref, 0), SHIFT_ONE: (first_ref, 1), B_Q: (qv_ref, 0), B_V: (qv_ref, 1)}
    values = []
    for index, length in enumerate(lengths):
        ref, line = late.get(index, (sums_ref, index))
        values.append(ref[line : line + 1, : 2 * levels * length])

    def lines(shard):
        rows = []
        for value, length in zip(values, lengths):
            part = value[:, shard * length : (shard + 1) * length]
            if length % TILE:
                part = jnp.concatenate([part, jnp.zeros((1, -length % TILE), f32)], axis=1)
            rows += [part[:, at : at + TILE] for at in range(0, part.shape[1], TILE)]
        return jnp.concatenate(rows + [jnp.zeros((FEW - len(rows), TILE), f32)], axis=0)

    for z in range(levels):
        level = place_ref[Z] ^ z
        low, high = lines(2 * z), lines(2 * z + 1)
        keep_ref[level] = jnp.where(first, low, high).astype(bf16)
        send_ref[level] = jnp.where(first, high, low).astype(bf16)


def pack_vectors(order, sums, lengths, levels):
    shape = (levels, FEW, TILE)
    return order(
        functools.partial(pack_kernel, lengths),
        "pack_vectors",
        sums,
        [VMEM] * len(sums),
        [(VMEM, shape_of(shape))] * 2,
    )


def unpack_kernel(lengths, place_ref, own_ref, other_ref, out_ref):
    levels = own_ref.shape[0]
    first = place_ref[CORE] == 0
    shards = []
    for z in range(levels):
        own = own_ref[z].astype(f32)
        other = other_ref[z].astype(f32)
        shards += [jnp.where(first, own, other), jnp.where(first, other, own)]
    at = 0
    for index, length in enumerate(lengths):
        pieces = []
        for shard in shards:
            for line in range(lines_of(length)):
                pieces.append(shard[at + line : at + line + 1, : min(TILE, length - line * TILE)])
        out_ref[index : index + 1, : length * len(shards)] = jnp.concatenate(pieces, axis=1).astype(bf16)
        at += lines_of(length)


def unpack_vectors(order, own, other, lengths):
    levels = own.shape[0]
    return order(
        functools.partial(unpack_kernel, lengths),
        "unpack_vectors",
        [own, other],
        [VMEM] * 2,
        [(VMEM, shape_of((ROWS, 2 * levels * max(lengths))))],
    )[0]


def start_kernel(lengths, groups, place_ref, *refs):
    count = sum(len(g) for g in groups)
    vectors = refs[: len(refs) - count - len(groups)]
    shards, outs = refs[len(vectors) : len(vectors) + count], refs[len(vectors) + count :]
    at = 0
    for group, out_ref in zip(groups, outs):
        column = 0
        for _ in group:
            half = shards[at].shape[1]
            out_ref[:, column : column + half] = shards[at][...]
            column += half
            at += 1
    values = []
    for ref in vectors:
        value = ref[...].astype(f32)
        values += [value[i] for i in range(value.shape[0])] if value.ndim == 2 else [value]
    lines = []
    for value, length in zip(values, lengths):
        if length % TILE:
            value = jnp.concatenate([value, jnp.zeros((-length % TILE,), f32)])
        lines += [value[at : at + TILE].reshape(1, TILE) for at in range(0, value.shape[0], TILE)]
    lines.append(jnp.zeros((HALF - len(lines), TILE), f32))
    outs[0][:, outs[0].shape[1] - TILE :] = jnp.concatenate(lines, axis=0).astype(bf16)


def start_gather(order, vectors, lengths, groups):
    shards = [w for group in groups for w in group]
    outs = []
    for number, group in enumerate(groups):
        shape = (HALF, sum(w.shape[1] // 2 for w in group) + (TILE if number == 0 else 0))
        outs.append((out_whole(shape), shape_of(shape)))
    return order(
        functools.partial(start_kernel, lengths, groups),
        "quarters",
        list(vectors) + shards,
        [whole(v.shape) for v in vectors]
        + [pl.BlockSpec((w.shape[0] // 2, w.shape[1] // 2), lambda i, p: (p[Y], p[X])) for w in shards],
        outs,
        grid=(1,),
        vmem=56,
    )


def near_kernel(levels, place_ref, *refs):
    got, out_ref, lines = refs[:levels], refs[levels], refs[levels + 1 :]
    columns = out_ref.shape[2]
    for level, ref in enumerate(got):
        if level:
            out_ref[level - 1] = ref[:, :columns]
        for lines_ref in lines:
            lines_ref[place_ref[Z] ^ level] = ref[0:FEW, columns:]


def near_levels(order, got, lines, name):
    levels, (height, columns) = len(got), got[0].shape
    columns -= TILE if lines else 0
    outs = [(VMEM, shape_of((levels - 1, height, columns)))]
    if lines:
        outs.append((VMEM, shape_of((levels, FEW, TILE))))
    return order(
        functools.partial(near_kernel, levels),
        name,
        got,
        [VMEM] * levels,
        outs,
    )


def assemble_kernel(halves, place_ref, *refs):
    shards, refs = refs[: len(halves)], refs[len(halves) :]
    quarters, out_ref = refs[:4], refs[4]
    z = place_ref[Z]
    column = 0
    for shard in shards:
        columns = shard.shape[1]
        for y in (0, 1):
            out_ref[z, y, :, column : column + columns] = shard[y * HALF : (y + 1) * HALF, :]
        column += columns
    for x in (0, 1):

        @pl.when(place_ref[X] == x)
        def _():
            for quarter, ref in enumerate(quarters):
                y = place_ref[Y] ^ (quarter // 2)
                across = x ^ (quarter % 2)
                for level in range(ref.shape[0]):
                    source, column = 0, 0
                    for half in halves:
                        target = column + across * half
                        out_ref[z ^ (level + 1), y, :, target : target + half] = ref[level, :, source : source + half]
                        source, column = source + half, column + 2 * half


def assemble(order, shards, quarters, name):
    levels = quarters[0].shape[0] + 1
    halves = [shard.shape[1] // 2 for shard in shards]
    return order(
        functools.partial(assemble_kernel, halves),
        name,
        list(shards) + list(quarters),
        [VMEM] * (len(shards) + 4),
        [(VMEM, shape_of((levels, 2, HALF, 2 * sum(halves))))],
    )[0].reshape(levels, BAND, -1)


def across_plane(near, name):
    return [near] + [swap(near, name + "_plane", dp=j) for j in (1, 2, 3)]


def first_back_kernel(weight, place_ref, tok_ref, dx_ref, d_ref, vec_ref, *refs):
    arrays, (out_ref, sums_ref, w_ref, sems) = split_refs(refs, [weight])
    width = tok_ref.shape[1]

    @pl.when(pl.program_id(0) == 0)
    def _():
        fetch_all(place_ref, [weight], arrays, [w_ref], sems)
        sums_ref[...] = jnp.zeros_like(sums_ref)

    dh = dot_nt(d_ref[0], matrix(w_ref, slice(0, width)))
    dh = dh + dot_nt(d_ref[1], matrix(w_ref, slice(width, 2 * width)))
    dh = dh + dot_nt(d_ref[2], matrix(w_ref, slice(2 * width, 3 * width)))
    n1, inverse = normed(tok_ref[...].astype(f32))
    sums_ref[0:1, :] += jnp.sum(dh * n1, axis=0, keepdims=True)
    sums_ref[1:2, :] += jnp.sum(dh, axis=0, keepdims=True)
    t = dh * row(vec_ref, GAIN_ONE, width)
    inner = t - jnp.mean(t, axis=-1, keepdims=True) - n1 * jnp.mean(t * n1, axis=-1, keepdims=True)
    out_ref[...] = (dx_ref[...] + inverse * inner).astype(bf16)


def first_back(order, tokens, dx1, dqkv, weight, vectors, after):
    rows, width = tokens.shape
    size = row_tile(rows, 320)
    rowwise = pl.BlockSpec((size, width), lambda i, p: (i, 0))
    return order(
        functools.partial(first_back_kernel, weight),
        "first_back",
        [tokens, dx1, dqkv, vectors] + weight.arrays,
        [rowwise, rowwise, pl.BlockSpec((3, size, width), lambda i, p: (0, i, 0)), whole(vectors.shape)]
        + [ANY] * len(weight.arrays),
        [(rowwise, shape_of((rows, width))), (out_whole((2, width)), shape_of((2, width), f32))],
        grid=(rows // size,),
        after=after,
        scratch=weight_scratch([weight]),
        vmem=56,
    )


def local(
    tokens,
    ln1_gain,
    ln1_bias,
    w_qkv,
    qv_bias,
    w_proj,
    proj_bias,
    ln2_gain,
    ln2_bias,
    w_up,
    up_bias,
    w_down,
    down_bias,
    w_head,
    head_bias,
    clip_counts,
    cot_out,
    cot_align,
):
    rows, width = tokens.shape
    shards = lax.axis_size("fsdp")
    levels = shards // 2
    order = Order(position())
    own_vectors = (ln1_gain, ln1_bias, qv_bias, proj_bias, ln2_gain, ln2_bias, up_bias, down_bias, head_bias)
    parts = [[v.shape[-1]] * (v.size // v.shape[-1]) for v in own_vectors]
    lengths = [length for part in parts for length in part]
    paired = (
        lax.axis_size("dp") == 4
        and shards % 2 == 0
        and levels in (2, 4, 8)
        and w_qkv.shape[0] == BAND
        and sum(lines_of(n) for n in lengths) <= FEW
    )

    def gather(value):
        return lax.all_gather(value, "fsdp", axis=0, tiled=True)

    def scatter(value):
        return lax.psum_scatter(value, "fsdp", scatter_dimension=0, tiled=True)

    if paired:
        wide = [w_up, w_head, w_proj]
        p_qkv, p_wide = start_gather(order, own_vectors, lengths, [[w_qkv], wide])
        got = [p_qkv] + [swap(p_qkv, "qkv_column", fsdp=2 * level) for level in range(1, levels)]
        got_wide = [swap(p_wide, "wide_column", fsdp=2 * level) for level in range(2, levels)]
        bias = make_masks(order, clip_counts, rows)
        near, lines = near_levels(order, got, True, "qkv_near")
        quarters = across_plane(near, "qkv")
        other_lines = swap(lines, "vectors_core", fsdp=1)
        own = assemble(order, [w_qkv], quarters, "qkv_assemble")
        full_qkv = Weight([own, swap(own, "qkv_core", fsdp=1)], 0, (width, w_qkv.shape[1]))
        later, own = lax.optimization_barrier((p_wide, own))
        got_wide = [p_wide, swap(later, "wide_column", fsdp=2)] + got_wide
        vectors = unpack_vectors(order, lines, other_lines, lengths)
        (near,) = near_levels(order, got_wide, False, "wide_near")
        quarters = across_plane(near, "wide")
        later, near = lax.optimization_barrier((w_down, near))
        full_down = gather(later)
    else:
        pieces = [piece for v in own_vectors for piece in ([v[0], v[1]] if v.ndim == 2 else [v])]
        joined = gather(jnp.concatenate(pieces)[None])
        lines, at = [], 0
        for length in lengths:
            line = joined[:, at : at + length].reshape(1, -1)
            lines.append(jnp.pad(line, ((0, 0), (0, shards * max(lengths) - line.shape[1]))))
            at += length
        vectors = jnp.pad(jnp.concatenate(lines), ((0, ROWS - len(lines)), (0, 0)))
        full_qkv, full_proj, full_up, full_head = (
            Weight([full], 0, full.shape) for full in (gather(w) for w in (w_qkv, w_proj, w_up, w_head))
        )
        full_down = gather(w_down)
        bias = make_masks(order, clip_counts, rows)
    full_down = Weight([full_down], 0, full_down.shape)
    h1, q, k, v = project_qkv(order, tokens, vectors, full_qkv)
    o, lse = attend(order, bias, q, k, v)
    if paired:
        own = assemble(order, wide, quarters, "wide_assemble")
        both_cores = [own, swap(own, "wide_core", fsdp=1)]
        at = [0, w_up.shape[1], w_up.shape[1] + w_head.shape[1]]
        full_up, full_head, full_proj = (
            Weight(both_cores, column, (width, w.shape[1])) for column, w in zip(at, wide)
        )
    block_out, aligned, z, e_al, h2, g, du, dm, dx1, da, do, sums = middle(
        order,
        clip_counts,
        tokens,
        o,
        cot_out,
        cot_align,
        (full_proj, full_up, full_down, full_head),
        vectors,
    )
    d_down = scatter(outer(order, g, dm, 512, 768, "grad_down"))
    if paired:
        r_wide = Reduction(order, "wide")
        pair = outer_split(order, h2, du, levels, 768, w_up.shape[1], 0, (), "grad_up")
        r_wide.add(*pair, [w_up.shape[1]])
        members = [w_head.shape[1], w_proj.shape[1]]
        pair = outer_split(order, z, e_al, levels, 512, sum(members), 0, (), "grad_head")
        pair = outer_split(order, o, da, levels, 256, sum(members), members[0], pair, "grad_proj")
        r_wide.add(*pair, members)
        r_wide.split()
    dqkv, s_qv = attend_back(order, bias, q, k, v, o, do, lse)
    if paired:
        r_qkv = Reduction(order, "qkv")
        n = w_qkv.shape[1]
        r_qkv.add(*outer_split(order, h1, dqkv, levels, width, n, 0, (), "grad_qkv"), [n])
    grad_tokens, s_first = first_back(order, tokens, dx1, dqkv, full_qkv, vectors, [d_down])
    if paired:
        d_down = lax.psum_scatter(d_down, "dp", scatter_dimension=0, tiled=True)
        r_qkv.split()
        lines, send = pack_vectors(order, [sums, s_first, s_qv], lengths, levels)
        lines = [lines, swap(send, "vectors_core", fsdp=1)]
        r_wide.levels()
        r_qkv.levels(lines)
        r_wide.total([d_down])
        r_qkv.total()
        d_up, d_head, d_proj, d_down = r_wide.join(beside=w_down.shape)
        d_qkv, *mine = r_qkv.join(lengths=parts)
    else:

        def reduce(value):
            return lax.psum(scatter(value), "dp").astype(f32)

        d_down = lax.psum(d_down, "dp").astype(f32)
        d_up = reduce(outer(order, h2, du, 768, 512, "grad_up"))
        d_head = reduce(outer(order, z, e_al, 768, 512, "grad_head"))
        d_proj = reduce(outer(order, o, da, 768, 384, "grad_proj"))
        d_qkv = reduce(outer(order, h1, jnp.concatenate([dqkv[0], dqkv[1], dqkv[2]], axis=1), 768, 768, "grad_qkv"))
        late = {GAIN_ONE: s_first[0], SHIFT_ONE: s_first[1], B_Q: s_qv[0], B_V: s_qv[1]}
        lines = [late.get(i, sums[i])[: shards * n].reshape(shards, n) for i, n in enumerate(lengths)]
        joined = jnp.concatenate(lines, axis=1)
        joined = lax.psum(lax.psum_scatter(joined, "fsdp", scatter_dimension=0, tiled=True), "dp")[0]
        mine, at = [], 0
        for part in parts:
            size = sum(part)
            mine.append(joined[at : at + size].reshape((part[0],) if len(part) == 1 else (len(part), -1)))
            at += size
    d_gain_one, d_shift_one, d_qv, d_b_proj, d_gain_two, d_shift_two, d_b_up, d_b_down, d_b_head = mine
    return (
        block_out,
        aligned,
        grad_tokens,
        d_gain_one,
        d_shift_one,
        d_qkv,
        d_qv,
        d_proj,
        d_b_proj,
        d_gain_two,
        d_shift_two,
        d_up,
        d_b_up,
        d_down,
        d_b_down,
        d_head,
        d_b_head,
    )


def solution(mesh):
    rows = P(("dp", "fsdp"), None)
    matrix, vector, pair = P("fsdp", None), P("fsdp"), P(None, "fsdp")
    return jax.shard_map(
        local,
        mesh=mesh,
        in_specs=(
            rows,
            vector,
            vector,
            matrix,
            pair,
            matrix,
            vector,
            vector,
            vector,
            matrix,
            vector,
            matrix,
            vector,
            matrix,
            vector,
            P(),
            rows,
            rows,
        ),
        out_specs=(
            rows,
            rows,
            rows,
            vector,
            vector,
            matrix,
            pair,
            matrix,
            vector,
            vector,
            vector,
            matrix,
            vector,
            matrix,
            vector,
            matrix,
            vector,
        ),
        check_vma=False,
    )
```

```python
import functools
import math

import jax
import jax.numpy as jnp
from jax import lax
from jax.experimental import pallas as pl
from jax.experimental.pallas import tpu as pltpu
from jax.sharding import PartitionSpec as P

HEADS = 12
LONGEST = 157
EPSILON = 1e-06
MASKED = -1e30
TILE = 128

f32 = jnp.float32
bf16 = jnp.bfloat16


def dot_nn(left, right):
    return lax.dot_general(left, right, (((1,), (0,)), ((), ())), preferred_element_type=f32)


def dot_nt(left, right):
    return lax.dot_general(left, right, (((1,), (1,)), ((), ())), preferred_element_type=f32)


def dot_tn(left, right):
    return lax.dot_general(left, right, (((0,), (0,)), ((), ())), preferred_element_type=f32)


def attention_tiles(rows):
    tiles, offset = [], 0
    reach = LONGEST - 1
    for start in range(0, rows, TILE):
        size = min(TILE, rows - start)
        low = max(0, (start - reach) // 16 * 16)
        high = min(rows, -(-(start + size + reach) // 16) * 16)
        tiles.append((start, size, low, high - low, offset))
        offset += high - low
    return tiles, offset


def row_tile(rows, most):
    for size in range(most, 15, -16):
        if rows % size == 0:
            return size
    return rows


USUAL = 10
TIMES = {
    "attend_back": 60,
    "grad_down": 30,
    "pack_early": 30,
    "qkv_split": 1,
    "pack_late": 1,
    "wide_half_4": 1,
    "qkv_levels": 1,
    "wide_half_2": 1,
    "qkv_total": 1,
    "wide_total": 1,
}


def duration(name):
    return pl.CostEstimate(flops=TIMES.get(name, USUAL) * 10**9, bytes_accessed=1, transcendentals=0)


def whole(shape):
    return pl.BlockSpec(shape, lambda *_: (0,) * len(shape), pipeline_mode=pl.Buffered(1))


def out_whole(shape):
    return pl.BlockSpec(shape, lambda *_: (0,) * len(shape))


SMEM = pl.BlockSpec(memory_space=pltpu.SMEM)
VMEM = pl.BlockSpec(memory_space=pltpu.VMEM)
ANY = pl.BlockSpec(memory_space=pl.ANY)


def shape_of(shape, dtype=bf16):
    return jax.ShapeDtypeStruct(tuple(shape), dtype)


class Order:
    def __init__(self, place):
        self.place, self.last = place, None

    def __call__(self, kernel, name, arrays, in_specs, outs, grid=(), scratch=(), into=(), after=(), vmem=32):
        in_specs, arrays = list(in_specs), list(arrays)
        seen = 1 + len(arrays)
        aliases = {seen + i: i for i in range(len(into))}
        extra = (list(into) or ([] if self.last is None else [self.last])) + list(after)
        in_specs += [ANY] * len(extra)
        arrays += extra

        def body(*refs):
            kernel(*refs[:seen], *refs[seen + len(extra) :])

        result = pl.pallas_call(
            body,
            grid_spec=pltpu.PrefetchScalarGridSpec(
                num_scalar_prefetch=1,
                grid=grid,
                in_specs=in_specs,
                out_specs=tuple(spec for spec, _ in outs),
                scratch_shapes=list(scratch),
            ),
            out_shape=tuple(shape for _, shape in outs),
            cost_estimate=duration(name),
            input_output_aliases=aliases,
            compiler_params=pltpu.CompilerParams(vmem_limit_bytes=vmem << 20),
            name=name,
        )(self.place, *arrays)
        self.last = result[0]
        return result


Z, CORE, Y, X, SEQ = range(5)


def position():
    dp, fsdp = lax.axis_index("dp"), lax.axis_index("fsdp")
    seq = dp * lax.axis_size("fsdp") + fsdp
    return jnp.stack([fsdp // 2, fsdp % 2, dp // 2, dp % 2, seq]).astype(jnp.int32)


def swap(value, name, dp=0, fsdp=0):
    m, n = lax.axis_size("dp"), lax.axis_size("fsdp")
    pairs = [(i * n + j, (i ^ dp) * n + (j ^ fsdp)) for i in range(m) for j in range(n)]
    with jax.named_scope(f"{name}_{dp}_{fsdp}"):
        return lax.ppermute(value, ("dp", "fsdp"), pairs)


class Weight:
    def __init__(self, arrays, column, shape):
        self.arrays, self.column, self.shape = list(arrays), column, tuple(shape)
        if len(self.arrays) == 1:
            self.scratch = self.shape
        else:
            levels, rows, _ = arrays[0].shape
            self.scratch = (levels, 2, rows, shape[1])

    def copies(self, place, refs, weight, sems, first):
        columns = pl.ds(self.column, self.shape[1])
        if len(refs) == 1:
            return [pltpu.make_async_copy(refs[0], weight, sems.at[first])]
        return [
            pltpu.make_async_copy(ref.at[:, :, columns], weight.at[:, place[CORE] ^ i], sems.at[first + i])
            for i, ref in enumerate(refs)
        ]


def matrix(ref, columns=slice(None)):
    if len(ref.shape) == 2:
        return ref[:, columns]
    value = ref[:, :, :, columns]
    return value.reshape(-1, value.shape[-1])


def fetch_all(place, weights, arrays, scratch, sems):
    copies = []
    for weight, refs, target in zip(weights, arrays, scratch):
        copies += weight.copies(place, refs, target, sems, len(copies))
    for copy in copies:
        copy.start()
    for copy in copies:
        copy.wait()


def split_refs(refs, weights):
    groups, at = [], 0
    for weight in weights:
        groups.append(refs[at : at + len(weight.arrays)])
        at += len(weight.arrays)
    return groups, refs[at:]


def weight_scratch(weights):
    scratch = [pltpu.VMEM(w.scratch, bf16) for w in weights]
    return scratch + [pltpu.SemaphoreType.DMA((sum(len(w.arrays) for w in weights),))]


GAIN_ONE, SHIFT_ONE, B_Q, B_V, B_PROJ, GAIN_TWO, SHIFT_TWO, B_UP, B_DOWN, B_HEAD = range(10)
ROWS = 16


def row(vectors_ref, index, length):
    return vectors_ref[index : index + 1, :length].astype(f32)


def mask_kernel(tiles, place_ref, counts_ref, bias_ref, seg_ref):
    rows = seg_ref.shape[0]
    slots = counts_ref.shape[1]
    seq = place_ref[SEQ]
    ends, total = [], jnp.int32(0)
    for slot in range(slots):
        total = total + counts_ref[seq, slot]
        ends.append(total)
    places = lax.broadcasted_iota(jnp.int32, (rows, TILE), 0)
    seg = jnp.zeros((rows, TILE), jnp.int32)
    for end in ends:
        seg = seg + jnp.where(places >= end, 1, 0)
    seg_ref[...] = seg
    lanes = lax.broadcasted_iota(jnp.int32, (8, TILE), 1)
    for start, size, low, keys, offset in tiles:
        own = start + jnp.where(lanes >= size, lanes - size, lanes)
        seg_own = jnp.zeros((8, TILE), jnp.int32)
        for end in ends:
            seg_own = seg_own + jnp.where(own >= end, 1, 0)
        same = seg_ref[low : low + keys, :] == seg_own[0:1, :]
        bias_ref[offset : offset + keys, :] = jnp.where(same, 0.0, MASKED).astype(f32)


def make_masks(order, counts, rows):
    tiles, total = attention_tiles(rows)
    return order(
        functools.partial(mask_kernel, tiles),
        "masks",
        [counts],
        [SMEM],
        [(out_whole((total, TILE)), shape_of((total, TILE), f32))],
        scratch=[pltpu.VMEM((rows, TILE), jnp.int32)],
    )[0]


def normed(values):
    center = values - jnp.mean(values, axis=-1, keepdims=True)
    spread = jnp.mean(center * center, axis=-1, keepdims=True)
    inverse = lax.rsqrt(spread + EPSILON)
    return center * inverse, inverse


def qkv_kernel(scale, weight, place_ref, tok_ref, vec_ref, *refs):
    arrays, (h_ref, q_ref, k_ref, v_ref, w_ref, sems) = split_refs(refs, [weight])
    width = tok_ref.shape[1]

    @pl.when(pl.program_id(0) == 0)
    def _():
        fetch_all(place_ref, [weight], arrays, [w_ref], sems)

    n1, _ = normed(tok_ref[...].astype(f32))
    hidden = (n1 * row(vec_ref, GAIN_ONE, width) + row(vec_ref, SHIFT_ONE, width)).astype(bf16)
    h_ref[...] = hidden
    q = dot_nn(hidden, matrix(w_ref, slice(0, width)))
    q_ref[...] = ((q + row(vec_ref, B_Q, width)) * scale).astype(bf16)
    k = dot_nn(hidden, matrix(w_ref, slice(width, 2 * width)))
    k_ref[...] = k.astype(bf16)
    v = dot_nn(hidden, matrix(w_ref, slice(2 * width, 3 * width)))
    v_ref[...] = (v + row(vec_ref, B_V, width)).astype(bf16)


def project_qkv(order, tokens, vectors, weight):
    rows, width = tokens.shape
    scale = (width // HEADS) ** (-0.5)
    size = row_tile(rows, 320)
    rowwise = pl.BlockSpec((size, width), lambda i, p: (i, 0))
    return order(
        functools.partial(qkv_kernel, scale, weight),
        "norm_qkv",
        [tokens, vectors] + weight.arrays,
        [rowwise, whole(vectors.shape)] + [ANY] * len(weight.arrays),
        [(rowwise, shape_of((rows, width)))] * 4,
        grid=(rows // size,),
        scratch=weight_scratch([weight]),
    )


def stack_heads(pair, size):
    lanes = lax.broadcasted_iota(jnp.int32, pair.shape, 1)
    half = pair.shape[1] // 2
    zero = jnp.zeros_like(pair)
    first = jnp.where(lanes < half, pair, zero)
    second = jnp.where(lanes < half, zero, pair)
    return jnp.concatenate([first, second], axis=0)


def both(bias, size):
    return bias if size < TILE else jnp.concatenate([bias, bias], axis=1)


def unstack(columns, size, half):
    return jnp.concatenate([columns[:half, :size], columns[half:, size:]], axis=0).T


def attend_kernel(tiles, place_ref, bias_ref, q_ref, k_ref, v_ref, o_ref, lse_ref):
    half = q_ref.shape[1] // 2
    scores = []
    for start, size, low, keys, offset in tiles:
        stacked = stack_heads(q_ref[start : start + size, :], size)
        value = dot_nt(k_ref[low : low + keys, :], stacked)
        scores.append(value + both(bias_ref[offset : offset + keys, :], size))
    parts = []
    for value in scores:
        top = jnp.max(value, axis=0, keepdims=True)
        weights = jnp.exp(value - top)
        parts.append((weights.astype(bf16), top, jnp.sum(weights, axis=0, keepdims=True)))
    for index, (start, size, low, keys, _) in enumerate(tiles):
        weights, top, total = parts[index]
        columns = dot_tn(v_ref[low : low + keys, :], weights) * (1.0 / total)
        o_ref[start : start + size, :] = unstack(columns, size, half).astype(bf16)
        lse_ref[0, index : index + 1, : 2 * size] = top + jnp.log(total)


def attend(order, bias, q, k, v):
    rows, width = q.shape
    tiles, total = attention_tiles(rows)
    span = 2 * (width // HEADS)
    pairs = HEADS // 2
    column = pl.BlockSpec((rows, span), lambda i, p: (0, i))
    return order(
        functools.partial(attend_kernel, tiles),
        "attend",
        [bias, q, k, v],
        [whole(bias.shape), column, column, column],
        [
            (column, shape_of((rows, width))),
            (
                pl.BlockSpec((1, len(tiles), 2 * TILE), lambda i, p: (i, 0, 0)),
                shape_of((pairs, len(tiles), 2 * TILE), f32),
            ),
        ],
        grid=(pairs,),
    )


def attend_back_kernel(
    tiles, scale, place_ref, bias_ref, q_ref, k_ref, v_ref, o_ref, do_ref, lse_ref, d_ref, dqv_ref, dk_sum, dv_sum
):
    half = q_ref.shape[1] // 2
    dk_sum[...] = jnp.zeros_like(dk_sum)
    dv_sum[...] = jnp.zeros_like(dv_sum)
    dq_total = jnp.zeros((1, 2 * half), f32)
    for pair in range(0, len(tiles), 2):
        group = list(enumerate(tiles))[pair : pair + 2]
        held = []
        for index, (start, size, low, keys, offset) in group:
            window, rows = slice(low, low + keys), slice(start, start + size)
            q2 = stack_heads(q_ref[rows, :], size)
            grads = do_ref[rows, :]
            do2 = stack_heads(grads, size)
            scores = dot_nt(k_ref[window, :], q2) + both(bias_ref[offset : offset + keys, :], size)
            dprobs = dot_nt(v_ref[window, :], do2)
            meet = (grads.astype(f32) * o_ref[rows, :].astype(f32)).T
            delta = jnp.concatenate(
                [
                    jnp.sum(meet[:half, :], axis=0, keepdims=True),
                    jnp.sum(meet[half:, :], axis=0, keepdims=True),
                ],
                axis=1,
            )
            held.append((q2, do2, scores, dprobs, delta))
        lows = []
        for (index, (start, size, *_)), (q2, do2, scores, dprobs, delta) in zip(group, held):
            probs = jnp.exp(scores - lse_ref[0, index : index + 1, : 2 * size])
            lows.append((probs.astype(bf16), (probs * (dprobs - delta)).astype(bf16)))
        for (index, (start, size, low, keys, _)), (q2, do2, *_), (probs, dscores) in zip(group, held, lows):
            window, rows = slice(low, low + keys), slice(start, start + size)
            dv_sum[window, :] += dot_nn(probs, do2)
            dk_sum[window, :] += dot_nn(dscores, q2)
            columns = dot_tn(k_ref[window, :], dscores)
            dq = unstack(columns, size, half).astype(bf16) * bf16(scale)
            d_ref[0, rows, :] = dq
            dq_total = dq_total + jnp.sum(dq.astype(f32), axis=0, keepdims=True)
    d_ref[1, :, :] = dk_sum[...].astype(bf16)
    dv = dv_sum[...].astype(bf16)
    d_ref[2, :, :] = dv
    dqv_ref[0:1, :] = dq_total
    dqv_ref[1:2, :] = jnp.sum(dv.astype(f32), axis=0, keepdims=True)


def attend_back(order, bias, q, k, v, o, do, lse):
    rows, width = q.shape
    tiles, total = attention_tiles(rows)
    span = 2 * (width // HEADS)
    pairs = HEADS // 2
    scale = (width // HEADS) ** (-0.5)
    column = pl.BlockSpec((rows, span), lambda i, p: (0, i))
    return order(
        functools.partial(attend_back_kernel, tiles, scale),
        "attend_back",
        [bias, q, k, v, o, do, lse],
        [whole(bias.shape)]
        + [column] * 5
        + [pl.BlockSpec((1, len(tiles), 2 * TILE), lambda i, p: (i, 0, 0))],
        [
            (pl.BlockSpec((3, rows, span), lambda i, p: (0, 0, i)), shape_of((3, rows, width))),
            (pl.BlockSpec((2, span), lambda i, p: (0, i)), shape_of((2, width), f32)),
        ],
        grid=(pairs,),
        scratch=[pltpu.VMEM((rows, span), f32)] * 2,
        vmem=56,
    )


PARTS = 4


def middle_kernel(weights, place_ref, counts_ref, tok_ref, o_ref, cot_out_ref, cot_align_ref, vec_ref, *refs):
    arrays, refs = split_refs(refs, weights)
    out_ref, aligned_ref, z_ref, e_ref, h_ref, g_ref, du_ref, dm_ref, da_ref, do_ref = refs[:10]
    sums_ref, w_proj_ref, w_up_ref, w_down_ref, w_head_ref, sems = refs[10:]
    step = pl.program_id(0)
    size, width = tok_ref.shape
    hidden_units = w_up_ref.shape[-1]
    part = hidden_units // PARTS
    seq = place_ref[SEQ]
    total = jnp.int32(0)
    for slot in range(counts_ref.shape[1]):
        total = total + counts_ref[seq, slot]
    places = lax.broadcasted_iota(jnp.int32, (size, 1), 0) + step * size
    valid = jnp.where(places < total, 1.0, 0.0).astype(f32)

    @pl.when(step == 0)
    def _():
        fetch_all(place_ref, weights, arrays, [w_proj_ref, w_up_ref, w_down_ref, w_head_ref], sems)
        sums_ref[...] = jnp.zeros_like(sums_ref)

    def add_sum(index, first, value):
        columns = slice(first, first + value.shape[1])
        sums_ref[index : index + 1, columns] += jnp.sum(value.astype(f32), axis=0, keepdims=True)

    x1 = tok_ref[...].astype(f32) + dot_nn(o_ref[...], matrix(w_proj_ref)) + row(vec_ref, B_PROJ, width)
    n2, inverse = normed(x1)
    gain = row(vec_ref, GAIN_TWO, width)
    h2 = (n2 * gain + row(vec_ref, SHIFT_TWO, width)).astype(bf16)
    h_ref[...] = h2

    e_al = (cot_align_ref[...].astype(f32) * valid).astype(bf16)
    e_ref[...] = e_al
    add_sum(B_HEAD, 0, e_al)
    dx2 = cot_out_ref[...].astype(f32) * valid + dot_nt(e_al, matrix(w_head_ref))
    dm = dx2.astype(bf16)
    dm_ref[...] = dm
    add_sum(B_DOWN, 0, dm)

    x2 = x1 + row(vec_ref, B_DOWN, width)
    dh2 = jnp.zeros((size, width), f32)
    for index in range(PARTS):
        span = slice(index * part, (index + 1) * part)
        u = dot_nn(h2, matrix(w_up_ref, span)) + vec_ref[B_UP : B_UP + 1, span].astype(f32)
        cdf = 0.5 * (1.0 + lax.erf(u * (1.0 / math.sqrt(2.0))))
        pdf = jnp.exp(-0.5 * u * u) * (1.0 / math.sqrt(2.0 * math.pi))
        g = (u * cdf).astype(bf16)
        g_ref[:, span] = g
        x2 = x2 + dot_nn(g, w_down_ref[span, :])
        du = (dot_nt(dm, w_down_ref[span, :]) * (cdf + u * pdf)).astype(bf16)
        du_ref[:, span] = du
        add_sum(B_UP, index * part, du)
        dh2 = dh2 + dot_nt(du, matrix(w_up_ref, span))
    out_ref[...] = (x2 * valid).astype(bf16)
    z = x2.astype(bf16)
    z_ref[...] = z
    aligned_ref[...] = ((dot_nn(z, matrix(w_head_ref)) + row(vec_ref, B_HEAD, cot_align_ref.shape[1])) * valid).astype(bf16)

    add_sum(GAIN_TWO, 0, dh2 * n2)
    add_sum(SHIFT_TWO, 0, dh2)
    t = dh2 * gain
    inner = t - jnp.mean(t, axis=-1, keepdims=True) - n2 * jnp.mean(t * n2, axis=-1, keepdims=True)
    dx1 = dx2 + inverse * inner
    da = dx1.astype(bf16)
    da_ref[...] = da
    add_sum(B_PROJ, 0, da)
    do_ref[...] = dot_nt(da, matrix(w_proj_ref)).astype(bf16)


def middle(order, counts, tokens, o, cot_out, cot_align, weights, vectors):
    rows, width = tokens.shape
    hidden, align = weights[1].shape[1], weights[3].shape[1]
    size = row_tile(rows, 320)

    def by_row(columns):
        return pl.BlockSpec((size, columns), lambda i, p: (i, 0))

    def row_shape(columns, dtype=bf16):
        return shape_of((rows, columns), dtype)

    outs = [
        (by_row(width), row_shape(width)),
        (by_row(align), row_shape(align)),
        (by_row(width), row_shape(width)),
        (by_row(align), row_shape(align)),
        (by_row(width), row_shape(width)),
        (by_row(hidden), row_shape(hidden)),
        (by_row(hidden), row_shape(hidden)),
        (by_row(width), row_shape(width)),
        (by_row(width), row_shape(width)),
        (by_row(width), row_shape(width)),
    ]
    outs.append((out_whole(vectors.shape), shape_of(vectors.shape, f32)))
    arrays = [array for weight in weights for array in weight.arrays]
    return order(
        functools.partial(middle_kernel, weights),
        "middle",
        [counts, tokens, o, cot_out, cot_align, vectors, *arrays],
        [SMEM, by_row(width), by_row(width), by_row(width), by_row(align), whole(vectors.shape)]
        + [ANY] * len(arrays),
        outs,
        grid=(rows // size,),
        vmem=54,
        scratch=weight_scratch(weights),
    )


def outer_kernel(place_ref, l_ref, r_ref, out_ref):
    out_ref[...] = dot_tn(l_ref[...], r_ref[...]).astype(out_ref.dtype)


def outer(order, left, right, rows_out, columns_out, name):
    rows, m = left.shape
    n = right.shape[1]
    tm, tn = min(rows_out, m), min(columns_out, n)
    return order(
        outer_kernel,
        name,
        [left, right],
        [pl.BlockSpec((rows, tm), lambda i, j, p: (0, i)), pl.BlockSpec((rows, tn), lambda i, j, p: (0, j))],
        [(pl.BlockSpec((tm, tn), lambda i, j, p: (i, j)), shape_of((m, n)))],
        grid=(m // tm, n // tn),
        vmem=56,
    )[0]


BAND = 96
HALF = BAND // 2
FEW = 16


def outer_split_kernel(place_ref, l_ref, r_ref, keep_ref, send_ref, l_scratch):
    levels, _, _, columns = keep_ref.shape

    @pl.when(pl.program_id(0) == 0)
    def _():
        l_scratch[...] = l_ref[...].T

    right = r_ref[0] if len(r_ref.shape) == 3 else r_ref[...]
    total = dot_nn(l_scratch[...], right).astype(bf16)
    shape = (2, HALF, columns)
    first = place_ref[CORE] == 0
    for z in range(levels):
        low = total[2 * z * BAND : (2 * z + 1) * BAND].reshape(shape)
        high = total[(2 * z + 1) * BAND : (2 * z + 2) * BAND].reshape(shape)
        level = place_ref[Z] ^ z
        keep_ref[level] = jnp.where(first, low, high)
        send_ref[level] = jnp.where(first, high, low)


def outer_split(order, left, right, levels, columns_out, total, at, into, name, after=()):
    rows, m = left.shape
    n = right.shape[-1] * (right.shape[0] if right.ndim == 3 else 1)
    if right.ndim == 3:
        columns_out = right.shape[-1]
        r_spec = pl.BlockSpec((1, rows, columns_out), lambda j, p: (j, 0, 0))
    else:
        r_spec = pl.BlockSpec((rows, columns_out), lambda j, p: (0, j))
    out = shape_of((levels, 2, HALF, total))
    out_spec = pl.BlockSpec((levels, 2, HALF, columns_out), lambda j, p: (0, 0, 0, at // columns_out + j))
    return order(
        outer_split_kernel,
        name,
        [left, right],
        [whole(left.shape), r_spec],
        [(out_spec, out)] * 2,
        grid=(n // columns_out,),
        scratch=[pltpu.VMEM((m, rows), bf16)],
        into=into,
        vmem=56,
        after=after,
    )


def outer_group_kernel(steps, place_ref, *refs):
    count = len(steps)
    lefts, rights, outs = refs[:count], refs[count : 2 * count], refs[2 * count : 4 * count]
    turned, held, sems = refs[4 * count], refs[4 * count + 1 : 5 * count], refs[5 * count]
    step = pl.program_id(0)
    first = place_ref[CORE] == 0
    copies = [pltpu.make_async_copy(lefts[i], held[i - 1], sems.at[i - 1]) for i in range(1, count)]

    @pl.when(step == 0)
    def _():
        for copy in copies:
            copy.start()

    begin = 0
    for i, length in enumerate(steps):
        keep_ref, send_ref = outs[2 * i], outs[2 * i + 1]

        @pl.when(step == begin)
        def _():
            if i:
                copies[i - 1].wait()
                turned[...] = held[i - 1][...].T
            else:
                turned[...] = lefts[0][...].T

        @pl.when((step >= begin) & (step < begin + length))
        def _():
            total = dot_nn(turned[...], rights[i][...]).astype(bf16)
            levels, _, _, columns = keep_ref.shape
            shape = (2, HALF, columns)
            for z in range(levels):
                low = total[2 * z * BAND : (2 * z + 1) * BAND].reshape(shape)
                high = total[(2 * z + 1) * BAND : (2 * z + 2) * BAND].reshape(shape)
                level = place_ref[Z] ^ z
                keep_ref[level] = jnp.where(first, low, high)
                send_ref[level] = jnp.where(first, high, low)

        begin += length


def outer_group(order, pairs, columns_out, levels, name):
    rows, m = pairs[0][0].shape
    steps = [right.shape[1] // columns for (_, right), columns in zip(pairs, columns_out)]
    rights, outs, begin = [], [], 0
    for (_, right), columns, length in zip(pairs, columns_out, steps):

        def at(j, begin=begin, length=length):
            return jnp.clip(j - begin, 0, length - 1)

        rights.append(pl.BlockSpec((rows, columns), lambda j, p, at=at: (0, at(j))))
        out_spec = pl.BlockSpec((levels, 2, HALF, columns), lambda j, p, at=at: (0, 0, 0, at(j)))
        outs += [(out_spec, shape_of((levels, 2, HALF, right.shape[1])))] * 2
        begin += length
    results = order(
        functools.partial(outer_group_kernel, steps),
        name,
        [left for left, _ in pairs] + [right for _, right in pairs],
        [whole((rows, m))] + [ANY] * (len(pairs) - 1) + rights,
        outs,
        grid=(sum(steps),),
        scratch=[pltpu.VMEM((m, rows), bf16)]
        + [pltpu.VMEM((rows, m), bf16)] * (len(pairs) - 1)
        + [pltpu.SemaphoreType.DMA((len(pairs) - 1,))],
        vmem=56,
    )
    return [results[2 * i : 2 * i + 2] for i in range(len(pairs))]


def split_kernel(sets, place_ref, *refs):
    pairs, outs = refs[: 2 * len(sets)], refs[2 * len(sets) :]
    for own in range(4):

        @pl.when(place_ref[Y] * 2 + place_ref[X] == own)
        def _():
            for quarter, out_ref in enumerate(outs):
                y, x = divmod(own ^ quarter, 2)
                at = 0
                for number, members in enumerate(sets):
                    keep_ref, got_ref = pairs[2 * number : 2 * number + 2]
                    first = 0
                    for columns in members:
                        half = columns // 2
                        part = slice(first + x * half, first + (x + 1) * half)
                        out_ref[:, :, at : at + half] = keep_ref[:, y, :, part] + got_ref[:, y, :, part]
                        at, first = at + half, first + columns


def split(order, sets, pairs, name):
    levels = pairs[0][0].shape[0]
    total = sum(keep.shape[3] for keep, _ in pairs)
    shape = (levels, HALF, total // 2)
    if len(pairs) == 1:
        ins, out, grid, vmem = [VMEM] * 2, VMEM, (), 32
    else:
        ins = [pl.BlockSpec((1,) + keep.shape[1:], lambda k, p: (k, 0, 0, 0)) for keep, _ in pairs for _ in range(2)]
        out, grid, vmem = pl.BlockSpec((1,) + shape[1:], lambda k, p: (k, 0, 0)), (levels,), 56
    return order(
        functools.partial(split_kernel, sets),
        name,
        [array for pair in pairs for array in pair],
        ins,
        [(out, shape_of(shape))] * 4,
        grid=grid,
        vmem=vmem,
    )


def levels_kernel(levels, place_ref, *refs):
    ins, lines, outs = refs[:4], refs[4:-levels], refs[-levels:]
    columns = ins[0].shape[2]
    for level, out_ref in enumerate(outs):
        total = ins[0][level].astype(f32)
        for ref in ins[1:]:
            total = total + ref[level].astype(f32)
        out_ref[:, :columns] = total.astype(bf16)
        if lines:
            total = lines[0][level].astype(f32)
            for ref in lines[1:]:
                total = total + ref[level].astype(f32)
            out_ref[0:FEW, columns:] = total.astype(bf16)
            out_ref[FEW:, columns:] = jnp.zeros((HALF - FEW, TILE), bf16)


def by_level(order, quarters, lines, name):
    levels, height, columns = quarters[0].shape
    columns += TILE if lines else 0
    return order(
        functools.partial(levels_kernel, levels),
        name,
        list(quarters) + list(lines),
        [VMEM] * (4 + len(lines)),
        [(VMEM, shape_of((height, columns)))] * levels,
    )


def halves_kernel(place_ref, *refs):
    ins, outs = refs[:-2], refs[-2:]
    half = ins[0].shape[0] // 2
    for out, out_ref in enumerate(outs):
        part = slice(out * half, (out + 1) * half)
        total = ins[0][part].astype(f32)
        for ref in ins[1:]:
            total = total + ref[part].astype(f32)
        out_ref[...] = total.astype(bf16).reshape(out_ref.shape)


def by_half(order, arrays, name):
    levels, height, columns = arrays[0].shape
    shape = (height, columns) if levels == 2 else (levels // 2, height, columns)
    return order(halves_kernel, name, arrays, [VMEM] * len(arrays), [(VMEM, shape_of(shape))] * 2)


def add_kernel(parts, place_ref, *refs):
    ins, beside, out_ref = refs[:parts], refs[parts:-1], refs[-1]
    columns = ins[0].shape[1]
    total = ins[0][...].astype(f32)
    for ref in ins[1:]:
        total = total + ref[...].astype(f32)
    out_ref[:, :columns] = total.astype(bf16)
    for ref in beside:
        width = ref.shape[1]
        for band in range(ref.shape[0] // HALF):
            out_ref[:, columns : columns + width] = ref[band * HALF : (band + 1) * HALF, :]
            columns += width


def add_up(order, arrays, beside, name):
    height, columns = arrays[0].shape
    columns += sum(b.size // height for b in beside)
    return order(
        functools.partial(add_kernel, len(arrays)),
        name,
        list(arrays) + list(beside),
        [VMEM] * (len(arrays) + len(beside)),
        [(VMEM, shape_of((height, columns)))],
    )[0]


def join_kernel(members, lengths, beside, place_ref, *refs):
    quarters, outs = refs[:4], refs[4:]
    for x in (0, 1):

        @pl.when(place_ref[X] == x)
        def _():
            for quarter, ref in enumerate(quarters):
                y = place_ref[Y] ^ (quarter // 2)
                across = x ^ (quarter % 2)
                at = 0
                for number, columns in enumerate(members):
                    half = columns // 2
                    outs[number][y, :, across * half : (across + 1) * half] = ref[:, at : at + half].astype(f32)
                    at += half

    if beside:
        at = sum(members) // 2 + (TILE if lengths else 0)
        out_ref = outs[len(members)]
        width = out_ref.shape[3]
        for quarter, ref in enumerate(quarters):
            owner = (place_ref[Y] * 2 + place_ref[X]) ^ quarter
            for band in range(out_ref.shape[1]):
                columns = slice(at + band * width, at + (band + 1) * width)
                out_ref[owner, band] = ref[:, columns].astype(f32)

    if lengths:
        at = sum(members) // 2
        lines = quarters[0][0:FEW, at : at + TILE].astype(f32)
        for ref in quarters[1:]:
            lines = lines + ref[0:FEW, at : at + TILE].astype(f32)
        line = 0
        for part, out_ref in zip(lengths, outs[len(members) + (1 if beside else 0) :]):
            rows = []
            for length in part:
                pieces = []
                for i in range(lines_of(length)):
                    pieces.append(lines[line + i : line + i + 1, : min(TILE, length - i * TILE)])
                rows.append(jnp.concatenate(pieces, axis=1) if len(pieces) > 1 else pieces[0])
                line += lines_of(length)
            if len(rows) == 1:
                out_ref[...] = rows[0][0]
            else:
                for i, value in enumerate(rows):
                    out_ref[i : i + 1, :] = value


def join(order, quarters, members, lengths, beside, name):
    outs = [(VMEM, shape_of((2, HALF, columns), f32)) for columns in members]
    if beside:
        rows, columns = beside
        outs.append((VMEM, shape_of((4, rows // (4 * HALF), HALF, columns), f32)))
    for part in lengths:
        outs.append((VMEM, shape_of((part[0],) if len(part) == 1 else (len(part), part[0]), f32)))
    results = order(
        functools.partial(join_kernel, members, lengths, beside),
        name,
        quarters,
        [VMEM] * 4,
        outs,
    )
    matrices = len(members) + (1 if beside else 0)
    return [r.reshape(-1, r.shape[-1]) for r in results[:matrices]] + list(results[matrices:])


class Reduction:
    def __init__(self, order, name):
        self.order, self.name = order, name
        self.sets, self.pairs = [], []

    def add(self, keep, send, members):
        self.sets.append(members)
        self.pairs.append((keep, swap(send, self.name + "_core", fsdp=1)))

    def split(self):
        quarters = split(self.order, self.sets, self.pairs, self.name + "_split")
        self.quarters = [quarters[0]] + [swap(quarters[j], self.name + "_plane", dp=j) for j in (1, 2, 3)]

    def levels(self, lines=()):
        parts = by_level(self.order, self.quarters, lines, self.name + "_levels")
        self.parts = [parts[0]]
        self.parts += [swap(part, self.name + "_column", fsdp=2 * level) for level, part in enumerate(parts) if level]

    def halve(self):
        arrays = self.quarters
        levels = arrays[0].shape[0]
        near, far = by_half(self.order, arrays, f"{self.name}_half_{levels}")
        self.quarters = [near, swap(far, self.name + "_column", fsdp=levels)]
        self.parts = self.quarters

    def total(self, beside=()):
        near = add_up(self.order, self.parts, beside, self.name + "_total")
        self.near = [near] + [swap(near, self.name + "_back", dp=j) for j in (1, 2, 3)]

    def join(self, lengths=(), beside=()):
        members = [columns for members in self.sets for columns in members]
        return join(self.order, self.near, members, lengths, beside, self.name + "_join")


def lines_of(length):
    return -(-length // TILE)


def pack_kernel(lengths, members, place_ref, *refs):
    arrays, (keep_ref, send_ref) = refs[:-2], refs[-2:]
    levels = keep_ref.shape[0]
    first = place_ref[CORE] == 0
    values = []
    for index, length in enumerate(lengths):
        if index in members:
            array, line = members[index]
            values.append(arrays[array][line : line + 1, : 2 * levels * length])
        else:
            values.append(jnp.zeros((1, 2 * levels * length), f32))

    def lines(shard):
        rows = []
        for value, length in zip(values, lengths):
            part = value[:, shard * length : (shard + 1) * length]
            if length % TILE:
                part = jnp.concatenate([part, jnp.zeros((1, -length % TILE), f32)], axis=1)
            rows += [part[:, at : at + TILE] for at in range(0, part.shape[1], TILE)]
        return jnp.concatenate(rows + [jnp.zeros((FEW - len(rows), TILE), f32)], axis=0)

    for z in range(levels):
        level = place_ref[Z] ^ z
        low, high = lines(2 * z), lines(2 * z + 1)
        keep_ref[level] = jnp.where(first, low, high).astype(bf16)
        send_ref[level] = jnp.where(first, high, low).astype(bf16)


def pack_vectors(order, arrays, members, lengths, levels, name, after=()):
    shape = (levels, FEW, TILE)
    return order(
        functools.partial(pack_kernel, lengths, members),
        name,
        arrays,
        [VMEM] * len(arrays),
        [(VMEM, shape_of(shape))] * 2,
        after=after,
    )


def unpack_kernel(lengths, place_ref, own_ref, other_ref, out_ref):
    levels = own_ref.shape[0]
    first = place_ref[CORE] == 0
    shards = []
    for z in range(levels):
        own = own_ref[z].astype(f32)
        other = other_ref[z].astype(f32)
        shards += [jnp.where(first, own, other), jnp.where(first, other, own)]
    at = 0
    for index, length in enumerate(lengths):
        pieces = []
        for shard in shards:
            for line in range(lines_of(length)):
                pieces.append(shard[at + line : at + line + 1, : min(TILE, length - line * TILE)])
        out_ref[index : index + 1, : length * len(shards)] = jnp.concatenate(pieces, axis=1).astype(bf16)
        at += lines_of(length)


def unpack_vectors(order, own, other, lengths):
    levels = own.shape[0]
    return order(
        functools.partial(unpack_kernel, lengths),
        "unpack_vectors",
        [own, other],
        [VMEM] * 2,
        [(VMEM, shape_of((ROWS, 2 * levels * max(lengths))))],
    )[0]


def start_kernel(lengths, groups, place_ref, *refs):
    count = sum(len(g) for g in groups)
    vectors = refs[: len(refs) - count - len(groups)]
    shards, outs = refs[len(vectors) : len(vectors) + count], refs[len(vectors) + count :]
    at = 0
    for group, out_ref in zip(groups, outs):
        column = 0
        for _ in group:
            half = shards[at].shape[1]
            out_ref[:, column : column + half] = shards[at][...]
            column += half
            at += 1
    values = []
    for ref in vectors:
        value = ref[...].astype(f32)
        values += [value[i] for i in range(value.shape[0])] if value.ndim == 2 else [value]
    lines = []
    for value, length in zip(values, lengths):
        if length % TILE:
            value = jnp.concatenate([value, jnp.zeros((-length % TILE,), f32)])
        lines += [value[at : at + TILE].reshape(1, TILE) for at in range(0, value.shape[0], TILE)]
    lines.append(jnp.zeros((HALF - len(lines), TILE), f32))
    outs[0][:, outs[0].shape[1] - TILE :] = jnp.concatenate(lines, axis=0).astype(bf16)


def start_gather(order, vectors, lengths, groups):
    shards = [w for group in groups for w in group]
    outs = []
    for number, group in enumerate(groups):
        shape = (HALF, sum(w.shape[1] // 2 for w in group) + (TILE if number == 0 else 0))
        outs.append((out_whole(shape), shape_of(shape)))
    return order(
        functools.partial(start_kernel, lengths, groups),
        "quarters",
        list(vectors) + shards,
        [whole(v.shape) for v in vectors]
        + [pl.BlockSpec((w.shape[0] // 2, w.shape[1] // 2), lambda i, p: (p[Y], p[X])) for w in shards],
        outs,
        grid=(1,),
        vmem=56,
    )


def near_kernel(levels, place_ref, *refs):
    got, out_ref, lines = refs[:levels], refs[levels], refs[levels + 1 :]
    columns = out_ref.shape[2]
    for level, ref in enumerate(got):
        if level:
            out_ref[level - 1] = ref[:, :columns]
        for lines_ref in lines:
            lines_ref[place_ref[Z] ^ level] = ref[0:FEW, columns:]


def near_levels(order, got, lines, name):
    levels, (height, columns) = len(got), got[0].shape
    columns -= TILE if lines else 0
    outs = [(VMEM, shape_of((levels - 1, height, columns)))]
    if lines:
        outs.append((VMEM, shape_of((levels, FEW, TILE))))
    return order(
        functools.partial(near_kernel, levels),
        name,
        got,
        [VMEM] * levels,
        outs,
    )


def assemble_kernel(halves, place_ref, *refs):
    shards, refs = refs[: len(halves)], refs[len(halves) :]
    quarters, out_ref = refs[:4], refs[4]
    z = place_ref[Z]
    column = 0
    for shard in shards:
        columns = shard.shape[1]
        for y in (0, 1):
            out_ref[z, y, :, column : column + columns] = shard[y * HALF : (y + 1) * HALF, :]
        column += columns
    for x in (0, 1):

        @pl.when(place_ref[X] == x)
        def _():
            for quarter, ref in enumerate(quarters):
                y = place_ref[Y] ^ (quarter // 2)
                across = x ^ (quarter % 2)
                for level in range(ref.shape[0]):
                    source, column = 0, 0
                    for half in halves:
                        target = column + across * half
                        out_ref[z ^ (level + 1), y, :, target : target + half] = ref[level, :, source : source + half]
                        source, column = source + half, column + 2 * half


def assemble(order, shards, quarters, name):
    levels = quarters[0].shape[0] + 1
    halves = [shard.shape[1] // 2 for shard in shards]
    return order(
        functools.partial(assemble_kernel, halves),
        name,
        list(shards) + list(quarters),
        [VMEM] * (len(shards) + 4),
        [(VMEM, shape_of((levels, 2, HALF, 2 * sum(halves))))],
    )[0].reshape(levels, BAND, -1)


def across_plane(near, name):
    return [near] + [swap(near, name + "_plane", dp=j) for j in (1, 2, 3)]


def first_back_kernel(weight, place_ref, tok_ref, dx_ref, d_ref, vec_ref, *refs):
    arrays, (out_ref, sums_ref, w_ref, sems) = split_refs(refs, [weight])
    width = tok_ref.shape[1]

    @pl.when(pl.program_id(0) == 0)
    def _():
        fetch_all(place_ref, [weight], arrays, [w_ref], sems)
        sums_ref[...] = jnp.zeros_like(sums_ref)

    dh = dot_nt(d_ref[0], matrix(w_ref, slice(0, width)))
    dh = dh + dot_nt(d_ref[1], matrix(w_ref, slice(width, 2 * width)))
    dh = dh + dot_nt(d_ref[2], matrix(w_ref, slice(2 * width, 3 * width)))
    n1, inverse = normed(tok_ref[...].astype(f32))
    sums_ref[0:1, :] += jnp.sum(dh * n1, axis=0, keepdims=True)
    sums_ref[1:2, :] += jnp.sum(dh, axis=0, keepdims=True)
    t = dh * row(vec_ref, GAIN_ONE, width)
    inner = t - jnp.mean(t, axis=-1, keepdims=True) - n1 * jnp.mean(t * n1, axis=-1, keepdims=True)
    out_ref[...] = (dx_ref[...].astype(f32) + inverse * inner).astype(bf16)


def first_back(order, tokens, dx1, dqkv, weight, vectors):
    rows, width = tokens.shape
    size = row_tile(rows, 320)
    rowwise = pl.BlockSpec((size, width), lambda i, p: (i, 0))
    return order(
        functools.partial(first_back_kernel, weight),
        "first_back",
        [tokens, dx1, dqkv, vectors] + weight.arrays,
        [rowwise, rowwise, pl.BlockSpec((3, size, width), lambda i, p: (0, i, 0)), whole(vectors.shape)]
        + [ANY] * len(weight.arrays),
        [(rowwise, shape_of((rows, width))), (out_whole((2, width)), shape_of((2, width), f32))],
        grid=(rows // size,),
        scratch=weight_scratch([weight]),
        vmem=56,
    )


def local(
    tokens,
    ln1_gain,
    ln1_bias,
    w_qkv,
    qv_bias,
    w_proj,
    proj_bias,
    ln2_gain,
    ln2_bias,
    w_up,
    up_bias,
    w_down,
    down_bias,
    w_head,
    head_bias,
    clip_counts,
    cot_out,
    cot_align,
):
    rows, width = tokens.shape
    shards = lax.axis_size("fsdp")
    levels = shards // 2
    order = Order(position())
    own_vectors = (ln1_gain, ln1_bias, qv_bias, proj_bias, ln2_gain, ln2_bias, up_bias, down_bias, head_bias)
    parts = [[v.shape[-1]] * (v.size // v.shape[-1]) for v in own_vectors]
    lengths = [length for part in parts for length in part]
    paired = (
        lax.axis_size("dp") == 4
        and shards % 2 == 0
        and levels in (2, 4, 8)
        and w_qkv.shape[0] == BAND
        and sum(lines_of(n) for n in lengths) <= FEW
    )

    def gather(value):
        return lax.all_gather(value, "fsdp", axis=0, tiled=True)

    def scatter(value):
        return lax.psum_scatter(value, "fsdp", scatter_dimension=0, tiled=True)

    if paired:
        wide = [w_up, w_head, w_proj]
        p_qkv, p_wide = start_gather(order, own_vectors, lengths, [[w_qkv], wide])
        got = [p_qkv] + [swap(p_qkv, "qkv_column", fsdp=2 * level) for level in range(1, levels)]
        got_wide = [p_wide] + [swap(p_wide, "wide_column", fsdp=2 * level) for level in range(1, levels)]
        bias = make_masks(order, clip_counts, rows)
        near, lines = near_levels(order, got, True, "qkv_near")
        quarters = across_plane(near, "qkv")
        other_lines = swap(lines, "vectors_core", fsdp=1)
        own = assemble(order, [w_qkv], quarters, "qkv_assemble")
        full_qkv = Weight([own, swap(own, "qkv_core", fsdp=1)], 0, (width, w_qkv.shape[1]))
        later, own = lax.optimization_barrier((w_down, own))
        full_down = gather(later)
        vectors = unpack_vectors(order, lines, other_lines, lengths)
        (near,) = near_levels(order, got_wide, False, "wide_near")
        quarters = across_plane(near, "wide")
    else:
        pieces = [piece for v in own_vectors for piece in ([v[0], v[1]] if v.ndim == 2 else [v])]
        joined = gather(jnp.concatenate(pieces)[None])
        lines, at = [], 0
        for length in lengths:
            line = joined[:, at : at + length].reshape(1, -1)
            lines.append(jnp.pad(line, ((0, 0), (0, shards * max(lengths) - line.shape[1]))))
            at += length
        vectors = jnp.pad(jnp.concatenate(lines), ((0, ROWS - len(lines)), (0, 0)))
        full_qkv, full_proj, full_up, full_head = (
            Weight([full], 0, full.shape) for full in (gather(w) for w in (w_qkv, w_proj, w_up, w_head))
        )
        full_down = gather(w_down)
        bias = make_masks(order, clip_counts, rows)
    full_down = Weight([full_down], 0, full_down.shape)
    h1, q, k, v = project_qkv(order, tokens, vectors, full_qkv)
    o, lse = attend(order, bias, q, k, v)
    if paired:
        own = assemble(order, wide, quarters, "wide_assemble")
        both_cores = [own, swap(own, "wide_core", fsdp=1)]
        at = [0, w_up.shape[1], w_up.shape[1] + w_head.shape[1]]
        full_up, full_head, full_proj = (
            Weight(both_cores, column, (width, w.shape[1])) for column, w in zip(at, wide)
        )
    block_out, aligned, z, e_al, h2, g, du, dm, da, do, sums = middle(
        order,
        clip_counts,
        tokens,
        o,
        cot_out,
        cot_align,
        (full_proj, full_up, full_down, full_head),
        vectors,
    )
    if paired:
        r_wide = Reduction(order, "wide")
        pairs = outer_group(order, [(h2, du), (z, e_al), (o, da)], [768, 512, 768], levels, "grad_wide")
        for pair, w in zip(pairs, wide):
            r_wide.add(*pair, [w.shape[1]])
    d_down = scatter(outer(order, g, dm, 512, 768, "grad_down"))
    if paired:
        r_wide.split()
    dqkv, s_qv = attend_back(order, bias, q, k, v, o, do, lse)
    if paired:
        r_qkv = Reduction(order, "qkv")
        n = w_qkv.shape[1]
        r_qkv.add(*outer_split(order, h1, dqkv, levels, width, n, 0, (), "grad_qkv"), [n])
        early = {B_Q: (1, 0), B_V: (1, 1)}
        early.update({i: (0, i) for i in range(B_PROJ, B_HEAD + 1)})
        keep, send = pack_vectors(order, [sums, s_qv], early, lengths, levels, "pack_early")
        lines = [keep, swap(send, "vectors_core", fsdp=1)]
        r_qkv.split()
        r_wide.halve()
    grad_tokens, s_first = first_back(order, tokens, da, dqkv, full_qkv, vectors)
    if paired:
        late = {GAIN_ONE: (0, 0), SHIFT_ONE: (0, 1)}
        keep, send = pack_vectors(order, [s_first], late, lengths, levels, "pack_late", [d_down])
        lines += [keep, swap(send, "vectors_core", fsdp=1)]
        d_down = lax.psum_scatter(d_down, "dp", scatter_dimension=0, tiled=True)
        r_qkv.levels(lines)
        while r_wide.quarters[0].ndim == 3:
            r_wide.halve()
        r_qkv.total([d_down])
        r_wide.total()
        d_qkv, d_down, *mine = r_qkv.join(lengths=parts, beside=w_down.shape)
        d_up, d_head, d_proj = r_wide.join()
    else:

        def reduce(value):
            return lax.psum(scatter(value), "dp").astype(f32)

        d_down = lax.psum(d_down, "dp").astype(f32)
        d_up = reduce(outer(order, h2, du, 768, 512, "grad_up"))
        d_head = reduce(outer(order, z, e_al, 768, 512, "grad_head"))
        d_proj = reduce(outer(order, o, da, 768, 384, "grad_proj"))
        d_qkv = reduce(outer(order, h1, jnp.concatenate([dqkv[0], dqkv[1], dqkv[2]], axis=1), 768, 768, "grad_qkv"))
        late = {GAIN_ONE: s_first[0], SHIFT_ONE: s_first[1], B_Q: s_qv[0], B_V: s_qv[1]}
        lines = [late.get(i, sums[i])[: shards * n].reshape(shards, n) for i, n in enumerate(lengths)]
        joined = jnp.concatenate(lines, axis=1)
        joined = lax.psum(lax.psum_scatter(joined, "fsdp", scatter_dimension=0, tiled=True), "dp")[0]
        mine, at = [], 0
        for part in parts:
            size = sum(part)
            mine.append(joined[at : at + size].reshape((part[0],) if len(part) == 1 else (len(part), -1)))
            at += size
    d_gain_one, d_shift_one, d_qv, d_b_proj, d_gain_two, d_shift_two, d_b_up, d_b_down, d_b_head = mine
    return (
        block_out,
        aligned,
        grad_tokens,
        d_gain_one,
        d_shift_one,
        d_qkv,
        d_qv,
        d_proj,
        d_b_proj,
        d_gain_two,
        d_shift_two,
        d_up,
        d_b_up,
        d_down,
        d_b_down,
        d_head,
        d_b_head,
    )


def solution(mesh):
    rows = P(("dp", "fsdp"), None)
    matrix, vector, pair = P("fsdp", None), P("fsdp"), P(None, "fsdp")
    return jax.shard_map(
        local,
        mesh=mesh,
        in_specs=(
            rows,
            vector,
            vector,
            matrix,
            pair,
            matrix,
            vector,
            vector,
            vector,
            matrix,
            vector,
            matrix,
            vector,
            matrix,
            vector,
            P(),
            rows,
            rows,
        ),
        out_specs=(
            rows,
            rows,
            rows,
            vector,
            vector,
            matrix,
            pair,
            matrix,
            vector,
            vector,
            vector,
            matrix,
            vector,
            matrix,
            vector,
            matrix,
            vector,
        ),
        check_vma=False,
    )
```

```python
import functools
import math

import jax
import jax.numpy as jnp
from jax import lax
from jax.experimental import pallas as pl
from jax.experimental.pallas import tpu as pltpu
from jax.sharding import PartitionSpec as P

HEADS = 12
LONGEST = 157
EPSILON = 1e-06
MASKED = -1e30
TILE = 128

f32 = jnp.float32
bf16 = jnp.bfloat16


def dot_nn(left, right):
    return lax.dot_general(left, right, (((1,), (0,)), ((), ())), preferred_element_type=f32)


def dot_nt(left, right):
    return lax.dot_general(left, right, (((1,), (1,)), ((), ())), preferred_element_type=f32)


def dot_tn(left, right):
    return lax.dot_general(left, right, (((0,), (0,)), ((), ())), preferred_element_type=f32)


def attention_tiles(rows):
    tiles, offset = [], 0
    reach = LONGEST - 1
    for start in range(0, rows, TILE):
        size = min(TILE, rows - start)
        low = max(0, (start - reach) // 16 * 16)
        high = min(rows, -(-(start + size + reach) // 16) * 16)
        tiles.append((start, size, low, high - low, offset))
        offset += high - low
    return tiles, offset


def row_tile(rows, most):
    for size in range(most, 15, -16):
        if rows % size == 0:
            return size
    return rows


USUAL = 10
TIMES = {
    "attend_back": 60,
    "grad_down": 30,
    "pack_early": 30,
    "qkv_split": 1,
    "pack_late": 1,
    "wide_half_4": 1,
    "qkv_levels": 1,
    "wide_half_2": 1,
    "qkv_total": 1,
    "wide_total": 1,
}


def duration(name):
    return pl.CostEstimate(flops=TIMES.get(name, USUAL) * 10**9, bytes_accessed=1, transcendentals=0)


def whole(shape):
    return pl.BlockSpec(shape, lambda *_: (0,) * len(shape), pipeline_mode=pl.Buffered(1))


def out_whole(shape):
    return pl.BlockSpec(shape, lambda *_: (0,) * len(shape))


SMEM = pl.BlockSpec(memory_space=pltpu.SMEM)
VMEM = pl.BlockSpec(memory_space=pltpu.VMEM)
ANY = pl.BlockSpec(memory_space=pl.ANY)


def shape_of(shape, dtype=bf16):
    return jax.ShapeDtypeStruct(tuple(shape), dtype)


class Order:
    def __init__(self, place):
        self.place, self.last = place, None

    def __call__(self, kernel, name, arrays, in_specs, outs, grid=(), scratch=(), into=(), after=(), vmem=32):
        in_specs, arrays = list(in_specs), list(arrays)
        seen = 1 + len(arrays)
        aliases = {seen + i: i for i in range(len(into))}
        extra = (list(into) or ([] if self.last is None else [self.last])) + list(after)
        in_specs += [ANY] * len(extra)
        arrays += extra

        def body(*refs):
            kernel(*refs[:seen], *refs[seen + len(extra) :])

        result = pl.pallas_call(
            body,
            grid_spec=pltpu.PrefetchScalarGridSpec(
                num_scalar_prefetch=1,
                grid=grid,
                in_specs=in_specs,
                out_specs=tuple(spec for spec, _ in outs),
                scratch_shapes=list(scratch),
            ),
            out_shape=tuple(shape for _, shape in outs),
            cost_estimate=duration(name),
            input_output_aliases=aliases,
            compiler_params=pltpu.CompilerParams(vmem_limit_bytes=vmem << 20),
            name=name,
        )(self.place, *arrays)
        self.last = result[0]
        return result


Z, CORE, Y, X, SEQ = range(5)


def position():
    dp, fsdp = lax.axis_index("dp"), lax.axis_index("fsdp")
    seq = dp * lax.axis_size("fsdp") + fsdp
    return jnp.stack([fsdp // 2, fsdp % 2, dp // 2, dp % 2, seq]).astype(jnp.int32)


def swap(value, name, dp=0, fsdp=0):
    m, n = lax.axis_size("dp"), lax.axis_size("fsdp")
    pairs = [(i * n + j, (i ^ dp) * n + (j ^ fsdp)) for i in range(m) for j in range(n)]
    with jax.named_scope(f"{name}_{dp}_{fsdp}"):
        return lax.ppermute(value, ("dp", "fsdp"), pairs)


class Weight:
    def __init__(self, arrays, column, shape):
        self.arrays, self.column, self.shape = list(arrays), column, tuple(shape)
        if len(self.arrays) == 1:
            self.scratch = self.shape
        else:
            levels, rows, _ = arrays[0].shape
            self.scratch = (levels, 2, rows, shape[1])

    def copies(self, place, refs, weight, sems, first):
        columns = pl.ds(self.column, self.shape[1])
        if len(refs) == 1:
            return [pltpu.make_async_copy(refs[0], weight, sems.at[first])]
        return [
            pltpu.make_async_copy(ref.at[:, :, columns], weight.at[:, place[CORE] ^ i], sems.at[first + i])
            for i, ref in enumerate(refs)
        ]


def matrix(ref, columns=slice(None)):
    if len(ref.shape) == 2:
        return ref[:, columns]
    value = ref[:, :, :, columns]
    return value.reshape(-1, value.shape[-1])


def fetch_all(place, weights, arrays, scratch, sems):
    copies = []
    for weight, refs, target in zip(weights, arrays, scratch):
        copies += weight.copies(place, refs, target, sems, len(copies))
    for copy in copies:
        copy.start()
    for copy in copies:
        copy.wait()


def split_refs(refs, weights):
    groups, at = [], 0
    for weight in weights:
        groups.append(refs[at : at + len(weight.arrays)])
        at += len(weight.arrays)
    return groups, refs[at:]


def weight_scratch(weights):
    scratch = [pltpu.VMEM(w.scratch, bf16) for w in weights]
    return scratch + [pltpu.SemaphoreType.DMA((sum(len(w.arrays) for w in weights),))]


GAIN_ONE, SHIFT_ONE, B_Q, B_V, B_PROJ, GAIN_TWO, SHIFT_TWO, B_UP, B_DOWN, B_HEAD = range(10)
ROWS = 16


def row(vectors_ref, index, length):
    return vectors_ref[index : index + 1, :length].astype(f32)


def mask_kernel(tiles, place_ref, counts_ref, bias_ref, seg_ref):
    rows = seg_ref.shape[0]
    slots = counts_ref.shape[1]
    seq = place_ref[SEQ]
    ends, total = [], jnp.int32(0)
    for slot in range(slots):
        total = total + counts_ref[seq, slot]
        ends.append(total)
    places = lax.broadcasted_iota(jnp.int32, (rows, TILE), 0)
    seg = jnp.zeros((rows, TILE), jnp.int32)
    for end in ends:
        seg = seg + jnp.where(places >= end, 1, 0)
    seg_ref[...] = seg
    lanes = lax.broadcasted_iota(jnp.int32, (8, TILE), 1)
    for start, size, low, keys, offset in tiles:
        own = start + jnp.where(lanes >= size, lanes - size, lanes)
        seg_own = jnp.zeros((8, TILE), jnp.int32)
        for end in ends:
            seg_own = seg_own + jnp.where(own >= end, 1, 0)
        same = seg_ref[low : low + keys, :] == seg_own[0:1, :]
        bias_ref[offset : offset + keys, :] = jnp.where(same, 0.0, MASKED).astype(f32)


def make_masks(order, counts, rows):
    tiles, total = attention_tiles(rows)
    return order(
        functools.partial(mask_kernel, tiles),
        "masks",
        [counts],
        [SMEM],
        [(out_whole((total, TILE)), shape_of((total, TILE), f32))],
        scratch=[pltpu.VMEM((rows, TILE), jnp.int32)],
    )[0]


def normed(values):
    center = values - jnp.mean(values, axis=-1, keepdims=True)
    spread = jnp.mean(center * center, axis=-1, keepdims=True)
    inverse = lax.rsqrt(spread + EPSILON)
    return center * inverse, inverse


def qkv_kernel(scale, weight, place_ref, tok_ref, vec_ref, *refs):
    arrays, (h_ref, q_ref, k_ref, v_ref, w_ref, sems) = split_refs(refs, [weight])
    width = tok_ref.shape[1]

    @pl.when(pl.program_id(0) == 0)
    def _():
        fetch_all(place_ref, [weight], arrays, [w_ref], sems)

    n1, _ = normed(tok_ref[...].astype(f32))
    hidden = (n1 * row(vec_ref, GAIN_ONE, width) + row(vec_ref, SHIFT_ONE, width)).astype(bf16)
    h_ref[...] = hidden
    q = dot_nn(hidden, matrix(w_ref, slice(0, width)))
    q_ref[...] = ((q + row(vec_ref, B_Q, width)) * scale).astype(bf16)
    k = dot_nn(hidden, matrix(w_ref, slice(width, 2 * width)))
    k_ref[...] = k.astype(bf16)
    v = dot_nn(hidden, matrix(w_ref, slice(2 * width, 3 * width)))
    v_ref[...] = (v + row(vec_ref, B_V, width)).astype(bf16)


def project_qkv(order, tokens, vectors, weight):
    rows, width = tokens.shape
    scale = (width // HEADS) ** (-0.5)
    size = row_tile(rows, 320)
    rowwise = pl.BlockSpec((size, width), lambda i, p: (i, 0))
    return order(
        functools.partial(qkv_kernel, scale, weight),
        "norm_qkv",
        [tokens, vectors] + weight.arrays,
        [rowwise, whole(vectors.shape)] + [ANY] * len(weight.arrays),
        [(rowwise, shape_of((rows, width)))] * 4,
        grid=(rows // size,),
        scratch=weight_scratch([weight]),
    )


def stack_heads(pair, size):
    lanes = lax.broadcasted_iota(jnp.int32, pair.shape, 1)
    half = pair.shape[1] // 2
    zero = jnp.zeros_like(pair)
    first = jnp.where(lanes < half, pair, zero)
    second = jnp.where(lanes < half, zero, pair)
    return jnp.concatenate([first, second], axis=0)


def both(bias, size):
    return bias if size < TILE else jnp.concatenate([bias, bias], axis=1)


def unstack(columns, size, half):
    return jnp.concatenate([columns[:half, :size], columns[half:, size:]], axis=0).T


def attend_kernel(tiles, place_ref, bias_ref, q_ref, k_ref, v_ref, o_ref, lse_ref):
    half = q_ref.shape[1] // 2
    scores = []
    for start, size, low, keys, offset in tiles:
        stacked = stack_heads(q_ref[start : start + size, :], size)
        value = dot_nt(k_ref[low : low + keys, :], stacked)
        scores.append(value + both(bias_ref[offset : offset + keys, :], size))
    parts = []
    for value in scores:
        top = jnp.max(value, axis=0, keepdims=True)
        weights = jnp.exp(value - top)
        parts.append((weights.astype(bf16), top, jnp.sum(weights, axis=0, keepdims=True)))
    for index, (start, size, low, keys, _) in enumerate(tiles):
        weights, top, total = parts[index]
        columns = dot_tn(v_ref[low : low + keys, :], weights) * (1.0 / total)
        o_ref[start : start + size, :] = unstack(columns, size, half).astype(bf16)
        lse_ref[0, index : index + 1, : 2 * size] = top + jnp.log(total)


def attend(order, bias, q, k, v):
    rows, width = q.shape
    tiles, total = attention_tiles(rows)
    span = 2 * (width // HEADS)
    pairs = HEADS // 2
    column = pl.BlockSpec((rows, span), lambda i, p: (0, i))
    return order(
        functools.partial(attend_kernel, tiles),
        "attend",
        [bias, q, k, v],
        [whole(bias.shape), column, column, column],
        [
            (column, shape_of((rows, width))),
            (
                pl.BlockSpec((1, len(tiles), 2 * TILE), lambda i, p: (i, 0, 0)),
                shape_of((pairs, len(tiles), 2 * TILE), f32),
            ),
        ],
        grid=(pairs,),
    )


def attend_back_kernel(
    tiles, scale, place_ref, bias_ref, q_ref, k_ref, v_ref, o_ref, do_ref, lse_ref, d_ref, dqv_ref, dk_sum, dv_sum
):
    half = q_ref.shape[1] // 2
    dk_sum[...] = jnp.zeros_like(dk_sum)
    dv_sum[...] = jnp.zeros_like(dv_sum)
    dq_total = jnp.zeros((1, 2 * half), f32)
    for pair in range(0, len(tiles), 2):
        group = list(enumerate(tiles))[pair : pair + 2]
        held = []
        for index, (start, size, low, keys, offset) in group:
            window, rows = slice(low, low + keys), slice(start, start + size)
            q2 = stack_heads(q_ref[rows, :], size)
            grads = do_ref[rows, :]
            do2 = stack_heads(grads, size)
            scores = dot_nt(k_ref[window, :], q2) + both(bias_ref[offset : offset + keys, :], size)
            dprobs = dot_nt(v_ref[window, :], do2)
            meet = (grads.astype(f32) * o_ref[rows, :].astype(f32)).T
            delta = jnp.concatenate(
                [
                    jnp.sum(meet[:half, :], axis=0, keepdims=True),
                    jnp.sum(meet[half:, :], axis=0, keepdims=True),
                ],
                axis=1,
            )
            held.append((q2, do2, scores, dprobs, delta))
        lows = []
        for (index, (start, size, *_)), (q2, do2, scores, dprobs, delta) in zip(group, held):
            probs = jnp.exp(scores - lse_ref[0, index : index + 1, : 2 * size])
            lows.append((probs.astype(bf16), (probs * (dprobs - delta)).astype(bf16)))
        for (index, (start, size, low, keys, _)), (q2, do2, *_), (probs, dscores) in zip(group, held, lows):
            window, rows = slice(low, low + keys), slice(start, start + size)
            dv_sum[window, :] += dot_nn(probs, do2)
            dk_sum[window, :] += dot_nn(dscores, q2)
            columns = dot_tn(k_ref[window, :], dscores)
            dq = unstack(columns, size, half).astype(bf16) * bf16(scale)
            d_ref[0, rows, :] = dq
            dq_total = dq_total + jnp.sum(dq.astype(f32), axis=0, keepdims=True)
    d_ref[1, :, :] = dk_sum[...].astype(bf16)
    dv = dv_sum[...].astype(bf16)
    d_ref[2, :, :] = dv
    dqv_ref[0:1, :] = dq_total
    dqv_ref[1:2, :] = jnp.sum(dv.astype(f32), axis=0, keepdims=True)


def attend_back(order, bias, q, k, v, o, do, lse):
    rows, width = q.shape
    tiles, total = attention_tiles(rows)
    span = 2 * (width // HEADS)
    pairs = HEADS // 2
    scale = (width // HEADS) ** (-0.5)
    column = pl.BlockSpec((rows, span), lambda i, p: (0, i))
    return order(
        functools.partial(attend_back_kernel, tiles, scale),
        "attend_back",
        [bias, q, k, v, o, do, lse],
        [whole(bias.shape)]
        + [column] * 5
        + [pl.BlockSpec((1, len(tiles), 2 * TILE), lambda i, p: (i, 0, 0))],
        [
            (pl.BlockSpec((3, rows, span), lambda i, p: (0, 0, i)), shape_of((3, rows, width))),
            (pl.BlockSpec((2, span), lambda i, p: (0, i)), shape_of((2, width), f32)),
        ],
        grid=(pairs,),
        scratch=[pltpu.VMEM((rows, span), f32)] * 2,
        vmem=56,
    )


PARTS = 4


def middle_kernel(weights, place_ref, counts_ref, tok_ref, o_ref, cot_out_ref, cot_align_ref, vec_ref, *refs):
    arrays, refs = split_refs(refs, weights)
    out_ref, z_ref, e_ref, h_ref, g_ref, du_ref, dm_ref, da_ref, do_ref = refs[:9]
    sums_ref, w_proj_ref, w_up_ref, w_down_ref, w_head_ref, sems = refs[9:]
    step = pl.program_id(0)
    size, width = tok_ref.shape
    hidden_units = w_up_ref.shape[-1]
    part = hidden_units // PARTS
    valid = rows_valid(place_ref, counts_ref, step, size)

    @pl.when(step == 0)
    def _():
        fetch_all(place_ref, weights, arrays, [w_proj_ref, w_up_ref, w_down_ref, w_head_ref], sems)
        sums_ref[...] = jnp.zeros_like(sums_ref)

    def add_sum(index, first, value):
        columns = slice(first, first + value.shape[1])
        sums_ref[index : index + 1, columns] += jnp.sum(value.astype(f32), axis=0, keepdims=True)

    x1 = tok_ref[...].astype(f32) + dot_nn(o_ref[...], matrix(w_proj_ref)) + row(vec_ref, B_PROJ, width)
    n2, inverse = normed(x1)
    gain = row(vec_ref, GAIN_TWO, width)
    h2 = (n2 * gain + row(vec_ref, SHIFT_TWO, width)).astype(bf16)
    h_ref[...] = h2

    e_al = (cot_align_ref[...].astype(f32) * valid).astype(bf16)
    e_ref[...] = e_al
    add_sum(B_HEAD, 0, e_al)
    dx2 = cot_out_ref[...].astype(f32) * valid + dot_nt(e_al, matrix(w_head_ref))
    dm = dx2.astype(bf16)
    dm_ref[...] = dm
    add_sum(B_DOWN, 0, dm)

    x2 = x1 + row(vec_ref, B_DOWN, width)
    dh2 = jnp.zeros((size, width), f32)
    for index in range(PARTS):
        span = slice(index * part, (index + 1) * part)
        u = dot_nn(h2, matrix(w_up_ref, span)) + vec_ref[B_UP : B_UP + 1, span].astype(f32)
        cdf = 0.5 * (1.0 + lax.erf(u * (1.0 / math.sqrt(2.0))))
        pdf = jnp.exp(-0.5 * u * u) * (1.0 / math.sqrt(2.0 * math.pi))
        g = (u * cdf).astype(bf16)
        g_ref[:, span] = g
        x2 = x2 + dot_nn(g, w_down_ref[span, :])
        du = (dot_nt(dm, w_down_ref[span, :]) * (cdf + u * pdf)).astype(bf16)
        du_ref[:, span] = du
        add_sum(B_UP, index * part, du)
        dh2 = dh2 + dot_nt(du, matrix(w_up_ref, span))
    out_ref[...] = (x2 * valid).astype(bf16)
    z = x2.astype(bf16)
    z_ref[...] = z

    add_sum(GAIN_TWO, 0, dh2 * n2)
    add_sum(SHIFT_TWO, 0, dh2)
    t = dh2 * gain
    inner = t - jnp.mean(t, axis=-1, keepdims=True) - n2 * jnp.mean(t * n2, axis=-1, keepdims=True)
    dx1 = dx2 + inverse * inner
    da = dx1.astype(bf16)
    da_ref[...] = da
    add_sum(B_PROJ, 0, da)
    do_ref[...] = dot_nt(da, matrix(w_proj_ref)).astype(bf16)


def middle(order, counts, tokens, o, cot_out, cot_align, weights, vectors):
    rows, width = tokens.shape
    hidden, align = weights[1].shape[1], weights[3].shape[1]
    size = row_tile(rows, 320)

    def by_row(columns):
        return pl.BlockSpec((size, columns), lambda i, p: (i, 0))

    def row_shape(columns, dtype=bf16):
        return shape_of((rows, columns), dtype)

    outs = [
        (by_row(width), row_shape(width)),
        (by_row(width), row_shape(width)),
        (by_row(align), row_shape(align)),
        (by_row(width), row_shape(width)),
        (by_row(hidden), row_shape(hidden)),
        (by_row(hidden), row_shape(hidden)),
        (by_row(width), row_shape(width)),
        (by_row(width), row_shape(width)),
        (by_row(width), row_shape(width)),
    ]
    outs.append((out_whole(vectors.shape), shape_of(vectors.shape, f32)))
    arrays = [array for weight in weights for array in weight.arrays]
    return order(
        functools.partial(middle_kernel, weights),
        "middle",
        [counts, tokens, o, cot_out, cot_align, vectors, *arrays],
        [SMEM, by_row(width), by_row(width), by_row(width), by_row(align), whole(vectors.shape)]
        + [ANY] * len(arrays),
        outs,
        grid=(rows // size,),
        vmem=54,
        scratch=weight_scratch(weights),
    )


def rows_valid(place_ref, counts_ref, step, size):
    total = jnp.int32(0)
    for slot in range(counts_ref.shape[1]):
        total = total + counts_ref[place_ref[SEQ], slot]
    places = lax.broadcasted_iota(jnp.int32, (size, 1), 0) + step * size
    return jnp.where(places < total, 1.0, 0.0).astype(f32)


def align_kernel(weight, place_ref, counts_ref, z_ref, vec_ref, *refs):
    arrays, (out_ref, w_ref, sems) = split_refs(refs, [weight])
    step = pl.program_id(0)

    @pl.when(step == 0)
    def _():
        fetch_all(place_ref, [weight], arrays, [w_ref], sems)

    valid = rows_valid(place_ref, counts_ref, step, z_ref.shape[0])
    value = dot_nn(z_ref[...], matrix(w_ref)) + row(vec_ref, B_HEAD, out_ref.shape[1])
    out_ref[...] = (value * valid).astype(bf16)


def align(order, counts, z, weight, vectors):
    rows, width = z.shape
    size = row_tile(rows, 320)
    return order(
        functools.partial(align_kernel, weight),
        "align",
        [counts, z, vectors] + weight.arrays,
        [SMEM, pl.BlockSpec((size, width), lambda i, p: (i, 0)), whole(vectors.shape)] + [ANY] * len(weight.arrays),
        [(pl.BlockSpec((size, weight.shape[1]), lambda i, p: (i, 0)), shape_of((rows, weight.shape[1])))],
        grid=(rows // size,),
        scratch=weight_scratch([weight]),
        vmem=56,
    )[0]


def outer_kernel(place_ref, l_ref, r_ref, out_ref):
    out_ref[...] = dot_tn(l_ref[...], r_ref[...]).astype(out_ref.dtype)


def outer(order, left, right, rows_out, columns_out, name):
    rows, m = left.shape
    n = right.shape[1]
    tm, tn = min(rows_out, m), min(columns_out, n)
    return order(
        outer_kernel,
        name,
        [left, right],
        [pl.BlockSpec((rows, tm), lambda i, j, p: (0, i)), pl.BlockSpec((rows, tn), lambda i, j, p: (0, j))],
        [(pl.BlockSpec((tm, tn), lambda i, j, p: (i, j)), shape_of((m, n)))],
        grid=(m // tm, n // tn),
        vmem=56,
    )[0]


BAND = 96
HALF = BAND // 2
FEW = 16


def outer_split_kernel(place_ref, l_ref, r_ref, keep_ref, send_ref, l_scratch):
    levels, _, _, columns = keep_ref.shape

    @pl.when(pl.program_id(0) == 0)
    def _():
        l_scratch[...] = l_ref[...].T

    right = r_ref[0] if len(r_ref.shape) == 3 else r_ref[...]
    total = dot_nn(l_scratch[...], right).astype(bf16)
    shape = (2, HALF, columns)
    first = place_ref[CORE] == 0
    for z in range(levels):
        low = total[2 * z * BAND : (2 * z + 1) * BAND].reshape(shape)
        high = total[(2 * z + 1) * BAND : (2 * z + 2) * BAND].reshape(shape)
        level = place_ref[Z] ^ z
        keep_ref[level] = jnp.where(first, low, high)
        send_ref[level] = jnp.where(first, high, low)


def outer_split(order, left, right, levels, columns_out, total, at, into, name, after=()):
    rows, m = left.shape
    n = right.shape[-1] * (right.shape[0] if right.ndim == 3 else 1)
    if right.ndim == 3:
        columns_out = right.shape[-1]
        r_spec = pl.BlockSpec((1, rows, columns_out), lambda j, p: (j, 0, 0))
    else:
        r_spec = pl.BlockSpec((rows, columns_out), lambda j, p: (0, j))
    out = shape_of((levels, 2, HALF, total))
    out_spec = pl.BlockSpec((levels, 2, HALF, columns_out), lambda j, p: (0, 0, 0, at // columns_out + j))
    return order(
        outer_split_kernel,
        name,
        [left, right],
        [whole(left.shape), r_spec],
        [(out_spec, out)] * 2,
        grid=(n // columns_out,),
        scratch=[pltpu.VMEM((m, rows), bf16)],
        into=into,
        vmem=56,
        after=after,
    )


def outer_group_kernel(steps, place_ref, *refs):
    count = len(steps)
    lefts, rights, outs = refs[:count], refs[count : 2 * count], refs[2 * count : 4 * count]
    turned, held, sems = refs[4 * count], refs[4 * count + 1 : 5 * count], refs[5 * count]
    step = pl.program_id(0)
    first = place_ref[CORE] == 0
    copies = [pltpu.make_async_copy(lefts[i], held[i - 1], sems.at[i - 1]) for i in range(1, count)]

    @pl.when(step == 0)
    def _():
        for copy in copies:
            copy.start()

    begin = 0
    for i, length in enumerate(steps):
        keep_ref, send_ref = outs[2 * i], outs[2 * i + 1]

        @pl.when(step == begin)
        def _():
            if i:
                copies[i - 1].wait()
                turned[...] = held[i - 1][...].T
            else:
                turned[...] = lefts[0][...].T

        @pl.when((step >= begin) & (step < begin + length))
        def _():
            total = dot_nn(turned[...], rights[i][...]).astype(bf16)
            levels, _, _, columns = keep_ref.shape
            shape = (2, HALF, columns)
            for z in range(levels):
                low = total[2 * z * BAND : (2 * z + 1) * BAND].reshape(shape)
                high = total[(2 * z + 1) * BAND : (2 * z + 2) * BAND].reshape(shape)
                level = place_ref[Z] ^ z
                keep_ref[level] = jnp.where(first, low, high)
                send_ref[level] = jnp.where(first, high, low)

        begin += length


def outer_group(order, pairs, columns_out, levels, name):
    rows, m = pairs[0][0].shape
    steps = [right.shape[1] // columns for (_, right), columns in zip(pairs, columns_out)]
    rights, outs, begin = [], [], 0
    for (_, right), columns, length in zip(pairs, columns_out, steps):

        def at(j, begin=begin, length=length):
            return jnp.clip(j - begin, 0, length - 1)

        rights.append(pl.BlockSpec((rows, columns), lambda j, p, at=at: (0, at(j))))
        out_spec = pl.BlockSpec((levels, 2, HALF, columns), lambda j, p, at=at: (0, 0, 0, at(j)))
        outs += [(out_spec, shape_of((levels, 2, HALF, right.shape[1])))] * 2
        begin += length
    results = order(
        functools.partial(outer_group_kernel, steps),
        name,
        [left for left, _ in pairs] + [right for _, right in pairs],
        [whole((rows, m))] + [ANY] * (len(pairs) - 1) + rights,
        outs,
        grid=(sum(steps),),
        scratch=[pltpu.VMEM((m, rows), bf16)]
        + [pltpu.VMEM((rows, m), bf16)] * (len(pairs) - 1)
        + [pltpu.SemaphoreType.DMA((len(pairs) - 1,))],
        vmem=56,
    )
    return [results[2 * i : 2 * i + 2] for i in range(len(pairs))]


def split_kernel(sets, place_ref, *refs):
    pairs, outs = refs[: 2 * len(sets)], refs[2 * len(sets) :]
    for own in range(4):

        @pl.when(place_ref[Y] * 2 + place_ref[X] == own)
        def _():
            for quarter, out_ref in enumerate(outs):
                y, x = divmod(own ^ quarter, 2)
                at = 0
                for number, members in enumerate(sets):
                    keep_ref, got_ref = pairs[2 * number : 2 * number + 2]
                    first = 0
                    for columns in members:
                        half = columns // 2
                        part = slice(first + x * half, first + (x + 1) * half)
                        out_ref[:, :, at : at + half] = keep_ref[:, y, :, part] + got_ref[:, y, :, part]
                        at, first = at + half, first + columns


def split(order, sets, pairs, name):
    levels = pairs[0][0].shape[0]
    total = sum(keep.shape[3] for keep, _ in pairs)
    shape = (levels, HALF, total // 2)
    if len(pairs) == 1:
        ins, out, grid, vmem = [VMEM] * 2, VMEM, (), 32
    else:
        ins = [pl.BlockSpec((1,) + keep.shape[1:], lambda k, p: (k, 0, 0, 0)) for keep, _ in pairs for _ in range(2)]
        out, grid, vmem = pl.BlockSpec((1,) + shape[1:], lambda k, p: (k, 0, 0)), (levels,), 56
    return order(
        functools.partial(split_kernel, sets),
        name,
        [array for pair in pairs for array in pair],
        ins,
        [(out, shape_of(shape))] * 4,
        grid=grid,
        vmem=vmem,
    )


def levels_kernel(levels, place_ref, *refs):
    ins, lines, outs = refs[:4], refs[4:-levels], refs[-levels:]
    columns = ins[0].shape[2]
    for level, out_ref in enumerate(outs):
        total = ins[0][level].astype(f32)
        for ref in ins[1:]:
            total = total + ref[level].astype(f32)
        out_ref[:, :columns] = total.astype(bf16)
        if lines:
            total = lines[0][level].astype(f32)
            for ref in lines[1:]:
                total = total + ref[level].astype(f32)
            out_ref[0:FEW, columns:] = total.astype(bf16)
            out_ref[FEW:, columns:] = jnp.zeros((HALF - FEW, TILE), bf16)


def by_level(order, quarters, lines, name):
    levels, height, columns = quarters[0].shape
    columns += TILE if lines else 0
    return order(
        functools.partial(levels_kernel, levels),
        name,
        list(quarters) + list(lines),
        [VMEM] * (4 + len(lines)),
        [(VMEM, shape_of((height, columns)))] * levels,
    )


def halves_kernel(place_ref, *refs):
    ins, outs = refs[:-2], refs[-2:]
    half = ins[0].shape[0] // 2
    for out, out_ref in enumerate(outs):
        part = slice(out * half, (out + 1) * half)
        total = ins[0][part].astype(f32)
        for ref in ins[1:]:
            total = total + ref[part].astype(f32)
        out_ref[...] = total.astype(bf16).reshape(out_ref.shape)


def by_half(order, arrays, name):
    levels, height, columns = arrays[0].shape
    shape = (height, columns) if levels == 2 else (levels // 2, height, columns)
    return order(halves_kernel, name, arrays, [VMEM] * len(arrays), [(VMEM, shape_of(shape))] * 2)


def add_kernel(parts, place_ref, *refs):
    ins, beside, out_ref = refs[:parts], refs[parts:-1], refs[-1]
    columns = ins[0].shape[1]
    total = ins[0][...].astype(f32)
    for ref in ins[1:]:
        total = total + ref[...].astype(f32)
    out_ref[:, :columns] = total.astype(bf16)
    for ref in beside:
        width = ref.shape[1]
        for band in range(ref.shape[0] // HALF):
            out_ref[:, columns : columns + width] = ref[band * HALF : (band + 1) * HALF, :]
            columns += width


def add_up(order, arrays, beside, name):
    height, columns = arrays[0].shape
    columns += sum(b.size // height for b in beside)
    return order(
        functools.partial(add_kernel, len(arrays)),
        name,
        list(arrays) + list(beside),
        [VMEM] * (len(arrays) + len(beside)),
        [(VMEM, shape_of((height, columns)))],
    )[0]


def join_kernel(members, lengths, beside, place_ref, *refs):
    quarters, outs = refs[:4], refs[4:]
    for x in (0, 1):

        @pl.when(place_ref[X] == x)
        def _():
            for quarter, ref in enumerate(quarters):
                y = place_ref[Y] ^ (quarter // 2)
                across = x ^ (quarter % 2)
                at = 0
                for number, columns in enumerate(members):
                    half = columns // 2
                    outs[number][y, :, across * half : (across + 1) * half] = ref[:, at : at + half].astype(f32)
                    at += half

    if beside:
        at = sum(members) // 2 + (TILE if lengths else 0)
        out_ref = outs[len(members)]
        width = out_ref.shape[3]
        for quarter, ref in enumerate(quarters):
            owner = (place_ref[Y] * 2 + place_ref[X]) ^ quarter
            for band in range(out_ref.shape[1]):
                columns = slice(at + band * width, at + (band + 1) * width)
                out_ref[owner, band] = ref[:, columns].astype(f32)

    if lengths:
        at = sum(members) // 2
        lines = quarters[0][0:FEW, at : at + TILE].astype(f32)
        for ref in quarters[1:]:
            lines = lines + ref[0:FEW, at : at + TILE].astype(f32)
        line = 0
        for part, out_ref in zip(lengths, outs[len(members) + (1 if beside else 0) :]):
            rows = []
            for length in part:
                pieces = []
                for i in range(lines_of(length)):
                    pieces.append(lines[line + i : line + i + 1, : min(TILE, length - i * TILE)])
                rows.append(jnp.concatenate(pieces, axis=1) if len(pieces) > 1 else pieces[0])
                line += lines_of(length)
            if len(rows) == 1:
                out_ref[...] = rows[0][0]
            else:
                for i, value in enumerate(rows):
                    out_ref[i : i + 1, :] = value


def join(order, quarters, members, lengths, beside, name):
    outs = [(VMEM, shape_of((2, HALF, columns), f32)) for columns in members]
    if beside:
        rows, columns = beside
        outs.append((VMEM, shape_of((4, rows // (4 * HALF), HALF, columns), f32)))
    for part in lengths:
        outs.append((VMEM, shape_of((part[0],) if len(part) == 1 else (len(part), part[0]), f32)))
    results = order(
        functools.partial(join_kernel, members, lengths, beside),
        name,
        quarters,
        [VMEM] * 4,
        outs,
    )
    matrices = len(members) + (1 if beside else 0)
    return [r.reshape(-1, r.shape[-1]) for r in results[:matrices]] + list(results[matrices:])


class Reduction:
    def __init__(self, order, name):
        self.order, self.name = order, name
        self.sets, self.pairs = [], []

    def add(self, keep, send, members):
        self.sets.append(members)
        self.pairs.append((keep, swap(send, self.name + "_core", fsdp=1)))

    def split(self):
        quarters = split(self.order, self.sets, self.pairs, self.name + "_split")
        self.quarters = [quarters[0]] + [swap(quarters[j], self.name + "_plane", dp=j) for j in (1, 2, 3)]

    def levels(self, lines=()):
        parts = by_level(self.order, self.quarters, lines, self.name + "_levels")
        self.parts = [parts[0]]
        self.parts += [swap(part, self.name + "_column", fsdp=2 * level) for level, part in enumerate(parts) if level]

    def halve(self):
        arrays = self.quarters
        levels = arrays[0].shape[0]
        near, far = by_half(self.order, arrays, f"{self.name}_half_{levels}")
        self.quarters = [near, swap(far, self.name + "_column", fsdp=levels)]
        self.parts = self.quarters

    def total(self, beside=()):
        near = add_up(self.order, self.parts, beside, self.name + "_total")
        self.near = [near] + [swap(near, self.name + "_back", dp=j) for j in (1, 2, 3)]

    def join(self, lengths=(), beside=()):
        members = [columns for members in self.sets for columns in members]
        return join(self.order, self.near, members, lengths, beside, self.name + "_join")


def lines_of(length):
    return -(-length // TILE)


def pack_kernel(lengths, members, place_ref, *refs):
    arrays, (keep_ref, send_ref) = refs[:-2], refs[-2:]
    levels = keep_ref.shape[0]
    first = place_ref[CORE] == 0
    values = []
    for index, length in enumerate(lengths):
        if index in members:
            array, line = members[index]
            values.append(arrays[array][line : line + 1, : 2 * levels * length])
        else:
            values.append(jnp.zeros((1, 2 * levels * length), f32))

    def lines(shard):
        rows = []
        for value, length in zip(values, lengths):
            part = value[:, shard * length : (shard + 1) * length]
            if length % TILE:
                part = jnp.concatenate([part, jnp.zeros((1, -length % TILE), f32)], axis=1)
            rows += [part[:, at : at + TILE] for at in range(0, part.shape[1], TILE)]
        return jnp.concatenate(rows + [jnp.zeros((FEW - len(rows), TILE), f32)], axis=0)

    for z in range(levels):
        level = place_ref[Z] ^ z
        low, high = lines(2 * z), lines(2 * z + 1)
        keep_ref[level] = jnp.where(first, low, high).astype(bf16)
        send_ref[level] = jnp.where(first, high, low).astype(bf16)


def pack_vectors(order, arrays, members, lengths, levels, name, after=()):
    shape = (levels, FEW, TILE)
    return order(
        functools.partial(pack_kernel, lengths, members),
        name,
        arrays,
        [VMEM] * len(arrays),
        [(VMEM, shape_of(shape))] * 2,
        after=after,
    )


def unpack_kernel(lengths, place_ref, own_ref, other_ref, out_ref):
    levels = own_ref.shape[0]
    first = place_ref[CORE] == 0
    shards = []
    for z in range(levels):
        own = own_ref[z].astype(f32)
        other = other_ref[z].astype(f32)
        shards += [jnp.where(first, own, other), jnp.where(first, other, own)]
    at = 0
    for index, length in enumerate(lengths):
        pieces = []
        for shard in shards:
            for line in range(lines_of(length)):
                pieces.append(shard[at + line : at + line + 1, : min(TILE, length - line * TILE)])
        out_ref[index : index + 1, : length * len(shards)] = jnp.concatenate(pieces, axis=1).astype(bf16)
        at += lines_of(length)


def unpack_vectors(order, own, other, lengths):
    levels = own.shape[0]
    return order(
        functools.partial(unpack_kernel, lengths),
        "unpack_vectors",
        [own, other],
        [VMEM] * 2,
        [(VMEM, shape_of((ROWS, 2 * levels * max(lengths))))],
    )[0]


def start_kernel(lengths, groups, place_ref, *refs):
    count = sum(len(g) for g in groups)
    vectors = refs[: len(refs) - count - len(groups)]
    shards, outs = refs[len(vectors) : len(vectors) + count], refs[len(vectors) + count :]
    at = 0
    for group, out_ref in zip(groups, outs):
        column = 0
        for _ in group:
            half = shards[at].shape[1]
            out_ref[:, column : column + half] = shards[at][...]
            column += half
            at += 1
    values = []
    for ref in vectors:
        value = ref[...].astype(f32)
        values += [value[i] for i in range(value.shape[0])] if value.ndim == 2 else [value]
    lines = []
    for value, length in zip(values, lengths):
        if length % TILE:
            value = jnp.concatenate([value, jnp.zeros((-length % TILE,), f32)])
        lines += [value[at : at + TILE].reshape(1, TILE) for at in range(0, value.shape[0], TILE)]
    lines.append(jnp.zeros((HALF - len(lines), TILE), f32))
    outs[0][:, outs[0].shape[1] - TILE :] = jnp.concatenate(lines, axis=0).astype(bf16)


def start_gather(order, vectors, lengths, groups):
    shards = [w for group in groups for w in group]
    outs = []
    for number, group in enumerate(groups):
        shape = (HALF, sum(w.shape[1] // 2 for w in group) + (TILE if number == 0 else 0))
        outs.append((out_whole(shape), shape_of(shape)))
    return order(
        functools.partial(start_kernel, lengths, groups),
        "quarters",
        list(vectors) + shards,
        [whole(v.shape) for v in vectors]
        + [pl.BlockSpec((w.shape[0] // 2, w.shape[1] // 2), lambda i, p: (p[Y], p[X])) for w in shards],
        outs,
        grid=(1,),
        vmem=56,
    )


def near_kernel(levels, place_ref, *refs):
    got, out_ref, lines = refs[:levels], refs[levels], refs[levels + 1 :]
    columns = out_ref.shape[2]
    for level, ref in enumerate(got):
        if level:
            out_ref[level - 1] = ref[:, :columns]
        for lines_ref in lines:
            lines_ref[place_ref[Z] ^ level] = ref[0:FEW, columns:]


def near_levels(order, got, lines, name):
    levels, (height, columns) = len(got), got[0].shape
    columns -= TILE if lines else 0
    outs = [(VMEM, shape_of((levels - 1, height, columns)))]
    if lines:
        outs.append((VMEM, shape_of((levels, FEW, TILE))))
    return order(
        functools.partial(near_kernel, levels),
        name,
        got,
        [VMEM] * levels,
        outs,
    )


def assemble_kernel(halves, place_ref, *refs):
    shards, refs = refs[: len(halves)], refs[len(halves) :]
    quarters, out_ref = refs[:4], refs[4]
    z = place_ref[Z]
    column = 0
    for shard in shards:
        columns = shard.shape[1]
        for y in (0, 1):
            out_ref[z, y, :, column : column + columns] = shard[y * HALF : (y + 1) * HALF, :]
        column += columns
    for x in (0, 1):

        @pl.when(place_ref[X] == x)
        def _():
            for quarter, ref in enumerate(quarters):
                y = place_ref[Y] ^ (quarter // 2)
                across = x ^ (quarter % 2)
                for level in range(ref.shape[0]):
                    source, column = 0, 0
                    for half in halves:
                        target = column + across * half
                        out_ref[z ^ (level + 1), y, :, target : target + half] = ref[level, :, source : source + half]
                        source, column = source + half, column + 2 * half


def assemble(order, shards, quarters, name):
    levels = quarters[0].shape[0] + 1
    halves = [shard.shape[1] // 2 for shard in shards]
    return order(
        functools.partial(assemble_kernel, halves),
        name,
        list(shards) + list(quarters),
        [VMEM] * (len(shards) + 4),
        [(VMEM, shape_of((levels, 2, HALF, 2 * sum(halves))))],
    )[0].reshape(levels, BAND, -1)


def across_plane(near, name):
    return [near] + [swap(near, name + "_plane", dp=j) for j in (1, 2, 3)]


def first_back_kernel(weight, place_ref, tok_ref, dx_ref, d_ref, vec_ref, *refs):
    arrays, (out_ref, sums_ref, w_ref, sems) = split_refs(refs, [weight])
    width = tok_ref.shape[1]

    @pl.when(pl.program_id(0) == 0)
    def _():
        fetch_all(place_ref, [weight], arrays, [w_ref], sems)
        sums_ref[...] = jnp.zeros_like(sums_ref)

    dh = dot_nt(d_ref[0], matrix(w_ref, slice(0, width)))
    dh = dh + dot_nt(d_ref[1], matrix(w_ref, slice(width, 2 * width)))
    dh = dh + dot_nt(d_ref[2], matrix(w_ref, slice(2 * width, 3 * width)))
    n1, inverse = normed(tok_ref[...].astype(f32))
    sums_ref[0:1, :] += jnp.sum(dh * n1, axis=0, keepdims=True)
    sums_ref[1:2, :] += jnp.sum(dh, axis=0, keepdims=True)
    t = dh * row(vec_ref, GAIN_ONE, width)
    inner = t - jnp.mean(t, axis=-1, keepdims=True) - n1 * jnp.mean(t * n1, axis=-1, keepdims=True)
    out_ref[...] = (dx_ref[...].astype(f32) + inverse * inner).astype(bf16)


def first_back(order, tokens, dx1, dqkv, weight, vectors, after):
    rows, width = tokens.shape
    size = row_tile(rows, 320)
    rowwise = pl.BlockSpec((size, width), lambda i, p: (i, 0))
    return order(
        functools.partial(first_back_kernel, weight),
        "first_back",
        [tokens, dx1, dqkv, vectors] + weight.arrays,
        [rowwise, rowwise, pl.BlockSpec((3, size, width), lambda i, p: (0, i, 0)), whole(vectors.shape)]
        + [ANY] * len(weight.arrays),
        [(rowwise, shape_of((rows, width))), (out_whole((2, width)), shape_of((2, width), f32))],
        grid=(rows // size,),
        after=after,
        scratch=weight_scratch([weight]),
        vmem=56,
    )


def local(
    tokens,
    ln1_gain,
    ln1_bias,
    w_qkv,
    qv_bias,
    w_proj,
    proj_bias,
    ln2_gain,
    ln2_bias,
    w_up,
    up_bias,
    w_down,
    down_bias,
    w_head,
    head_bias,
    clip_counts,
    cot_out,
    cot_align,
):
    rows, width = tokens.shape
    shards = lax.axis_size("fsdp")
    levels = shards // 2
    order = Order(position())
    own_vectors = (ln1_gain, ln1_bias, qv_bias, proj_bias, ln2_gain, ln2_bias, up_bias, down_bias, head_bias)
    parts = [[v.shape[-1]] * (v.size // v.shape[-1]) for v in own_vectors]
    lengths = [length for part in parts for length in part]
    paired = (
        lax.axis_size("dp") == 4
        and shards % 2 == 0
        and levels in (2, 4, 8)
        and w_qkv.shape[0] == BAND
        and sum(lines_of(n) for n in lengths) <= FEW
    )

    def gather(value):
        return lax.all_gather(value, "fsdp", axis=0, tiled=True)

    def scatter(value):
        return lax.psum_scatter(value, "fsdp", scatter_dimension=0, tiled=True)

    if paired:
        wide = [w_up, w_head, w_proj]
        p_qkv, p_wide = start_gather(order, own_vectors, lengths, [[w_qkv], wide])
        got = [p_qkv] + [swap(p_qkv, "qkv_column", fsdp=2 * level) for level in range(1, levels)]
        got_wide = [p_wide] + [swap(p_wide, "wide_column", fsdp=2 * level) for level in range(1, levels)]
        bias = make_masks(order, clip_counts, rows)
        near, lines = near_levels(order, got, True, "qkv_near")
        quarters = across_plane(near, "qkv")
        other_lines = swap(lines, "vectors_core", fsdp=1)
        own = assemble(order, [w_qkv], quarters, "qkv_assemble")
        full_qkv = Weight([own, swap(own, "qkv_core", fsdp=1)], 0, (width, w_qkv.shape[1]))
        later, own = lax.optimization_barrier((w_down, own))
        full_down = gather(later)
        vectors = unpack_vectors(order, lines, other_lines, lengths)
        (near,) = near_levels(order, got_wide, False, "wide_near")
        quarters = across_plane(near, "wide")
    else:
        pieces = [piece for v in own_vectors for piece in ([v[0], v[1]] if v.ndim == 2 else [v])]
        joined = gather(jnp.concatenate(pieces)[None])
        lines, at = [], 0
        for length in lengths:
            line = joined[:, at : at + length].reshape(1, -1)
            lines.append(jnp.pad(line, ((0, 0), (0, shards * max(lengths) - line.shape[1]))))
            at += length
        vectors = jnp.pad(jnp.concatenate(lines), ((0, ROWS - len(lines)), (0, 0)))
        full_qkv, full_proj, full_up, full_head = (
            Weight([full], 0, full.shape) for full in (gather(w) for w in (w_qkv, w_proj, w_up, w_head))
        )
        full_down = gather(w_down)
        bias = make_masks(order, clip_counts, rows)
    full_down = Weight([full_down], 0, full_down.shape)
    h1, q, k, v = project_qkv(order, tokens, vectors, full_qkv)
    o, lse = attend(order, bias, q, k, v)
    if paired:
        own = assemble(order, wide, quarters, "wide_assemble")
        both_cores = [own, swap(own, "wide_core", fsdp=1)]
        at = [0, w_up.shape[1], w_up.shape[1] + w_head.shape[1]]
        full_up, full_head, full_proj = (
            Weight(both_cores, column, (width, w.shape[1])) for column, w in zip(at, wide)
        )
    block_out, z, e_al, h2, g, du, dm, da, do, sums = middle(
        order,
        clip_counts,
        tokens,
        o,
        cot_out,
        cot_align,
        (full_proj, full_up, full_down, full_head),
        vectors,
    )
    if paired:
        r_wide = Reduction(order, "wide")
        pairs = outer_group(order, [(h2, du), (z, e_al), (o, da)], [768, 512, 768], levels, "grad_wide")
        for pair, w in zip(pairs, wide):
            r_wide.add(*pair, [w.shape[1]])
    d_down = scatter(outer(order, g, dm, 1024, 768, "grad_down"))
    if paired:
        r_wide.split()
    dqkv, s_qv = attend_back(order, bias, q, k, v, o, do, lse)
    if paired:
        r_qkv = Reduction(order, "qkv")
        n = w_qkv.shape[1]
        r_qkv.add(*outer_split(order, h1, dqkv, levels, width, n, 0, (), "grad_qkv"), [n])
        early = {B_Q: (1, 0), B_V: (1, 1)}
        early.update({i: (0, i) for i in range(B_PROJ, B_HEAD + 1)})
        keep, send = pack_vectors(order, [sums, s_qv], early, lengths, levels, "pack_early")
        lines = [keep, swap(send, "vectors_core", fsdp=1)]
        r_qkv.split()
        aligned = align(order, clip_counts, z, full_head, vectors)
        r_wide.halve()
    grad_tokens, s_first = first_back(order, tokens, da, dqkv, full_qkv, vectors, [d_down] if paired else [])
    if paired:
        late = {GAIN_ONE: (0, 0), SHIFT_ONE: (0, 1)}
        keep, send = pack_vectors(order, [s_first], late, lengths, levels, "pack_late")
        lines += [keep, swap(send, "vectors_core", fsdp=1)]
        d_down = lax.psum_scatter(d_down, "dp", scatter_dimension=0, tiled=True)
        r_qkv.levels(lines)
        while r_wide.quarters[0].ndim == 3:
            r_wide.halve()
        r_qkv.total([d_down])
        r_wide.total()
        d_qkv, d_down, *mine = r_qkv.join(lengths=parts, beside=w_down.shape)
        d_up, d_head, d_proj = r_wide.join()
    else:
        aligned = align(order, clip_counts, z, full_head, vectors)

        def reduce(value):
            return lax.psum(scatter(value), "dp").astype(f32)

        d_down = lax.psum(d_down, "dp").astype(f32)
        d_up = reduce(outer(order, h2, du, 768, 512, "grad_up"))
        d_head = reduce(outer(order, z, e_al, 768, 512, "grad_head"))
        d_proj = reduce(outer(order, o, da, 768, 384, "grad_proj"))
        d_qkv = reduce(outer(order, h1, jnp.concatenate([dqkv[0], dqkv[1], dqkv[2]], axis=1), 768, 768, "grad_qkv"))
        late = {GAIN_ONE: s_first[0], SHIFT_ONE: s_first[1], B_Q: s_qv[0], B_V: s_qv[1]}
        lines = [late.get(i, sums[i])[: shards * n].reshape(shards, n) for i, n in enumerate(lengths)]
        joined = jnp.concatenate(lines, axis=1)
        joined = lax.psum(lax.psum_scatter(joined, "fsdp", scatter_dimension=0, tiled=True), "dp")[0]
        mine, at = [], 0
        for part in parts:
            size = sum(part)
            mine.append(joined[at : at + size].reshape((part[0],) if len(part) == 1 else (len(part), -1)))
            at += size
    d_gain_one, d_shift_one, d_qv, d_b_proj, d_gain_two, d_shift_two, d_b_up, d_b_down, d_b_head = mine
    return (
        block_out,
        aligned,
        grad_tokens,
        d_gain_one,
        d_shift_one,
        d_qkv,
        d_qv,
        d_proj,
        d_b_proj,
        d_gain_two,
        d_shift_two,
        d_up,
        d_b_up,
        d_down,
        d_b_down,
        d_head,
        d_b_head,
    )


def solution(mesh):
    rows = P(("dp", "fsdp"), None)
    matrix, vector, pair = P("fsdp", None), P("fsdp"), P(None, "fsdp")
    return jax.shard_map(
        local,
        mesh=mesh,
        in_specs=(
            rows,
            vector,
            vector,
            matrix,
            pair,
            matrix,
            vector,
            vector,
            vector,
            matrix,
            vector,
            matrix,
            vector,
            matrix,
            vector,
            P(),
            rows,
            rows,
        ),
        out_specs=(
            rows,
            rows,
            rows,
            vector,
            vector,
            matrix,
            pair,
            matrix,
            vector,
            vector,
            vector,
            matrix,
            vector,
            matrix,
            vector,
            matrix,
            vector,
        ),
        check_vma=False,
    )
```

```python
import functools
import math

import jax
import jax.numpy as jnp
from jax import lax
from jax.experimental import pallas as pl
from jax.experimental.pallas import tpu as pltpu
from jax.sharding import PartitionSpec as P

HEADS = 12
LONGEST = 157
EPSILON = 1e-06
MASKED = -1e30
TILE = 128

f32 = jnp.float32
bf16 = jnp.bfloat16


def dot_nn(left, right):
    return lax.dot_general(left, right, (((1,), (0,)), ((), ())), preferred_element_type=f32)


def dot_nt(left, right):
    return lax.dot_general(left, right, (((1,), (1,)), ((), ())), preferred_element_type=f32)


def dot_tn(left, right):
    return lax.dot_general(left, right, (((0,), (0,)), ((), ())), preferred_element_type=f32)


def attention_tiles(rows):
    tiles, offset = [], 0
    reach = LONGEST - 1
    for start in range(0, rows, TILE):
        size = min(TILE, rows - start)
        low = max(0, (start - reach) // 16 * 16)
        high = min(rows, -(-(start + size + reach) // 16) * 16)
        tiles.append((start, size, low, high - low, offset))
        offset += high - low
    return tiles, offset


def row_tile(rows, most):
    for size in range(most, 15, -16):
        if rows % size == 0:
            return size
    return rows


USUAL = 10
TIMES = {
    "attend_back": 60,
    "grad_down": 30,
    "pack_early": 30,
    "qkv_split": 1,
    "pack_late": 1,
    "wide_half_4": 1,
    "qkv_levels": 1,
    "wide_half_2": 1,
    "qkv_total": 1,
    "wide_total": 1,
}


def duration(name):
    return pl.CostEstimate(flops=TIMES.get(name, USUAL) * 10**9, bytes_accessed=1, transcendentals=0)


def whole(shape):
    return pl.BlockSpec(shape, lambda *_: (0,) * len(shape), pipeline_mode=pl.Buffered(1))


def out_whole(shape):
    return pl.BlockSpec(shape, lambda *_: (0,) * len(shape))


SMEM = pl.BlockSpec(memory_space=pltpu.SMEM)
VMEM = pl.BlockSpec(memory_space=pltpu.VMEM)
ANY = pl.BlockSpec(memory_space=pl.ANY)


def shape_of(shape, dtype=bf16):
    return jax.ShapeDtypeStruct(tuple(shape), dtype)


class Order:
    def __init__(self, place):
        self.place, self.last = place, None

    def __call__(self, kernel, name, arrays, in_specs, outs, grid=(), scratch=(), into=(), after=(), vmem=32):
        in_specs, arrays = list(in_specs), list(arrays)
        seen = 1 + len(arrays)
        aliases = {seen + i: i for i in range(len(into))}
        extra = (list(into) or ([] if self.last is None else [self.last])) + list(after)
        in_specs += [ANY] * len(extra)
        arrays += extra

        def body(*refs):
            kernel(*refs[:seen], *refs[seen + len(extra) :])

        result = pl.pallas_call(
            body,
            grid_spec=pltpu.PrefetchScalarGridSpec(
                num_scalar_prefetch=1,
                grid=grid,
                in_specs=in_specs,
                out_specs=tuple(spec for spec, _ in outs),
                scratch_shapes=list(scratch),
            ),
            out_shape=tuple(shape for _, shape in outs),
            cost_estimate=duration(name),
            input_output_aliases=aliases,
            compiler_params=pltpu.CompilerParams(vmem_limit_bytes=vmem << 20),
            name=name,
        )(self.place, *arrays)
        self.last = result[0]
        return result


Z, CORE, Y, X, SEQ = range(5)


def position():
    dp, fsdp = lax.axis_index("dp"), lax.axis_index("fsdp")
    seq = dp * lax.axis_size("fsdp") + fsdp
    return jnp.stack([fsdp // 2, fsdp % 2, dp // 2, dp % 2, seq]).astype(jnp.int32)


def swap(value, name, dp=0, fsdp=0):
    m, n = lax.axis_size("dp"), lax.axis_size("fsdp")
    pairs = [(i * n + j, (i ^ dp) * n + (j ^ fsdp)) for i in range(m) for j in range(n)]
    with jax.named_scope(f"{name}_{dp}_{fsdp}"):
        return lax.ppermute(value, ("dp", "fsdp"), pairs)


class Weight:
    def __init__(self, arrays, column, shape):
        self.arrays, self.column, self.shape = list(arrays), column, tuple(shape)
        if len(self.arrays) == 1:
            self.scratch = self.shape
        else:
            levels, rows, _ = arrays[0].shape
            self.scratch = (levels, 2, rows, shape[1])

    def copies(self, place, refs, weight, sems, first):
        columns = pl.ds(self.column, self.shape[1])
        if len(refs) == 1:
            return [pltpu.make_async_copy(refs[0], weight, sems.at[first])]
        return [
            pltpu.make_async_copy(ref.at[:, :, columns], weight.at[:, place[CORE] ^ i], sems.at[first + i])
            for i, ref in enumerate(refs)
        ]


def matrix(ref, columns=slice(None)):
    if len(ref.shape) == 2:
        return ref[:, columns]
    value = ref[:, :, :, columns]
    return value.reshape(-1, value.shape[-1])


def fetch_all(place, weights, arrays, scratch, sems):
    copies = []
    for weight, refs, target in zip(weights, arrays, scratch):
        copies += weight.copies(place, refs, target, sems, len(copies))
    for copy in copies:
        copy.start()
    for copy in copies:
        copy.wait()


def split_refs(refs, weights):
    groups, at = [], 0
    for weight in weights:
        groups.append(refs[at : at + len(weight.arrays)])
        at += len(weight.arrays)
    return groups, refs[at:]


def weight_scratch(weights):
    scratch = [pltpu.VMEM(w.scratch, bf16) for w in weights]
    return scratch + [pltpu.SemaphoreType.DMA((sum(len(w.arrays) for w in weights),))]


GAIN_ONE, SHIFT_ONE, B_Q, B_V, B_PROJ, GAIN_TWO, SHIFT_TWO, B_UP, B_DOWN, B_HEAD = range(10)
ROWS = 16


def row(vectors_ref, index, length):
    return vectors_ref[index : index + 1, :length]


def mask_kernel(tiles, place_ref, counts_ref, bias_ref, seg_ref):
    rows = seg_ref.shape[0]
    slots = counts_ref.shape[1]
    seq = place_ref[SEQ]
    ends, total = [], jnp.int32(0)
    for slot in range(slots):
        total = total + counts_ref[seq, slot]
        ends.append(total)
    places = lax.broadcasted_iota(jnp.int32, (rows, TILE), 0)
    seg = jnp.zeros((rows, TILE), jnp.int32)
    for end in ends:
        seg = seg + jnp.where(places >= end, 1, 0)
    seg_ref[...] = seg
    lanes = lax.broadcasted_iota(jnp.int32, (8, TILE), 1)
    for start, size, low, keys, offset in tiles:
        own = start + jnp.where(lanes >= size, lanes - size, lanes)
        seg_own = jnp.zeros((8, TILE), jnp.int32)
        for end in ends:
            seg_own = seg_own + jnp.where(own >= end, 1, 0)
        same = seg_ref[low : low + keys, :] == seg_own[0:1, :]
        bias_ref[offset : offset + keys, :] = jnp.where(same, 0.0, MASKED).astype(f32)


def make_masks(order, counts, rows):
    tiles, total = attention_tiles(rows)
    return order(
        functools.partial(mask_kernel, tiles),
        "masks",
        [counts],
        [SMEM],
        [(out_whole((total, TILE)), shape_of((total, TILE), f32))],
        scratch=[pltpu.VMEM((rows, TILE), jnp.int32)],
    )[0]


def normed(values):
    center = values - jnp.mean(values, axis=-1, keepdims=True)
    spread = jnp.mean(center * center, axis=-1, keepdims=True)
    inverse = lax.rsqrt(spread + EPSILON)
    return center * inverse, inverse


def qkv_kernel(scale, weight, place_ref, tok_ref, vec_ref, *refs):
    arrays, (h_ref, q_ref, k_ref, v_ref, w_ref, sems) = split_refs(refs, [weight])
    width = tok_ref.shape[1]

    @pl.when(pl.program_id(0) == 0)
    def _():
        fetch_all(place_ref, [weight], arrays, [w_ref], sems)

    n1, _ = normed(tok_ref[...].astype(f32))
    hidden = (n1 * row(vec_ref, GAIN_ONE, width) + row(vec_ref, SHIFT_ONE, width)).astype(bf16)
    h_ref[...] = hidden
    q = dot_nn(hidden, matrix(w_ref, slice(0, width)))
    q_ref[...] = ((q + row(vec_ref, B_Q, width)) * scale).astype(bf16)
    k = dot_nn(hidden, matrix(w_ref, slice(width, 2 * width)))
    k_ref[...] = k.astype(bf16)
    v = dot_nn(hidden, matrix(w_ref, slice(2 * width, 3 * width)))
    v_ref[...] = (v + row(vec_ref, B_V, width)).astype(bf16)


def project_qkv(order, tokens, vectors, weight):
    rows, width = tokens.shape
    scale = (width // HEADS) ** (-0.5)
    size = row_tile(rows, 320)
    rowwise = pl.BlockSpec((size, width), lambda i, p: (i, 0))
    return order(
        functools.partial(qkv_kernel, scale, weight),
        "norm_qkv",
        [tokens, vectors] + weight.arrays,
        [rowwise, whole(vectors.shape)] + [ANY] * len(weight.arrays),
        [(rowwise, shape_of((rows, width)))] * 4,
        grid=(rows // size,),
        scratch=weight_scratch([weight]),
    )


def stack_heads(pair, size):
    lanes = lax.broadcasted_iota(jnp.int32, pair.shape, 1)
    half = pair.shape[1] // 2
    zero = jnp.zeros_like(pair)
    first = jnp.where(lanes < half, pair, zero)
    second = jnp.where(lanes < half, zero, pair)
    return jnp.concatenate([first, second], axis=0)


def both(bias, size):
    return bias if size < TILE else jnp.concatenate([bias, bias], axis=1)


def unstack(columns, size, half):
    return jnp.concatenate([columns[:half, :size], columns[half:, size:]], axis=0).T


def attend_kernel(tiles, place_ref, bias_ref, q_ref, k_ref, v_ref, o_ref, lse_ref):
    half = q_ref.shape[1] // 2
    scores = []
    for start, size, low, keys, offset in tiles:
        stacked = stack_heads(q_ref[start : start + size, :], size)
        value = dot_nt(k_ref[low : low + keys, :], stacked)
        scores.append(value + both(bias_ref[offset : offset + keys, :], size))
    parts = []
    for value in scores:
        top = jnp.max(value, axis=0, keepdims=True)
        weights = jnp.exp(value - top)
        parts.append((weights.astype(bf16), top, jnp.sum(weights, axis=0, keepdims=True)))
    for index, (start, size, low, keys, _) in enumerate(tiles):
        weights, top, total = parts[index]
        columns = dot_tn(v_ref[low : low + keys, :], weights) * (1.0 / total)
        o_ref[start : start + size, :] = unstack(columns, size, half).astype(bf16)
        lse_ref[0, index : index + 1, : 2 * size] = top + jnp.log(total)


def attend(order, bias, q, k, v):
    rows, width = q.shape
    tiles, total = attention_tiles(rows)
    span = 2 * (width // HEADS)
    pairs = HEADS // 2
    column = pl.BlockSpec((rows, span), lambda i, p: (0, i))
    return order(
        functools.partial(attend_kernel, tiles),
        "attend",
        [bias, q, k, v],
        [whole(bias.shape), column, column, column],
        [
            (column, shape_of((rows, width))),
            (
                pl.BlockSpec((1, len(tiles), 2 * TILE), lambda i, p: (i, 0, 0)),
                shape_of((pairs, len(tiles), 2 * TILE), f32),
            ),
        ],
        grid=(pairs,),
    )


def attend_back_kernel(
    tiles, scale, place_ref, bias_ref, q_ref, k_ref, v_ref, o_ref, do_ref, lse_ref, d_ref, dqv_ref, dk_sum, dv_sum
):
    half = q_ref.shape[1] // 2
    dk_sum[...] = jnp.zeros_like(dk_sum)
    dv_sum[...] = jnp.zeros_like(dv_sum)
    dq_total = jnp.zeros((1, 2 * half), f32)
    for pair in range(0, len(tiles), 2):
        group = list(enumerate(tiles))[pair : pair + 2]
        held = []
        for index, (start, size, low, keys, offset) in group:
            window, rows = slice(low, low + keys), slice(start, start + size)
            q2 = stack_heads(q_ref[rows, :], size)
            grads = do_ref[rows, :]
            do2 = stack_heads(grads, size)
            scores = dot_nt(k_ref[window, :], q2) + both(bias_ref[offset : offset + keys, :], size)
            dprobs = dot_nt(v_ref[window, :], do2)
            meet = (grads.astype(f32) * o_ref[rows, :].astype(f32)).T
            delta = jnp.concatenate(
                [
                    jnp.sum(meet[:half, :], axis=0, keepdims=True),
                    jnp.sum(meet[half:, :], axis=0, keepdims=True),
                ],
                axis=1,
            )
            held.append((q2, do2, scores, dprobs, delta))
        lows = []
        for (index, (start, size, *_)), (q2, do2, scores, dprobs, delta) in zip(group, held):
            probs = jnp.exp(scores - lse_ref[0, index : index + 1, : 2 * size])
            lows.append((probs.astype(bf16), (probs * (dprobs - delta)).astype(bf16)))
        for (index, (start, size, low, keys, _)), (q2, do2, *_), (probs, dscores) in zip(group, held, lows):
            window, rows = slice(low, low + keys), slice(start, start + size)
            dv_sum[window, :] += dot_nn(probs, do2)
            dk_sum[window, :] += dot_nn(dscores, q2)
            columns = dot_tn(k_ref[window, :], dscores)
            dq = unstack(columns, size, half).astype(bf16) * bf16(scale)
            d_ref[0, rows, :] = dq
            dq_total = dq_total + jnp.sum(dq.astype(f32), axis=0, keepdims=True)
    d_ref[1, :, :] = dk_sum[...].astype(bf16)
    dv = dv_sum[...].astype(bf16)
    d_ref[2, :, :] = dv
    dqv_ref[0:1, :] = dq_total
    dqv_ref[1:2, :] = jnp.sum(dv.astype(f32), axis=0, keepdims=True)


def attend_back(order, bias, q, k, v, o, do, lse):
    rows, width = q.shape
    tiles, total = attention_tiles(rows)
    span = 2 * (width // HEADS)
    pairs = HEADS // 2
    scale = (width // HEADS) ** (-0.5)
    column = pl.BlockSpec((rows, span), lambda i, p: (0, i))
    return order(
        functools.partial(attend_back_kernel, tiles, scale),
        "attend_back",
        [bias, q, k, v, o, do, lse],
        [whole(bias.shape)]
        + [column] * 5
        + [pl.BlockSpec((1, len(tiles), 2 * TILE), lambda i, p: (i, 0, 0))],
        [
            (pl.BlockSpec((3, rows, span), lambda i, p: (0, 0, i)), shape_of((3, rows, width))),
            (pl.BlockSpec((2, span), lambda i, p: (0, i)), shape_of((2, width), f32)),
        ],
        grid=(pairs,),
        scratch=[pltpu.VMEM((rows, span), f32)] * 2,
        vmem=56,
    )


PARTS = 4


def middle_kernel(weights, place_ref, counts_ref, tok_ref, o_ref, cot_out_ref, cot_align_ref, vec_ref, *refs):
    arrays, refs = split_refs(refs, weights)
    out_ref, z_ref, e_ref, h_ref, g_ref, du_ref, dm_ref, da_ref, do_ref = refs[:9]
    sums_ref, w_proj_ref, w_up_ref, w_down_ref, w_head_ref, sems = refs[9:]
    step = pl.program_id(0)
    size, width = tok_ref.shape
    hidden_units = w_up_ref.shape[-1]
    part = hidden_units // PARTS
    valid = rows_valid(place_ref, counts_ref, step, size)

    @pl.when(step == 0)
    def _():
        fetch_all(place_ref, weights, arrays, [w_proj_ref, w_up_ref, w_down_ref, w_head_ref], sems)
        sums_ref[...] = jnp.zeros_like(sums_ref)

    def add_sum(index, first, value):
        columns = slice(first, first + value.shape[1])
        sums_ref[index : index + 1, columns] += jnp.sum(value.astype(f32), axis=0, keepdims=True)

    x1 = tok_ref[...].astype(f32) + dot_nn(o_ref[...], matrix(w_proj_ref)) + row(vec_ref, B_PROJ, width)
    n2, inverse = normed(x1)
    gain = row(vec_ref, GAIN_TWO, width)
    h2 = (n2 * gain + row(vec_ref, SHIFT_TWO, width)).astype(bf16)
    h_ref[...] = h2

    e_al = (cot_align_ref[...].astype(f32) * valid).astype(bf16)
    e_ref[...] = e_al
    add_sum(B_HEAD, 0, e_al)
    dx2 = cot_out_ref[...].astype(f32) * valid + dot_nt(e_al, matrix(w_head_ref))
    dm = dx2.astype(bf16)
    dm_ref[...] = dm
    add_sum(B_DOWN, 0, dm)

    x2 = x1 + row(vec_ref, B_DOWN, width)
    dh2 = jnp.zeros((size, width), f32)
    for index in range(PARTS):
        span = slice(index * part, (index + 1) * part)
        u = dot_nn(h2, matrix(w_up_ref, span)) + vec_ref[B_UP : B_UP + 1, span]
        cdf = 0.5 * (1.0 + lax.erf(u * (1.0 / math.sqrt(2.0))))
        pdf = jnp.exp(-0.5 * u * u) * (1.0 / math.sqrt(2.0 * math.pi))
        g = (u * cdf).astype(bf16)
        g_ref[:, span] = g
        x2 = x2 + dot_nn(g, w_down_ref[span, :])
        du = (dot_nt(dm, w_down_ref[span, :]) * (cdf + u * pdf)).astype(bf16)
        du_ref[:, span] = du
        add_sum(B_UP, index * part, du)
        dh2 = dh2 + dot_nt(du, matrix(w_up_ref, span))
    out_ref[...] = (x2 * valid).astype(bf16)
    z = x2.astype(bf16)
    z_ref[...] = z

    add_sum(GAIN_TWO, 0, dh2 * n2)
    add_sum(SHIFT_TWO, 0, dh2)
    t = dh2 * gain
    inner = t - jnp.mean(t, axis=-1, keepdims=True) - n2 * jnp.mean(t * n2, axis=-1, keepdims=True)
    dx1 = dx2 + inverse * inner
    da = dx1.astype(bf16)
    da_ref[...] = da
    add_sum(B_PROJ, 0, da)
    do_ref[...] = dot_nt(da, matrix(w_proj_ref)).astype(bf16)


def middle(order, counts, tokens, o, cot_out, cot_align, weights, vectors):
    rows, width = tokens.shape
    hidden, align = weights[1].shape[1], weights[3].shape[1]
    size = row_tile(rows, 320)

    def by_row(columns):
        return pl.BlockSpec((size, columns), lambda i, p: (i, 0))

    def row_shape(columns, dtype=bf16):
        return shape_of((rows, columns), dtype)

    outs = [
        (by_row(width), row_shape(width)),
        (by_row(width), row_shape(width)),
        (by_row(align), row_shape(align)),
        (by_row(width), row_shape(width)),
        (by_row(hidden), row_shape(hidden)),
        (by_row(hidden), row_shape(hidden)),
        (by_row(width), row_shape(width)),
        (by_row(width), row_shape(width)),
        (by_row(width), row_shape(width)),
    ]
    outs.append((out_whole(vectors.shape), shape_of(vectors.shape, f32)))
    arrays = [array for weight in weights for array in weight.arrays]
    return order(
        functools.partial(middle_kernel, weights),
        "middle",
        [counts, tokens, o, cot_out, cot_align, vectors, *arrays],
        [SMEM, by_row(width), by_row(width), by_row(width), by_row(align), whole(vectors.shape)]
        + [ANY] * len(arrays),
        outs,
        grid=(rows // size,),
        vmem=54,
        scratch=weight_scratch(weights),
    )


def rows_valid(place_ref, counts_ref, step, size):
    total = jnp.int32(0)
    for slot in range(counts_ref.shape[1]):
        total = total + counts_ref[place_ref[SEQ], slot]
    places = lax.broadcasted_iota(jnp.int32, (size, 1), 0) + step * size
    return jnp.where(places < total, 1.0, 0.0).astype(f32)


def align_kernel(weight, place_ref, counts_ref, z_ref, vec_ref, *refs):
    arrays, (out_ref, w_ref, sems) = split_refs(refs, [weight])
    step = pl.program_id(0)

    @pl.when(step == 0)
    def _():
        fetch_all(place_ref, [weight], arrays, [w_ref], sems)

    valid = rows_valid(place_ref, counts_ref, step, z_ref.shape[0])
    value = dot_nn(z_ref[...], matrix(w_ref)) + row(vec_ref, B_HEAD, out_ref.shape[1])
    out_ref[...] = (value * valid).astype(bf16)


def align(order, counts, z, weight, vectors):
    rows, width = z.shape
    size = row_tile(rows, 320)
    return order(
        functools.partial(align_kernel, weight),
        "align",
        [counts, z, vectors] + weight.arrays,
        [SMEM, pl.BlockSpec((size, width), lambda i, p: (i, 0)), whole(vectors.shape)] + [ANY] * len(weight.arrays),
        [(pl.BlockSpec((size, weight.shape[1]), lambda i, p: (i, 0)), shape_of((rows, weight.shape[1])))],
        grid=(rows // size,),
        scratch=weight_scratch([weight]),
        vmem=56,
    )[0]


def outer_kernel(place_ref, l_ref, r_ref, out_ref):
    out_ref[...] = dot_tn(l_ref[...], r_ref[...]).astype(out_ref.dtype)


def outer(order, left, right, rows_out, columns_out, name):
    rows, m = left.shape
    n = right.shape[1]
    tm, tn = min(rows_out, m), min(columns_out, n)
    return order(
        outer_kernel,
        name,
        [left, right],
        [pl.BlockSpec((rows, tm), lambda i, j, p: (0, i)), pl.BlockSpec((rows, tn), lambda i, j, p: (0, j))],
        [(pl.BlockSpec((tm, tn), lambda i, j, p: (i, j)), shape_of((m, n)))],
        grid=(m // tm, n // tn),
        vmem=56,
    )[0]


BAND = 96
HALF = BAND // 2
FEW = 16


def outer_split_kernel(place_ref, l_ref, r_ref, keep_ref, send_ref, l_scratch):
    levels, _, _, columns = keep_ref.shape

    @pl.when(pl.program_id(0) == 0)
    def _():
        l_scratch[...] = l_ref[...].T

    right = r_ref[0] if len(r_ref.shape) == 3 else r_ref[...]
    total = dot_nn(l_scratch[...], right).astype(bf16)
    shape = (2, HALF, columns)
    first = place_ref[CORE] == 0
    for z in range(levels):
        low = total[2 * z * BAND : (2 * z + 1) * BAND].reshape(shape)
        high = total[(2 * z + 1) * BAND : (2 * z + 2) * BAND].reshape(shape)
        level = place_ref[Z] ^ z
        keep_ref[level] = jnp.where(first, low, high)
        send_ref[level] = jnp.where(first, high, low)


def outer_split(order, left, right, levels, columns_out, total, at, into, name, after=()):
    rows, m = left.shape
    n = right.shape[-1] * (right.shape[0] if right.ndim == 3 else 1)
    if right.ndim == 3:
        columns_out = right.shape[-1]
        r_spec = pl.BlockSpec((1, rows, columns_out), lambda j, p: (j, 0, 0))
    else:
        r_spec = pl.BlockSpec((rows, columns_out), lambda j, p: (0, j))
    out = shape_of((levels, 2, HALF, total))
    out_spec = pl.BlockSpec((levels, 2, HALF, columns_out), lambda j, p: (0, 0, 0, at // columns_out + j))
    return order(
        outer_split_kernel,
        name,
        [left, right],
        [whole(left.shape), r_spec],
        [(out_spec, out)] * 2,
        grid=(n // columns_out,),
        scratch=[pltpu.VMEM((m, rows), bf16)],
        into=into,
        vmem=56,
        after=after,
    )


def outer_group_kernel(steps, place_ref, *refs):
    count = len(steps)
    lefts, rights, outs = refs[:count], refs[count : 2 * count], refs[2 * count : 4 * count]
    turned, held, sems = refs[4 * count], refs[4 * count + 1 : 5 * count], refs[5 * count]
    step = pl.program_id(0)
    first = place_ref[CORE] == 0
    copies = [pltpu.make_async_copy(lefts[i], held[i - 1], sems.at[i - 1]) for i in range(1, count)]

    @pl.when(step == 0)
    def _():
        for copy in copies:
            copy.start()

    begin = 0
    for i, length in enumerate(steps):
        keep_ref, send_ref = outs[2 * i], outs[2 * i + 1]

        @pl.when(step == begin)
        def _():
            if i:
                copies[i - 1].wait()
                turned[...] = held[i - 1][...].T
            else:
                turned[...] = lefts[0][...].T

        @pl.when((step >= begin) & (step < begin + length))
        def _():
            total = dot_nn(turned[...], rights[i][...]).astype(bf16)
            levels, _, _, columns = keep_ref.shape
            shape = (2, HALF, columns)
            for z in range(levels):
                low = total[2 * z * BAND : (2 * z + 1) * BAND].reshape(shape)
                high = total[(2 * z + 1) * BAND : (2 * z + 2) * BAND].reshape(shape)
                level = place_ref[Z] ^ z
                keep_ref[level] = jnp.where(first, low, high)
                send_ref[level] = jnp.where(first, high, low)

        begin += length


def outer_group(order, pairs, columns_out, levels, name):
    rows, m = pairs[0][0].shape
    steps = [right.shape[1] // columns for (_, right), columns in zip(pairs, columns_out)]
    rights, outs, begin = [], [], 0
    for (_, right), columns, length in zip(pairs, columns_out, steps):

        def at(j, begin=begin, length=length):
            return jnp.clip(j - begin, 0, length - 1)

        rights.append(pl.BlockSpec((rows, columns), lambda j, p, at=at: (0, at(j))))
        out_spec = pl.BlockSpec((levels, 2, HALF, columns), lambda j, p, at=at: (0, 0, 0, at(j)))
        outs += [(out_spec, shape_of((levels, 2, HALF, right.shape[1])))] * 2
        begin += length
    results = order(
        functools.partial(outer_group_kernel, steps),
        name,
        [left for left, _ in pairs] + [right for _, right in pairs],
        [whole((rows, m))] + [ANY] * (len(pairs) - 1) + rights,
        outs,
        grid=(sum(steps),),
        scratch=[pltpu.VMEM((m, rows), bf16)]
        + [pltpu.VMEM((rows, m), bf16)] * (len(pairs) - 1)
        + [pltpu.SemaphoreType.DMA((len(pairs) - 1,))],
        vmem=56,
    )
    return [results[2 * i : 2 * i + 2] for i in range(len(pairs))]


def split_kernel(sets, place_ref, *refs):
    pairs, outs = refs[: 2 * len(sets)], refs[2 * len(sets) :]
    for own in range(4):

        @pl.when(place_ref[Y] * 2 + place_ref[X] == own)
        def _():
            for quarter, out_ref in enumerate(outs):
                y, x = divmod(own ^ quarter, 2)
                at = 0
                for number, members in enumerate(sets):
                    keep_ref, got_ref = pairs[2 * number : 2 * number + 2]
                    first = 0
                    for columns in members:
                        half = columns // 2
                        part = slice(first + x * half, first + (x + 1) * half)
                        out_ref[:, :, at : at + half] = keep_ref[:, y, :, part] + got_ref[:, y, :, part]
                        at, first = at + half, first + columns


def split(order, sets, pairs, name):
    levels = pairs[0][0].shape[0]
    total = sum(keep.shape[3] for keep, _ in pairs)
    shape = (levels, HALF, total // 2)
    if len(pairs) == 1:
        ins, out, grid, vmem = [VMEM] * 2, VMEM, (), 32
    else:
        ins = [pl.BlockSpec((1,) + keep.shape[1:], lambda k, p: (k, 0, 0, 0)) for keep, _ in pairs for _ in range(2)]
        out, grid, vmem = pl.BlockSpec((1,) + shape[1:], lambda k, p: (k, 0, 0)), (levels,), 56
    return order(
        functools.partial(split_kernel, sets),
        name,
        [array for pair in pairs for array in pair],
        ins,
        [(out, shape_of(shape))] * 4,
        grid=grid,
        vmem=vmem,
    )


def levels_kernel(levels, place_ref, *refs):
    ins, lines, outs = refs[:4], refs[4:-levels], refs[-levels:]
    columns = ins[0].shape[2]
    for level, out_ref in enumerate(outs):
        total = ins[0][level].astype(f32)
        for ref in ins[1:]:
            total = total + ref[level].astype(f32)
        out_ref[:, :columns] = total.astype(bf16)
        if lines:
            total = lines[0][level].astype(f32)
            for ref in lines[1:]:
                total = total + ref[level].astype(f32)
            out_ref[0:FEW, columns:] = total.astype(bf16)
            out_ref[FEW:, columns:] = jnp.zeros((HALF - FEW, TILE), bf16)


def by_level(order, quarters, lines, name):
    levels, height, columns = quarters[0].shape
    columns += TILE if lines else 0
    return order(
        functools.partial(levels_kernel, levels),
        name,
        list(quarters) + list(lines),
        [VMEM] * (4 + len(lines)),
        [(VMEM, shape_of((height, columns)))] * levels,
    )


def halves_kernel(place_ref, *refs):
    ins, outs = refs[:-2], refs[-2:]
    half = ins[0].shape[0] // 2
    for out, out_ref in enumerate(outs):
        part = slice(out * half, (out + 1) * half)
        total = ins[0][part].astype(f32)
        for ref in ins[1:]:
            total = total + ref[part].astype(f32)
        out_ref[...] = total.astype(bf16).reshape(out_ref.shape)


def by_half(order, arrays, name):
    levels, height, columns = arrays[0].shape
    shape = (height, columns) if levels == 2 else (levels // 2, height, columns)
    return order(halves_kernel, name, arrays, [VMEM] * len(arrays), [(VMEM, shape_of(shape))] * 2)


def add_kernel(parts, place_ref, *refs):
    ins, beside, out_ref = refs[:parts], refs[parts:-1], refs[-1]
    columns = ins[0].shape[1]
    total = ins[0][...].astype(f32)
    for ref in ins[1:]:
        total = total + ref[...].astype(f32)
    out_ref[:, :columns] = total.astype(bf16)
    for ref in beside:
        width = ref.shape[1]
        for band in range(ref.shape[0] // HALF):
            out_ref[:, columns : columns + width] = ref[band * HALF : (band + 1) * HALF, :]
            columns += width


def add_up(order, arrays, beside, name):
    height, columns = arrays[0].shape
    columns += sum(b.size // height for b in beside)
    return order(
        functools.partial(add_kernel, len(arrays)),
        name,
        list(arrays) + list(beside),
        [VMEM] * (len(arrays) + len(beside)),
        [(VMEM, shape_of((height, columns)))],
    )[0]


def join_kernel(members, lengths, beside, place_ref, *refs):
    quarters, outs = refs[:4], refs[4:]
    for x in (0, 1):

        @pl.when(place_ref[X] == x)
        def _():
            for quarter, ref in enumerate(quarters):
                y = place_ref[Y] ^ (quarter // 2)
                across = x ^ (quarter % 2)
                at = 0
                for number, columns in enumerate(members):
                    half = columns // 2
                    outs[number][y, :, across * half : (across + 1) * half] = ref[:, at : at + half].astype(f32)
                    at += half

    if beside:
        at = sum(members) // 2 + (TILE if lengths else 0)
        out_ref = outs[len(members)]
        width = out_ref.shape[3]
        for quarter, ref in enumerate(quarters):
            owner = (place_ref[Y] * 2 + place_ref[X]) ^ quarter
            for band in range(out_ref.shape[1]):
                columns = slice(at + band * width, at + (band + 1) * width)
                out_ref[owner, band] = ref[:, columns].astype(f32)

    if lengths:
        at = sum(members) // 2
        lines = quarters[0][0:FEW, at : at + TILE].astype(f32)
        for ref in quarters[1:]:
            lines = lines + ref[0:FEW, at : at + TILE].astype(f32)
        line = 0
        for part, out_ref in zip(lengths, outs[len(members) + (1 if beside else 0) :]):
            rows = []
            for length in part:
                pieces = []
                for i in range(lines_of(length)):
                    pieces.append(lines[line + i : line + i + 1, : min(TILE, length - i * TILE)])
                rows.append(jnp.concatenate(pieces, axis=1) if len(pieces) > 1 else pieces[0])
                line += lines_of(length)
            if len(rows) == 1:
                out_ref[...] = rows[0][0]
            else:
                for i, value in enumerate(rows):
                    out_ref[i : i + 1, :] = value


def join(order, quarters, members, lengths, beside, name):
    outs = [(VMEM, shape_of((2, HALF, columns), f32)) for columns in members]
    if beside:
        rows, columns = beside
        outs.append((VMEM, shape_of((4, rows // (4 * HALF), HALF, columns), f32)))
    for part in lengths:
        outs.append((VMEM, shape_of((part[0],) if len(part) == 1 else (len(part), part[0]), f32)))
    results = order(
        functools.partial(join_kernel, members, lengths, beside),
        name,
        quarters,
        [VMEM] * 4,
        outs,
    )
    matrices = len(members) + (1 if beside else 0)
    return [r.reshape(-1, r.shape[-1]) for r in results[:matrices]] + list(results[matrices:])


class Reduction:
    def __init__(self, order, name):
        self.order, self.name = order, name
        self.sets, self.pairs = [], []

    def add(self, keep, send, members):
        self.sets.append(members)
        self.pairs.append((keep, swap(send, self.name + "_core", fsdp=1)))

    def split(self):
        quarters = split(self.order, self.sets, self.pairs, self.name + "_split")
        self.quarters = [quarters[0]] + [swap(quarters[j], self.name + "_plane", dp=j) for j in (1, 2, 3)]

    def levels(self, lines=()):
        parts = by_level(self.order, self.quarters, lines, self.name + "_levels")
        self.parts = [parts[0]]
        self.parts += [swap(part, self.name + "_column", fsdp=2 * level) for level, part in enumerate(parts) if level]

    def halve(self):
        arrays = self.quarters
        levels = arrays[0].shape[0]
        near, far = by_half(self.order, arrays, f"{self.name}_half_{levels}")
        self.quarters = [near, swap(far, self.name + "_column", fsdp=levels)]
        self.parts = self.quarters

    def total(self, beside=()):
        near = add_up(self.order, self.parts, beside, self.name + "_total")
        self.near = [near] + [swap(near, self.name + "_back", dp=j) for j in (1, 2, 3)]

    def join(self, lengths=(), beside=()):
        members = [columns for members in self.sets for columns in members]
        return join(self.order, self.near, members, lengths, beside, self.name + "_join")


def lines_of(length):
    return -(-length // TILE)


def pack_kernel(lengths, members, place_ref, *refs):
    arrays, (keep_ref, send_ref) = refs[:-2], refs[-2:]
    levels = keep_ref.shape[0]
    first = place_ref[CORE] == 0
    values = []
    for index, length in enumerate(lengths):
        if index in members:
            array, line = members[index]
            values.append(arrays[array][line : line + 1, : 2 * levels * length])
        else:
            values.append(jnp.zeros((1, 2 * levels * length), f32))

    def lines(shard):
        rows = []
        for value, length in zip(values, lengths):
            part = value[:, shard * length : (shard + 1) * length]
            if length % TILE:
                part = jnp.concatenate([part, jnp.zeros((1, -length % TILE), f32)], axis=1)
            rows += [part[:, at : at + TILE] for at in range(0, part.shape[1], TILE)]
        return jnp.concatenate(rows + [jnp.zeros((FEW - len(rows), TILE), f32)], axis=0)

    for z in range(levels):
        level = place_ref[Z] ^ z
        low, high = lines(2 * z), lines(2 * z + 1)
        keep_ref[level] = jnp.where(first, low, high).astype(bf16)
        send_ref[level] = jnp.where(first, high, low).astype(bf16)


def pack_vectors(order, arrays, members, lengths, levels, name, after=()):
    shape = (levels, FEW, TILE)
    return order(
        functools.partial(pack_kernel, lengths, members),
        name,
        arrays,
        [VMEM] * len(arrays),
        [(VMEM, shape_of(shape))] * 2,
        after=after,
    )


def unpack_kernel(lengths, place_ref, own_ref, other_ref, out_ref):
    levels = own_ref.shape[0]
    first = place_ref[CORE] == 0
    shards = []
    for z in range(levels):
        own = own_ref[z].astype(f32)
        other = other_ref[z].astype(f32)
        shards += [jnp.where(first, own, other), jnp.where(first, other, own)]
    at = 0
    for index, length in enumerate(lengths):
        pieces = []
        for shard in shards:
            for line in range(lines_of(length)):
                pieces.append(shard[at + line : at + line + 1, : min(TILE, length - line * TILE)])
        out_ref[index : index + 1, : length * len(shards)] = jnp.concatenate(pieces, axis=1)
        at += lines_of(length)


def unpack_vectors(order, own, other, lengths):
    levels = own.shape[0]
    return order(
        functools.partial(unpack_kernel, lengths),
        "unpack_vectors",
        [own, other],
        [VMEM] * 2,
        [(VMEM, shape_of((ROWS, 2 * levels * max(lengths)), f32))],
    )[0]


def start_kernel(lengths, groups, place_ref, *refs):
    count = sum(len(g) for g in groups)
    vectors = refs[: len(refs) - count - len(groups)]
    shards, outs = refs[len(vectors) : len(vectors) + count], refs[len(vectors) + count :]
    at = 0
    for group, out_ref in zip(groups, outs):
        column = 0
        for _ in group:
            half = shards[at].shape[1]
            out_ref[:, column : column + half] = shards[at][...]
            column += half
            at += 1
    values = []
    for ref in vectors:
        value = ref[...].astype(f32)
        values += [value[i] for i in range(value.shape[0])] if value.ndim == 2 else [value]
    lines = []
    for value, length in zip(values, lengths):
        if length % TILE:
            value = jnp.concatenate([value, jnp.zeros((-length % TILE,), f32)])
        lines += [value[at : at + TILE].reshape(1, TILE) for at in range(0, value.shape[0], TILE)]
    lines.append(jnp.zeros((HALF - len(lines), TILE), f32))
    outs[0][:, outs[0].shape[1] - TILE :] = jnp.concatenate(lines, axis=0).astype(bf16)


def start_gather(order, vectors, lengths, groups):
    shards = [w for group in groups for w in group]
    outs = []
    for number, group in enumerate(groups):
        shape = (HALF, sum(w.shape[1] // 2 for w in group) + (TILE if number == 0 else 0))
        outs.append((out_whole(shape), shape_of(shape)))
    return order(
        functools.partial(start_kernel, lengths, groups),
        "quarters",
        list(vectors) + shards,
        [whole(v.shape) for v in vectors]
        + [pl.BlockSpec((w.shape[0] // 2, w.shape[1] // 2), lambda i, p: (p[Y], p[X])) for w in shards],
        outs,
        grid=(1,),
        vmem=56,
    )


def near_kernel(levels, place_ref, *refs):
    got, out_ref, lines = refs[:levels], refs[levels], refs[levels + 1 :]
    columns = out_ref.shape[2]
    for level, ref in enumerate(got):
        if level:
            out_ref[level - 1] = ref[:, :columns]
        for lines_ref in lines:
            lines_ref[place_ref[Z] ^ level] = ref[0:FEW, columns:]


def near_levels(order, got, lines, name):
    levels, (height, columns) = len(got), got[0].shape
    columns -= TILE if lines else 0
    outs = [(VMEM, shape_of((levels - 1, height, columns)))]
    if lines:
        outs.append((VMEM, shape_of((levels, FEW, TILE))))
    return order(
        functools.partial(near_kernel, levels),
        name,
        got,
        [VMEM] * levels,
        outs,
    )


def assemble_kernel(halves, place_ref, *refs):
    shards, refs = refs[: len(halves)], refs[len(halves) :]
    quarters, out_ref = refs[:4], refs[4]
    z = place_ref[Z]
    column = 0
    for shard in shards:
        columns = shard.shape[1]
        for y in (0, 1):
            out_ref[z, y, :, column : column + columns] = shard[y * HALF : (y + 1) * HALF, :]
        column += columns
    for x in (0, 1):

        @pl.when(place_ref[X] == x)
        def _():
            for quarter, ref in enumerate(quarters):
                y = place_ref[Y] ^ (quarter // 2)
                across = x ^ (quarter % 2)
                for level in range(ref.shape[0]):
                    source, column = 0, 0
                    for half in halves:
                        target = column + across * half
                        out_ref[z ^ (level + 1), y, :, target : target + half] = ref[level, :, source : source + half]
                        source, column = source + half, column + 2 * half


def assemble(order, shards, quarters, name):
    levels = quarters[0].shape[0] + 1
    halves = [shard.shape[1] // 2 for shard in shards]
    return order(
        functools.partial(assemble_kernel, halves),
        name,
        list(shards) + list(quarters),
        [VMEM] * (len(shards) + 4),
        [(VMEM, shape_of((levels, 2, HALF, 2 * sum(halves))))],
    )[0].reshape(levels, BAND, -1)


def across_plane(near, name):
    return [near] + [swap(near, name + "_plane", dp=j) for j in (1, 2, 3)]


def first_back_kernel(weight, place_ref, tok_ref, dx_ref, d_ref, vec_ref, *refs):
    arrays, (out_ref, sums_ref, w_ref, sems) = split_refs(refs, [weight])
    width = tok_ref.shape[1]

    @pl.when(pl.program_id(0) == 0)
    def _():
        fetch_all(place_ref, [weight], arrays, [w_ref], sems)
        sums_ref[...] = jnp.zeros_like(sums_ref)

    dh = dot_nt(d_ref[0], matrix(w_ref, slice(0, width)))
    dh = dh + dot_nt(d_ref[1], matrix(w_ref, slice(width, 2 * width)))
    dh = dh + dot_nt(d_ref[2], matrix(w_ref, slice(2 * width, 3 * width)))
    n1, inverse = normed(tok_ref[...].astype(f32))
    sums_ref[0:1, :] += jnp.sum(dh * n1, axis=0, keepdims=True)
    sums_ref[1:2, :] += jnp.sum(dh, axis=0, keepdims=True)
    t = dh * row(vec_ref, GAIN_ONE, width)
    inner = t - jnp.mean(t, axis=-1, keepdims=True) - n1 * jnp.mean(t * n1, axis=-1, keepdims=True)
    out_ref[...] = (dx_ref[...].astype(f32) + inverse * inner).astype(bf16)


def first_back(order, tokens, dx1, dqkv, weight, vectors, after):
    rows, width = tokens.shape
    size = row_tile(rows, 320)
    rowwise = pl.BlockSpec((size, width), lambda i, p: (i, 0))
    return order(
        functools.partial(first_back_kernel, weight),
        "first_back",
        [tokens, dx1, dqkv, vectors] + weight.arrays,
        [rowwise, rowwise, pl.BlockSpec((3, size, width), lambda i, p: (0, i, 0)), whole(vectors.shape)]
        + [ANY] * len(weight.arrays),
        [(rowwise, shape_of((rows, width))), (out_whole((2, width)), shape_of((2, width), f32))],
        grid=(rows // size,),
        after=after,
        scratch=weight_scratch([weight]),
        vmem=56,
    )


def local(
    tokens,
    ln1_gain,
    ln1_bias,
    w_qkv,
    qv_bias,
    w_proj,
    proj_bias,
    ln2_gain,
    ln2_bias,
    w_up,
    up_bias,
    w_down,
    down_bias,
    w_head,
    head_bias,
    clip_counts,
    cot_out,
    cot_align,
):
    rows, width = tokens.shape
    shards = lax.axis_size("fsdp")
    levels = shards // 2
    order = Order(position())
    own_vectors = (ln1_gain, ln1_bias, qv_bias, proj_bias, ln2_gain, ln2_bias, up_bias, down_bias, head_bias)
    parts = [[v.shape[-1]] * (v.size // v.shape[-1]) for v in own_vectors]
    lengths = [length for part in parts for length in part]
    paired = (
        lax.axis_size("dp") == 4
        and shards % 2 == 0
        and levels in (2, 4, 8)
        and w_qkv.shape[0] == BAND
        and sum(lines_of(n) for n in lengths) <= FEW
    )

    def gather(value):
        return lax.all_gather(value, "fsdp", axis=0, tiled=True)

    def scatter(value):
        return lax.psum_scatter(value, "fsdp", scatter_dimension=0, tiled=True)

    if paired:
        wide = [w_up, w_head, w_proj]
        p_qkv, p_wide = start_gather(order, own_vectors, lengths, [[w_qkv], wide])
        got = [p_qkv] + [swap(p_qkv, "qkv_column", fsdp=2 * level) for level in range(1, levels)]
        got_wide = [p_wide] + [swap(p_wide, "wide_column", fsdp=2 * level) for level in range(1, levels)]
        bias = make_masks(order, clip_counts, rows)
        near, lines = near_levels(order, got, True, "qkv_near")
        quarters = across_plane(near, "qkv")
        other_lines = swap(lines, "vectors_core", fsdp=1)
        own = assemble(order, [w_qkv], quarters, "qkv_assemble")
        full_qkv = Weight([own, swap(own, "qkv_core", fsdp=1)], 0, (width, w_qkv.shape[1]))
        later, own = lax.optimization_barrier((w_down, own))
        full_down = gather(later)
        vectors = unpack_vectors(order, lines, other_lines, lengths)
        (near,) = near_levels(order, got_wide, False, "wide_near")
        quarters = across_plane(near, "wide")
    else:
        pieces = [piece for v in own_vectors for piece in ([v[0], v[1]] if v.ndim == 2 else [v])]
        joined = gather(jnp.concatenate(pieces)[None])
        lines, at = [], 0
        for length in lengths:
            line = joined[:, at : at + length].reshape(1, -1)
            lines.append(jnp.pad(line, ((0, 0), (0, shards * max(lengths) - line.shape[1]))))
            at += length
        vectors = jnp.pad(jnp.concatenate(lines), ((0, ROWS - len(lines)), (0, 0))).astype(f32)
        full_qkv, full_proj, full_up, full_head = (
            Weight([full], 0, full.shape) for full in (gather(w) for w in (w_qkv, w_proj, w_up, w_head))
        )
        full_down = gather(w_down)
        bias = make_masks(order, clip_counts, rows)
    full_down = Weight([full_down], 0, full_down.shape)
    h1, q, k, v = project_qkv(order, tokens, vectors, full_qkv)
    o, lse = attend(order, bias, q, k, v)
    if paired:
        own = assemble(order, wide, quarters, "wide_assemble")
        both_cores = [own, swap(own, "wide_core", fsdp=1)]
        at = [0, w_up.shape[1], w_up.shape[1] + w_head.shape[1]]
        full_up, full_head, full_proj = (
            Weight(both_cores, column, (width, w.shape[1])) for column, w in zip(at, wide)
        )
    block_out, z, e_al, h2, g, du, dm, da, do, sums = middle(
        order,
        clip_counts,
        tokens,
        o,
        cot_out,
        cot_align,
        (full_proj, full_up, full_down, full_head),
        vectors,
    )
    if paired:
        r_wide = Reduction(order, "wide")
        pairs = outer_group(order, [(h2, du), (z, e_al), (o, da)], [768, 512, 768], levels, "grad_wide")
        for pair, w in zip(pairs, wide):
            r_wide.add(*pair, [w.shape[1]])
    d_down = scatter(outer(order, g, dm, 1024, 768, "grad_down"))
    if paired:
        r_wide.split()
    dqkv, s_qv = attend_back(order, bias, q, k, v, o, do, lse)
    if paired:
        r_qkv = Reduction(order, "qkv")
        n = w_qkv.shape[1]
        r_qkv.add(*outer_split(order, h1, dqkv, levels, width, n, 0, (), "grad_qkv"), [n])
        early = {B_Q: (1, 0), B_V: (1, 1)}
        early.update({i: (0, i) for i in range(B_PROJ, B_HEAD + 1)})
        keep, send = pack_vectors(order, [sums, s_qv], early, lengths, levels, "pack_early")
        lines = [keep, swap(send, "vectors_core", fsdp=1)]
        r_qkv.split()
        aligned = align(order, clip_counts, z, full_head, vectors)
        r_wide.halve()
    grad_tokens, s_first = first_back(order, tokens, da, dqkv, full_qkv, vectors, [d_down] if paired else [])
    if paired:
        late = {GAIN_ONE: (0, 0), SHIFT_ONE: (0, 1)}
        keep, send = pack_vectors(order, [s_first], late, lengths, levels, "pack_late")
        lines += [keep, swap(send, "vectors_core", fsdp=1)]
        d_down = lax.psum_scatter(d_down, "dp", scatter_dimension=0, tiled=True)
        r_qkv.levels(lines)
        while r_wide.quarters[0].ndim == 3:
            r_wide.halve()
        r_qkv.total([d_down])
        r_wide.total()
        d_qkv, d_down, *mine = r_qkv.join(lengths=parts, beside=w_down.shape)
        d_up, d_head, d_proj = r_wide.join()
    else:
        aligned = align(order, clip_counts, z, full_head, vectors)

        def reduce(value):
            return lax.psum(scatter(value), "dp").astype(f32)

        d_down = lax.psum(d_down, "dp").astype(f32)
        d_up = reduce(outer(order, h2, du, 768, 512, "grad_up"))
        d_head = reduce(outer(order, z, e_al, 768, 512, "grad_head"))
        d_proj = reduce(outer(order, o, da, 768, 384, "grad_proj"))
        d_qkv = reduce(outer(order, h1, jnp.concatenate([dqkv[0], dqkv[1], dqkv[2]], axis=1), 768, 768, "grad_qkv"))
        late = {GAIN_ONE: s_first[0], SHIFT_ONE: s_first[1], B_Q: s_qv[0], B_V: s_qv[1]}
        lines = [late.get(i, sums[i])[: shards * n].reshape(shards, n) for i, n in enumerate(lengths)]
        joined = jnp.concatenate(lines, axis=1)
        joined = lax.psum(lax.psum_scatter(joined, "fsdp", scatter_dimension=0, tiled=True), "dp")[0]
        mine, at = [], 0
        for part in parts:
            size = sum(part)
            mine.append(joined[at : at + size].reshape((part[0],) if len(part) == 1 else (len(part), -1)))
            at += size
    d_gain_one, d_shift_one, d_qv, d_b_proj, d_gain_two, d_shift_two, d_b_up, d_b_down, d_b_head = mine
    return (
        block_out,
        aligned,
        grad_tokens,
        d_gain_one,
        d_shift_one,
        d_qkv,
        d_qv,
        d_proj,
        d_b_proj,
        d_gain_two,
        d_shift_two,
        d_up,
        d_b_up,
        d_down,
        d_b_down,
        d_head,
        d_b_head,
    )


def solution(mesh):
    rows = P(("dp", "fsdp"), None)
    matrix, vector, pair = P("fsdp", None), P("fsdp"), P(None, "fsdp")
    return jax.shard_map(
        local,
        mesh=mesh,
        in_specs=(
            rows,
            vector,
            vector,
            matrix,
            pair,
            matrix,
            vector,
            vector,
            vector,
            matrix,
            vector,
            matrix,
            vector,
            matrix,
            vector,
            P(),
            rows,
            rows,
        ),
        out_specs=(
            rows,
            rows,
            rows,
            vector,
            vector,
            matrix,
            pair,
            matrix,
            vector,
            vector,
            vector,
            matrix,
            vector,
            matrix,
            vector,
            matrix,
            vector,
        ),
        check_vma=False,
    )
```
